32 devices in a mesh: groups: 2 (over y), brain: 4 (over x, core), slab: 4 (over z).
Axes of the slice: x: 2, y: 2, z: 4, core: 2. Of those that a mesh axis runs over, the one named last changes fastest.
Arguments:
- intensity: bfloat16 [8, 96, 8, 128], P(('groups', 'brain'), 'slab'), parts along dimension 0, may hold values from -6 to 6
- velocity: float32 [8, 3, 96, 8, 128], P(('groups', 'brain'), None, 'slab'), parts along dimension 0, may hold values from -0.1 to 0.1
- partner: int32 [8], P('groups'), parts along dimension 0, may hold values from 0 to 3, as said below
- offsets: int32 [8, 2], P('groups'), parts along dimension 0, may hold values from 0 to 3
Outputs:
- new_velocity: float32 [8, 3, 96, 8, 128], P(('groups', 'brain'), None, 'slab'), parts along dimension 0
The draws below stay inside these ranges and needn't reach their ends.
There are 2 independent parts, one for each index of `groups`. The reference program is written for one: setup_inputs(seed, part) draws one part's arguments, and reference() takes and returns one part's arrays. A program takes and returns all parts, laid end to end along the dimension named above; each array names one. Nothing has to cross between parts.
Inputs may be any that keep to these rules, and one draw needn't show every extreme that they name: partner[partner[b]] = b and partner[b] != b for every brain b of a cohort.
All inputs are finite; a program needn't handle non-finite values.
Results may differ from the reference program's by a relative error of at most 0.0013.
Values may be sent and summed in bfloat16 or wider, within the bound.
No kernel may reach another device: no remote copies, remote signals or barrier semaphores. Data moves between devices by JAX's collectives and lax.ppermute only.
A program may use at most 64 MiB of HBM per device.

```python
import jax
import jax.numpy as jnp
import numpy as np
from jax import lax

ROWS = 8
COLS = 128
OFFMAX = 4
BRAINS = 4
DEPTH = 96


def draw_partner(key, part):
    shuffled = jax.random.permutation(key, BRAINS).astype(jnp.int32)
    mates = shuffled[jnp.arange(BRAINS, dtype=jnp.int32) ^ 1]
    return jnp.zeros((BRAINS,), jnp.int32).at[shuffled].set(mates)


def with_ends(result, key, least, top_value):
    longest = result.shape.index(max(result.shape))
    spots = []
    for shift in (0, 1):
        where = [jax.random.randint(jax.random.fold_in(key, axis), (), 0, length) for axis, length in enumerate(result.shape)]
        where[longest] = (where[longest] + shift) % result.shape[longest]
        spots.append(tuple(where))
    return result.at[spots[0]].set(least).at[spots[1]].set(top_value)


def level_of(key, shape, shards, smallest, high):
    gain = 1.0
    for dim, shards_of in shards:
        draws = jax.random.uniform(jax.random.fold_in(jax.random.fold_in(key, 6), dim), (shards_of,), jnp.float32, smallest / len(shards), high / len(shards))
        gain = gain * jnp.repeat(jnp.exp(draws), shape[dim] // shards_of).reshape((-1,) + (1,) * (len(shape) - 1 - dim))
    return gain


def scatter_about(own_key, extent, width, reach, cuts=(), kind=jnp.bfloat16):
    gain = level_of(own_key, extent, cuts, -0.22, 0.18) if cuts else 1.0
    entries = jax.random.normal(own_key, extent, jnp.float32) * width * gain
    return jnp.minimum(jnp.maximum(entries, -reach), reach).astype(kind)


def setup_inputs(seed: int = 0, part: int = 0) -> dict:
    seeds = jax.random.split(jax.random.key(seed), 5)
    part_keys = jax.random.split(jax.random.fold_in(seeds[4], part), 5)
    return {
        "intensity": scatter_about(part_keys[0], (BRAINS, DEPTH, ROWS, COLS), 1.0, 6.0, ((0, 4), (1, 4))),
        "velocity": jnp.clip(jax.random.uniform(part_keys[1], (BRAINS, 3, DEPTH, ROWS, COLS), jnp.float32, -0.1, 0.1) * level_of(part_keys[1], (BRAINS, 3, DEPTH, ROWS, COLS), ((0, 4), (2, 4)), -0.4, 0.0), -0.1, 0.1),
        "partner": draw_partner(jax.random.fold_in(jax.random.fold_in(seeds[4], part), 71), part),
        "offsets": with_ends(jax.random.randint(part_keys[3], (BRAINS, 2), 0, OFFMAX), jax.random.fold_in(part_keys[3], 1), 0, OFFMAX - 1).astype(jnp.int32),
    }


NEIGHBOURS = ((1, 0, 0), (-1, 0, 0), (0, 1, 0), (0, -1, 0), (0, 0, 1), (0, 0, -1))
CHANNEL_PAIRS = tuple(((i, j) for i in range(6) for j in range(i + 1, 6) if i // 2 != j // 2))
SMOOTH_TAPS = tuple((float(v) for v in np.exp(-np.arange(-3, 4) ** 2 / 4.5) / np.exp(-np.arange(-3, 4) ** 2 / 4.5).sum()))
VARIANCE_EPSILON = 1e-05
SPREAD_OFFSET = 0.1
STEP_SIZE = 8.0

def shifted(values, dim_index, offset):
    if offset == 0:
        return values
    length = values.shape[dim_index]
    widths = [(0, 0)] * values.ndim
    widths[dim_index] = (max(-offset, 0), max(offset, 0))
    return lax.slice_in_dim(jnp.pad(values, widths), max(offset, 0), max(offset, 0) + length, axis=dim_index)

def plane_total(values, radius):
    dim_depth = values.ndim - 3
    planes = values.shape[dim_depth] - 2 * radius
    return sum((lax.slice_in_dim(values, j, j + planes, axis=dim_depth) for j in range(2 * radius + 1)))

def flat_total(values, radius):
    running = values
    for dim_index in (values.ndim - 2, values.ndim - 1):
        running = sum((shifted(running, dim_index, j) for j in range(-radius, radius + 1)))
    return running

def window_total(values, radius):
    return flat_total(plane_total(values, radius), radius)

def smoothed_field(values):
    dim_depth = values.ndim - 3
    planes = values.shape[dim_depth] - 6
    running = sum((SMOOTH_TAPS[j] * lax.slice_in_dim(values, j, j + planes, axis=dim_depth) for j in range(7)))
    for dim_index in (values.ndim - 2, values.ndim - 1):
        running = sum((SMOOTH_TAPS[j + 3] * shifted(running, dim_index, j) for j in range(-3, 4)))
    return running

def mask_planes(first_plane, planes, depth_all):
    global_plane = first_plane + jnp.arange(planes, dtype=jnp.int32)
    return ((global_plane >= 0) & (global_plane < depth_all)).astype(jnp.float32)[:, None, None]

def advected(fields, first_plane, depth_all):
    planes = fields.shape[1]
    source = fields[0]
    centre = source[1:planes - 1]
    speeds = fields[1:, 1:planes - 1]
    backward = [centre - source[0:planes - 2], centre - shifted(centre, 1, -1), centre - shifted(centre, 2, -1)]
    forward = [source[2:planes] - centre, shifted(centre, 1, 1) - centre, shifted(centre, 2, 1) - centre]
    transport = sum((jnp.maximum(speeds[j], 0.0) * backward[j] + jnp.minimum(speeds[j], 0.0) * forward[j] for j in range(3)))
    return (centre - transport) * mask_planes(first_plane + 1, planes - 2, depth_all)

def neighbour(values, offset):
    planes = values.shape[0]
    sliced = lax.slice_in_dim(values, 1 + offset[0], planes - 1 + offset[0], axis=0)
    return shifted(shifted(sliced, 1, offset[1]), 2, offset[2])

def squared(values, pair_ids, inner_mask):
    difference = neighbour(values, NEIGHBOURS[pair_ids[0]]) - neighbour(values, NEIGHBOURS[pair_ids[1]])
    return difference * difference * inner_mask

def descriptors(values, inner_mask, outer_mask):
    stacked = jnp.stack([squared(values, pair_ids, inner_mask) for pair_ids in CHANNEL_PAIRS])
    distance = window_total(stacked, 1) / 27.0
    spread = lax.optimization_barrier(jnp.sum(distance, axis=0)) / 12.0 + SPREAD_OFFSET
    return jnp.exp(-distance / spread[None]) * outer_mask[None]

def force_field(own_field, mate_field, first_plane, depth_all):
    planes = own_field.shape[0]
    inner_mask = mask_planes(first_plane + 1, planes - 2, depth_all)
    outer_mask = mask_planes(first_plane + 2, planes - 4, depth_all)
    inner_planes = planes - 4
    own_desc = descriptors(own_field, inner_mask, outer_mask)
    mate_desc = descriptors(mate_field, inner_mask, outer_mask)
    mean_own = window_total(own_desc, 4) / 729.0
    mean_mate = window_total(mate_desc, 4) / 729.0
    var_own = window_total(own_desc * own_desc, 4) / 729.0 - mean_own * mean_own + VARIANCE_EPSILON
    var_mate = window_total(mate_desc * mate_desc, 4) / 729.0 - mean_mate * mean_mate + VARIANCE_EPSILON
    covariance = window_total(own_desc * mate_desc, 4) / 729.0 - mean_own * mean_mate
    own_centre = own_desc[:, 4:inner_planes - 4]
    mate_centre = mate_desc[:, 4:inner_planes - 4]
    coefficient = (mate_centre - mean_mate - covariance / var_own * (own_centre - mean_own)) * lax.rsqrt(var_own * var_mate)
    gradients = [(own_desc[:, 5:inner_planes - 3] - own_desc[:, 3:inner_planes - 5]) * 0.5, (shifted(own_centre, 2, 1) - shifted(own_centre, 2, -1)) * 0.5, (shifted(own_centre, 3, 1) - shifted(own_centre, 3, -1)) * 0.5]
    running = jnp.stack([lax.optimization_barrier(jnp.sum(coefficient * grad_part, axis=0)) for grad_part in gradients])
    return running / 12.0 * mask_planes(first_plane + 6, planes - 12, depth_all)[None]

def aligned(values, row_shift, col_shift):
    padded = jnp.pad(values, ((0, 0), (OFFMAX, OFFMAX), (OFFMAX, OFFMAX)))
    zero_start = jnp.zeros((), jnp.int32)
    return lax.dynamic_slice(padded, (zero_start, (OFFMAX + row_shift).astype(jnp.int32), (OFFMAX + col_shift).astype(jnp.int32)), values.shape)

def reference(intensity, velocity, partner, offsets):

    def warp_one(brain_id):
        fields = jnp.concatenate([intensity[brain_id].astype(jnp.float32)[None], velocity[brain_id]], axis=0)
        padded = jnp.pad(fields, ((0, 0), (1, 1), (0, 0), (0, 0)))
        return advected(padded, -1, DEPTH).astype(jnp.bfloat16)
    warped = lax.map(warp_one, jnp.arange(BRAINS, dtype=jnp.int32))
    margin_planes = 6

    def update_one(brain_id):
        mate_index = partner[brain_id]
        row_shift = offsets[mate_index, 0] - offsets[brain_id, 0]
        col_shift = offsets[mate_index, 1] - offsets[brain_id, 1]
        own_field = jnp.pad(warped[brain_id].astype(jnp.float32), ((margin_planes, margin_planes), (0, 0), (0, 0)))
        mate_plain = aligned(warped[mate_index].astype(jnp.float32), row_shift, col_shift)
        mate_field = jnp.pad(mate_plain, ((margin_planes, margin_planes), (0, 0), (0, 0)))
        force = force_field(own_field, mate_field, -margin_planes, DEPTH)
        smoothed = smoothed_field(jnp.pad(force, ((0, 0), (3, 3), (0, 0), (0, 0))))
        return velocity[brain_id] + STEP_SIZE * smoothed
    return lax.map(update_one, jnp.arange(BRAINS, dtype=jnp.int32))
```

```python
import functools
import jax, jax.numpy as jnp, numpy as np
from jax import lax
from jax.experimental import pallas as pl
from jax.experimental.pallas import tpu as pltpu
from jax.sharding import PartitionSpec as P

PAIRS = tuple((i, j) for i in range(6) for j in range(i + 1, 6) if i // 2 != j // 2)
TAPS = tuple(float(v) for v in np.exp(-np.arange(-3, 4) ** 2 / 4.5) / np.exp(-np.arange(-3, 4) ** 2 / 4.5).sum())
f32, bf16 = jnp.float32, jnp.bfloat16
LOG2E = 1.4426950408889634


def split(v):
    hi = v.astype(bf16)
    return hi, (v - hi.astype(f32)).astype(bf16)


def main_kernel(planes, meta, own, m1, m2, m3, vel, out, mats, xs, raw, tb, desc, ys, lhs, res, frc):
    nx = planes + 18
    nd = planes + 16
    nf = planes + 8
    ng, nfg = nd // 8, nf // 8
    dr, dc = meta[1], meta[2]
    low, high = meta[3].astype(f32), meta[4].astype(f32)

    i = lax.broadcasted_iota(jnp.int32, (128, 128), 0)
    j = lax.broadcasted_iota(jnp.int32, (128, 128), 1)
    one = lambda cond: jnp.where(cond, 1.0, 0.0).astype(bf16)
    box9 = one(jnp.abs(i - j) <= 4)
    box3 = one(jnp.abs(i - j) <= 1)
    grad = jnp.where(i == j + 1, 1.0, jnp.where(i == j - 1, -1.0, 0.0)).astype(bf16)
    smooth = jnp.zeros((128, 128), f32)
    for d in range(4):
        smooth = jnp.where(jnp.abs(i - j) == d, TAPS[3 + d], smooth)
    shi, slo = split(smooth)
    for h in (0, 128):
        mats[0, h:h + 128] = box3
        mats[1, h:h + 128] = box9
        mats[2, h:h + 128] = grad
        mats[3, h:h + 128] = shi
    mats[4, 0:128] = slo
    row = lax.broadcasted_iota(jnp.int32, (8, 128), 0)

    x = own[...]
    for n, d in ((0, 0), (3, 1), (4, -1)):
        if d == 0:
            v = x.astype(f32)
        else:
            v = jnp.dot(x, one(i == j + d), preferred_element_type=f32)
        xs[0, n] = v
    which = meta[0]
    x = jnp.where(which == 1, m1[...], jnp.where(which == 2, m2[...], m3[...]))
    for n, d in ((0, 0), (1, 1), (2, -1)):
        sel = one((i == j + d + dc) & (j + d >= 0) & (j + d < 128))
        raw[n, pl.ds(8, nx * 8), :] = jnp.dot(x, sel, preferred_element_type=f32)

    def rowmask(d):
        return (row + d >= 0) & (row + d < 8)

    def prep(p, _):
        at = pl.multiple_of(p * 8, 8)
        for n, d in ((1, 1), (2, -1)):
            if True:
                v = raw_own(p, d)
                xs[0, n, pl.ds(at, 8), :] = jnp.where(rowmask(d), v, 0.0)
        for n, b, d in ((0, 0, 0), (1, 0, 1), (2, 0, -1), (3, 1, 0), (4, 2, 0)):
            v = raw[b, pl.ds(at + 8 + dr + d, 8), :]
            xs[1, n, pl.ds(at, 8), :] = jnp.where(rowmask(d) & rowmask(d + dr), v, 0.0)
        return 0

    def raw_own(p, d):
        return pltpu.roll(xs[0, 0, pl.ds(pl.multiple_of(p * 8, 8), 8), :], (-d) % 8, 0)
    lax.fori_loop(0, nx, prep, 0, unroll=6)

    for m in range(2):
        def squares(g, carry, m=m):
            c1, c2 = carry
            scale = jnp.where(g == 0, low, jnp.where(g == ng - 1, high, 1.0))
            for i in range(8):
                s = g * 8 + i
                ld = lambda n, p: xs[m, n, pl.ds(pl.multiple_of(p * 8, 8), 8), :]
                near = [ld(0, s + 2), ld(0, s)] + [ld(j, s + 1) for j in (1, 2, 3, 4)]
                n1, n2 = [], []
                for k, (a, b) in enumerate(PAIRS):
                    d = near[a] - near[b]
                    q = d * d * scale
                    tb[k, pl.ds(pl.multiple_of(s * 8, 8), 8), :] = c2[k] + q
                    n2.append(c1[k] + q)
                    n1.append(q)
                c1, c2 = n1, n2
            return c1, c2
        zero = [jnp.zeros((8, 128), f32)] * 12
        c1, c2 = lax.fori_loop(0, ng, squares, (zero, zero))
        for k in range(12):
            tb[k, pl.ds(nd * 8, 8), :] = c2[k]

        def descr(g, _, m=m):
            base = g * 64
            for k in range(12):
                t = [tb[k, pl.ds(base + 8 + r, 8, stride=8), :] for r in range(8)]
                p = [t[r] + t[r + 1] for r in range(7)]
                w = [p[0]] + [p[r - 1] + t[r + 1] for r in range(1, 7)] + [p[6]]
                hi, lo = split(jnp.concatenate(w, axis=0))
                lhs[pl.ds(k * 64, 64), 0:128] = hi
                lhs[pl.ds(k * 64, 64), 128:256] = lo
            ys[0, 0:768] = jnp.dot(lhs[0:768], mats[0], preferred_element_type=f32)
            mask = jnp.where(g == 0, low, jnp.where(g == ng - 1, high, 1.0))
            for r in range(8):
                v = [ys[0, pl.ds(k * 64 + r * 8, 8), :] for k in range(12)]
                total = functools.reduce(jnp.add, v)
                inv = (-LOG2E / 27.0) / (total * (1.0 / 324.0) + 0.1)
                for k in range(12):
                    desc[m, k, pl.ds(base + r, 8, stride=8), :] = jnp.exp2(v[k] * inv) * mask
            return 0
        lax.fori_loop(0, ng, descr, 0)

    def channel(k, _):
        for q in range(5):
            def val(t):
                ld = lambda m: desc[m, k, pl.ds(t * 8, 8), :]
                if q == 0:
                    return ld(0)
                if q == 1:
                    return ld(1)
                if q == 2:
                    v = ld(0)
                    return v * v
                if q == 3:
                    v = ld(1)
                    return v * v
                return ld(0) * ld(1)
            d = [val(t) for t in range(nd)]
            s2 = [d[t] + d[t + 1] for t in range(nd - 1)]
            s4 = [s2[t] + s2[t + 2] for t in range(nd - 3)]
            for f in range(nf):
                ys[q, pl.ds(f * 8, 8), :] = s4[f] + s4[f + 4] + d[f + 8]

        for g in range(nfg):
            base = g * 64
            for q in range(5):
                t = [ys[q, pl.ds(base + r, 8, stride=8), :] for r in range(8)]
                lo = (t[0] + t[1]) + (t[2] + t[3])
                hi = (t[4] + t[5]) + (t[6] + t[7])
                w = [None] * 8
                w[0] = lo + t[4]
                w[1] = w[0] + t[5]
                w[2] = w[1] + t[6]
                w[3] = lo + hi
                w[4] = w[3]
                w[7] = hi + t[3]
                w[6] = w[7] + t[2]
                w[5] = w[6] + t[1]
                hi, lo = split(jnp.concatenate(w, axis=0))
                at = pl.ds(q * nf * 8 + base, 64)
                lhs[at, 0:128] = hi
                lhs[at, 128:256] = lo
            a = [desc[0, k, pl.ds(base + 32 + r, 8, stride=8), :] for r in range(8)]
            hi, lo = split(jnp.concatenate(a, axis=0))
            at = pl.ds(5 * nf * 8 + base, 64)
            lhs[at, 0:128] = hi
            lhs[at, 128:256] = lo
        n5 = 5 * nf * 8
        res[0:n5] = jnp.dot(lhs[0:n5], mats[1], preferred_element_type=f32)
        res[n5:n5 + nf * 8] = jnp.dot(lhs[n5:n5 + nf * 8], mats[2], preferred_element_type=f32)

        for g in range(nfg):
            base = g * 64
            a = [desc[0, k, pl.ds(base + 32 + r, 8, stride=8), :] for r in range(8)]
            for r in range(8):
                mo, mm, so, sm, sc, gc = [res[pl.ds(q * nf * 8 + base + r * 8, 8), :] for q in range(6)]
                b = desc[1, k, pl.ds(base + 32 + r, 8, stride=8), :]
                vo = 729.0 * so - mo * mo + (1e-5 * 729.0 * 729.0)
                vm = 729.0 * sm - mm * mm + (1e-5 * 729.0 * 729.0)
                cv = 729.0 * sc - mo * mm
                io, im = lax.rsqrt(vo), lax.rsqrt(vm)
                coef = (729.0 * b - mm - (cv * io) * io * (729.0 * a[r] - mo)) * (io * im)
                gz = desc[0, k, pl.ds(base + 40 + r, 8, stride=8), :] - desc[0, k, pl.ds(base + 24 + r, 8, stride=8), :]
                if r == 0:
                    gr = a[1]
                elif r == 7:
                    gr = -a[6]
                else:
                    gr = a[r + 1] - a[r - 1]
                for c, gg in enumerate((gz, gr, gc)):
                    at = (c, pl.ds(base + r * 8, 8), slice(None))
                    frc[at] = frc[at] + coef * gg
        return 0
    frc[...] = jnp.zeros_like(frc)
    lax.fori_loop(0, 12, channel, 0)

    for c in range(3):
        scale = 729.0 / 24.0
        for g in range(nfg):
            for r in range(8):
                v = frc[c, pl.ds(g * 64 + r * 8, 8), :]
                if g == 0:
                    v = jnp.where(row >= 4, v, v * low)
                if g == nfg - 1:
                    v = jnp.where(row < 4, v, v * high)
                ys[0, pl.ds(g * 64 + r, 8, stride=8), :] = v
        for o in range(planes):
            p = [ys[0, pl.ds((o + 1 + j) * 8, 8), :] for j in range(7)]
            v = TAPS[3] * p[3]
            for j in range(3):
                v = v + TAPS[j] * (p[j] + p[6 - j])
            ys[1, pl.ds(o * 8, 8), :] = v
        for g in range(planes // 8):
            t = [ys[1, pl.ds(g * 64 + r, 8, stride=8), :] for r in range(8)]
            w = []
            for r in range(8):
                v = TAPS[3] * t[r]
                for j in range(1, 4):
                    n = [t[i] for i in (r - j, r + j) if 0 <= i < 8]
                    v = v + TAPS[3 + j] * (n[0] + n[1] if len(n) == 2 else n[0])
                w.append(v)
            hi, lo = split(jnp.concatenate(w, axis=0))
            lhs[pl.ds((c * planes + g * 8) * 8, 64), 0:128] = hi
            lhs[pl.ds((c * planes + g * 8) * 8, 64), 128:256] = lo
    n3 = 3 * planes * 8
    v = jnp.dot(lhs[0:n3], mats[3], preferred_element_type=f32)
    v = v + jnp.dot(lhs[0:n3, 0:128], mats[4, 0:128], preferred_element_type=f32)
    res[0:n3] = v
    for c in range(3):
        for g in range(planes // 8):
            for r in range(8):
                ys[0, pl.ds(g * 64 + r, 8, stride=8), :] = res[pl.ds((c * planes + g * 8 + r) * 8, 8), :]
        for o in range(planes):
            out[c, o] = vel[c, o] + (8.0 * scale) * ys[0, pl.ds(o * 8, 8), :]


EDGE = 13


def advect_kernel(planes, image, vel, warp, down, up):
    lane = lax.broadcasted_iota(jnp.int32, (8, 128), 1)
    row = lax.broadcasted_iota(jnp.int32, (8, 128), 0)

    def halves(x):
        hi = x.astype(bf16)
        return hi, (x - hi.astype(f32)).astype(bf16)

    for z in range(planes):
        x = image[0, z].astype(f32)
        before = image[0, z - 1].astype(f32) if z > 0 else x
        after = image[0, z + 1].astype(f32) if z < planes - 1 else x
        sides = (
            (before, after),
            (jnp.where(row >= 1, pltpu.roll(x, 1, 0), 0.0), jnp.where(row < 7, pltpu.roll(x, 7, 0), 0.0)),
            (jnp.where(lane >= 1, pltpu.roll(x, 1, 1), 0.0), jnp.where(lane < 127, pltpu.roll(x, 127, 1), 0.0)),
        )
        moved = 0.0
        for c, (lo, hi) in enumerate(sides):
            v = vel[0, c, z]
            moved = moved + (jnp.maximum(v, 0.0) * (x - lo) + jnp.minimum(v, 0.0) * (hi - x))
        y = x - moved
        warp[z] = y
        if z == 0 or z == planes - 1:
            ref, v = (down, jnp.maximum(vel[0, 0, z], 0.0)) if z == 0 else (up, jnp.minimum(vel[0, 0, z], 0.0))
            for n, part in enumerate(halves(y) + halves(v) + (image[0, z],)):
                ref[8 + n] = part
        if 1 <= z <= 8:
            down[z - 1] = y.astype(bf16)
        if planes - 9 <= z < planes - 1:
            up[z - (planes - 9)] = y.astype(bf16)


def widen_kernel(planes, warp, below, above, image, vel, out):
    has_low = lax.axis_index("slab") > 0
    has_high = lax.axis_index("slab") < lax.axis_size("slab") - 1
    ld = lambda ref, n: ref[n].astype(f32)
    first, last = image[0, 0].astype(f32), image[0, planes - 1].astype(f32)
    top = planes - 1
    for n in range(8):
        out[n] = below[n]
        out[planes + 10 + n] = above[n]
    out[8] = ((ld(below, 8) + ld(below, 9)) - (ld(below, 10) + ld(below, 11)) * (first - ld(below, 12))).astype(bf16)
    out[planes + 9] = ((ld(above, 8) + ld(above, 9)) - (ld(above, 10) + ld(above, 11)) * (ld(above, 12) - last)).astype(bf16)
    for z in range(1, top):
        out[9 + z] = warp[z].astype(bf16)
    out[9] = (warp[0] - jnp.maximum(vel[0, 0, 0], 0.0) * (first - ld(below, 12))).astype(bf16)
    out[9 + top] = (warp[top] - jnp.minimum(vel[0, 0, top], 0.0) * (ld(above, 12) - last)).astype(bf16)
    zero = jnp.zeros((9, 8, 128), bf16)

    @pl.when(jnp.logical_not(has_low))
    def _():
        out[0:9] = zero

    @pl.when(jnp.logical_not(has_high))
    def _():
        out[planes + 9:planes + 18] = zero


def shards(intensity, velocity, partner, offsets):
    planes = intensity.shape[1]
    slabs, brains = lax.axis_size("slab"), lax.axis_size("brain")
    vm = pl.BlockSpec(memory_space=pltpu.VMEM)
    edge = jax.ShapeDtypeStruct((EDGE, 8, 128), bf16)
    warp, down, up = pl.pallas_call(
        functools.partial(advect_kernel, planes),
        out_shape=(jax.ShapeDtypeStruct((planes, 8, 128), f32), edge, edge),
        in_specs=[vm, vm],
        out_specs=(vm, vm, vm),
        compiler_params=pltpu.CompilerParams(vmem_limit_bytes=8 * 2**20),
        name="advect",
    )(intensity, velocity)
    below = lax.ppermute(up, "slab", [(n, n + 1) for n in range(slabs - 1)])
    above = lax.ppermute(down, "slab", [(n + 1, n) for n in range(slabs - 1)])
    own = pl.pallas_call(
        functools.partial(widen_kernel, planes),
        out_shape=jax.ShapeDtypeStruct((planes + 18, 8, 128), bf16),
        in_specs=[vm] * 5,
        out_specs=vm,
        compiler_params=pltpu.CompilerParams(vmem_limit_bytes=8 * 2**20),
        name="widen",
    )(warp, below, above, intensity, velocity)
    me = lax.axis_index("brain")
    mate = partner[me]
    if brains == 4:
        mates = [lax.ppermute(own, "brain", [(n, n ^ k) for n in range(4)]) for k in (1, 2, 3)]
        which = me ^ mate
    else:
        gathered = lax.all_gather(own, "brain")
        mates = [lax.dynamic_index_in_dim(gathered, mate, 0, keepdims=False)] * 3
        which = jnp.int32(1)
    slab = lax.axis_index("slab")
    shift = offsets[mate] - offsets[me]
    meta = jnp.stack([which, shift[0], shift[1], (slab > 0).astype(jnp.int32), (slab < slabs - 1).astype(jnp.int32)])
    nx, nd, nf = planes + 18, planes + 16, planes + 8
    return pl.pallas_call(
        functools.partial(main_kernel, planes),
        out_shape=jax.ShapeDtypeStruct(velocity.shape[1:], f32),
        in_specs=[pl.BlockSpec(memory_space=pltpu.SMEM)] + [vm] * 5,
        out_specs=vm,
        scratch_shapes=[
            pltpu.VMEM((5, 256, 128), bf16),
            pltpu.VMEM((2, 5, nx * 8, 128), f32),
            pltpu.VMEM((3, nx * 8 + 16, 128), f32),
            pltpu.VMEM((12, (nd + 1) * 8, 128), f32),
            pltpu.VMEM((2, 12, nd * 8, 128), f32),
            pltpu.VMEM((5, max(nf * 8, 768), 128), f32),
            pltpu.VMEM((6 * nf * 8, 256), bf16),
            pltpu.VMEM((6 * nf * 8, 128), f32),
            pltpu.VMEM((3, nf * 8, 128), f32),
        ],
        compiler_params=pltpu.CompilerParams(vmem_limit_bytes=32 * 2**20),
        name="force",
    )(meta, own.reshape(-1, 128), *[m.reshape(-1, 128) for m in mates], velocity[0])[None]


def solution(mesh):
    return jax.shard_map(
        shards,
        mesh=mesh,
        in_specs=(
            P(("groups", "brain"), "slab", None, None),
            P(("groups", "brain"), None, "slab", None, None),
            P("groups"),
            P("groups", None),
        ),
        out_specs=P(("groups", "brain"), None, "slab", None, None),
        check_vma=False,
    )
```

```python
import functools
import jax, jax.numpy as jnp, numpy as np
from jax import lax
from jax.experimental import pallas as pl
from jax.experimental.pallas import tpu as pltpu
from jax.sharding import PartitionSpec as P

PAIRS = tuple((i, j) for i in range(6) for j in range(i + 1, 6) if i // 2 != j // 2)
TAPS = tuple(float(v) for v in np.exp(-np.arange(-3, 4) ** 2 / 4.5) / np.exp(-np.arange(-3, 4) ** 2 / 4.5).sum())
f32, bf16 = jnp.float32, jnp.bfloat16
LOG2E = 1.4426950408889634
EDGE = 13
VOLUME = 729.0
FLOOR = 1e-5 * VOLUME * VOLUME


def split(v):
    hi = v.astype(bf16)
    return hi, (v - hi.astype(f32)).astype(bf16)


def lanes():
    return (lax.broadcasted_iota(jnp.int32, (128, 128), 0), lax.broadcasted_iota(jnp.int32, (128, 128), 1))


def ones_where(cond):
    return jnp.where(cond, 1.0, 0.0).astype(bf16)


def put_split(lhs, start, parts):
    hi, lo = split(jnp.concatenate(parts, axis=0))
    at = pl.ds(start, 8 * len(parts))
    lhs[at, 0:128] = hi
    lhs[at, 128:256] = lo


def dot(a, b):
    return jnp.dot(a, b, preferred_element_type=f32)


def faces():
    slab = lax.axis_index("slab")
    one = jnp.float32(1.0)
    zero = jnp.float32(0.0)
    return jnp.where(slab > 0, one, zero), jnp.where(slab < lax.axis_size("slab") - 1, one, zero)


def row_inside(d):
    row = lax.broadcasted_iota(jnp.int32, (8, 128), 0)
    return (row + d >= 0) & (row + d < 8)


def describe(planes, xs, box3, tb, lhs, dst, desc, low, high):
    nd = planes + 16
    ng = nd // 8

    def squares(g, carry):
        c1, c2 = carry
        scale = jnp.where(g == 0, low, jnp.where(g == ng - 1, high, 1.0))
        for i in range(8):
            s = g * 8 + i
            ld = lambda n, p: xs[n, pl.ds(pl.multiple_of(p * 8, 8), 8), :]
            near = [ld(0, s + 2), ld(0, s)] + [ld(j, s + 1) for j in (1, 2, 3, 4)]
            n1, n2 = [], []
            for k, (a, b) in enumerate(PAIRS):
                d = near[a] - near[b]
                q = d * d * scale
                tb[k, pl.ds(pl.multiple_of(s * 8, 8), 8), :] = c2[k] + q
                n2.append(c1[k] + q)
                n1.append(q)
            c1, c2 = n1, n2
        return c1, c2
    zero = [jnp.zeros((8, 128), f32)] * 12
    c1, c2 = lax.fori_loop(0, ng, squares, (zero, zero))
    for k in range(12):
        tb[k, pl.ds(nd * 8, 8), :] = c2[k]

    def rows(g):
        for k in range(12):
            t = [tb[k, pl.ds(g * 64 + 8 + r, 8, stride=8), :] for r in range(8)]
            p = [t[r] + t[r + 1] for r in range(7)]
            w = [p[0]] + [p[r - 1] + t[r + 1] for r in range(1, 7)] + [p[6]]
            put_split(lhs, (g % 2) * 768 + k * 64, w)

    rows(0)
    for g in range(ng):
        h = g % 2
        if g + 1 < ng:
            rows(g + 1)
        dst[h * 768:h * 768 + 768] = dot(lhs[h * 768:h * 768 + 768], box3[...])
        for r in range(8):
            v = [dst[pl.ds(h * 768 + k * 64 + r * 8, 8), :] for k in range(12)]
            total = functools.reduce(jnp.add, v)
            inv = (-LOG2E / 27.0) / (total * (1.0 / 324.0) + 0.1)
            for k in range(12):
                e = jnp.exp2(v[k] * inv)
                if g == 0:
                    e = e * low
                if g == ng - 1:
                    e = e * high
                desc[k, pl.ds(g * 64 + r, 8, stride=8), :] = e


def depth_sums(planes, value, ys, q):
    nd, nf = planes + 16, planes + 8
    d = [value(t) for t in range(nd)]
    s2 = [d[t] + d[t + 1] for t in range(nd - 1)]
    s4 = [s2[t] + s2[t + 2] for t in range(nd - 3)]
    for f in range(nf):
        ys[q, pl.ds(f * 8, 8), :] = s4[f] + s4[f + 4] + d[f + 8]


def row_sums(planes, ys, lhs, count):
    nf = planes + 8
    for g in range(nf // 8):
        for q in range(count):
            t = [ys[q, pl.ds(g * 64 + r, 8, stride=8), :] for r in range(8)]
            lo = (t[0] + t[1]) + (t[2] + t[3])
            hi = (t[4] + t[5]) + (t[6] + t[7])
            w = [None] * 8
            w[0] = lo + t[4]
            w[1] = w[0] + t[5]
            w[2] = w[1] + t[6]
            w[3] = lo + hi
            w[4] = w[3]
            w[7] = hi + t[3]
            w[6] = w[7] + t[2]
            w[5] = w[6] + t[1]
            put_split(lhs, q * nf * 8 + g * 64, w)


def over_channels(sums, rows, product, use):
    sums(0)
    rows(0)

    def step(k, _):
        product(k)
        sums(k + 1)
        use(k)
        rows(k + 1)
        return 0
    lax.fori_loop(0, 11, step, 0)
    product(11)
    use(11)


def own_kernel(planes, own, desc, mean, slope, grads, box3, box9, grad, xs, tb, ys, lhs, dst, res):
    nx, nd, nf = planes + 18, planes + 16, planes + 8
    low, high = faces()
    i, j = lanes()
    for h in (0, 128):
        box3[h:h + 128] = ones_where(jnp.abs(i - j) <= 1)
        box9[h:h + 128] = ones_where(jnp.abs(i - j) <= 4)
        grad[h:h + 128] = jnp.where(i == j + 1, 1.0, jnp.where(i == j - 1, -1.0, 0.0)).astype(bf16)
    x = own[...]
    xs[0] = x.astype(f32)
    xs[3] = dot(x, ones_where(i == j + 1))
    xs[4] = dot(x, ones_where(i == j - 1))

    def prep(p, _):
        at = pl.ds(pl.multiple_of(p * 8, 8), 8)
        v = xs[0, at, :]
        xs[1, at, :] = jnp.where(row_inside(1), pltpu.roll(v, 7, 0), 0.0)
        xs[2, at, :] = jnp.where(row_inside(-1), pltpu.roll(v, 1, 0), 0.0)
        return 0
    lax.fori_loop(0, nx, prep, 0, unroll=6)
    describe(planes, xs, box3, tb, lhs, dst, desc, low, high)

    def sums(k):
        ld = lambda t: desc[k, pl.ds(t * 8, 8), :]
        depth_sums(planes, ld, ys, 0)
        depth_sums(planes, lambda t: ld(t) * ld(t), ys, 1)

    def rows(k):
        row_sums(planes, ys, lhs, 2)
        for g in range(nf // 8):
            put_split(lhs, 2 * nf * 8 + g * 64, [desc[k, pl.ds(g * 64 + 32 + r, 8, stride=8), :] for r in range(8)])

    def product(k):
        n = 2 * nf * 8
        res[0:n] = dot(lhs[0:n], box9[...])
        res[n:n + nf * 8] = dot(lhs[n:n + nf * 8], grad[...])

    def use(k):
        for g in range(nf // 8):
            a = [desc[k, pl.ds(g * 64 + 32 + r, 8, stride=8), :] for r in range(8)]
            for r in range(8):
                at = pl.ds(g * 64 + r * 8, 8)
                mo, so, gc = [res[pl.ds(q * nf * 8 + g * 64 + r * 8, 8), :] for q in range(3)]
                inv = lax.rsqrt(VOLUME * so - mo * mo + FLOOR)
                gz = desc[k, pl.ds(g * 64 + 40 + r, 8, stride=8), :] - desc[k, pl.ds(g * 64 + 24 + r, 8, stride=8), :]
                gr = a[1] if r == 0 else -a[6] if r == 7 else a[r + 1] - a[r - 1]
                mean[k, at, :] = mo
                slope[k, at, :] = (inv * inv) * (VOLUME * a[r] - mo)
                for c, gg in enumerate((gz, gr, gc)):
                    grads[c, k, at, :] = gg * inv
    over_channels(sums, rows, product, use)


def mate_kernel(planes, count, partner, offsets, *refs):
    mates = refs[:count]
    adesc, mean, slope, grads, vel, out, box3, box9, smooth, xs, raw, tb, desc, ys, lhs, dst, res, frc = refs[count:]
    nx, nd, nf = planes + 18, planes + 16, planes + 8
    low, high = faces()
    me = lax.axis_index("brain")
    mate = partner[me]
    dr = offsets[mate, 0] - offsets[me, 0]
    dc = offsets[mate, 1] - offsets[me, 1]
    i, j = lanes()
    weights = jnp.zeros((128, 128), f32)
    for d in range(4):
        weights = jnp.where(jnp.abs(i - j) == d, TAPS[3 + d], weights)
    whi, wlo = split(weights)
    for h in (0, 128):
        box3[h:h + 128] = ones_where(jnp.abs(i - j) <= 1)
        box9[h:h + 128] = ones_where(jnp.abs(i - j) <= 4)
        smooth[h:h + 128] = whi
    smooth[256:384] = wlo
    row = lax.broadcasted_iota(jnp.int32, (8, 128), 0)

    x = mates[0][...]
    for n in range(1, count):
        x = jnp.where((me ^ mate) == n + 1, mates[n][...], x)
    for n, d in ((0, 0), (1, 1), (2, -1)):
        take = ones_where((i == j + d + dc) & (j + d >= 0) & (j + d < 128))
        raw[n, pl.ds(8, nx * 8), :] = dot(x, take)

    def prep(p, _):
        at = pl.multiple_of(p * 8, 8)
        for n, b, d in ((0, 0, 0), (1, 0, 1), (2, 0, -1), (3, 1, 0), (4, 2, 0)):
            v = raw[b, pl.ds(at + 8 + dr + d, 8), :]
            xs[n, pl.ds(at, 8), :] = jnp.where(row_inside(d) & row_inside(d + dr), v, 0.0)
        return 0
    lax.fori_loop(0, nx, prep, 0, unroll=6)
    describe(planes, xs, box3, tb, lhs, dst, desc, low, high)

    def sums(k):
        lda = lambda t: adesc[k, pl.ds(t * 8, 8), :]
        ldb = lambda t: desc[k, pl.ds(t * 8, 8), :]
        depth_sums(planes, ldb, ys, 0)
        depth_sums(planes, lambda t: ldb(t) * ldb(t), ys, 1)
        depth_sums(planes, lambda t: lda(t) * ldb(t), ys, 2)

    def rows(k):
        row_sums(planes, ys, lhs, 3)

    def product(k):
        res[0:3 * nf * 8] = dot(lhs[0:3 * nf * 8], box9[...])

    def use(k):
        for g in range(nf // 8):
            for r in range(8):
                at = pl.ds(g * 64 + r * 8, 8)
                mm, sm, sc = [res[pl.ds(q * nf * 8 + g * 64 + r * 8, 8), :] for q in range(3)]
                b = desc[k, pl.ds(g * 64 + 32 + r, 8, stride=8), :]
                inv = lax.rsqrt(VOLUME * sm - mm * mm + FLOOR)
                cov = VOLUME * sc - mean[k, at, :] * mm
                coef = (VOLUME * b - mm - cov * slope[k, at, :]) * inv
                for c in range(3):
                    frc[c, at, :] = frc[c, at, :] + coef * grads[c, k, at, :]
    frc[...] = jnp.zeros_like(frc)
    over_channels(sums, rows, product, use)

    for c in range(3):
        for g in range(nf // 8):
            for r in range(8):
                v = frc[c, pl.ds(g * 64 + r * 8, 8), :]
                if g == 0:
                    v = jnp.where(row >= 4, v, v * low)
                if g == nf // 8 - 1:
                    v = jnp.where(row < 4, v, v * high)
                ys[0, pl.ds(g * 64 + r, 8, stride=8), :] = v
        for o in range(planes):
            p = [ys[0, pl.ds((o + 1 + n) * 8, 8), :] for n in range(7)]
            v = TAPS[3] * p[3]
            for n in range(3):
                v = v + TAPS[n] * (p[n] + p[6 - n])
            ys[1, pl.ds(o * 8, 8), :] = v
        for g in range(planes // 8):
            t = [ys[1, pl.ds(g * 64 + r, 8, stride=8), :] for r in range(8)]
            w = []
            for r in range(8):
                v = TAPS[3] * t[r]
                for n in range(1, 4):
                    s = [t[q] for q in (r - n, r + n) if 0 <= q < 8]
                    v = v + TAPS[3 + n] * (s[0] + s[1] if len(s) == 2 else s[0])
                w.append(v)
            put_split(lhs, (c * planes + g * 8) * 8, w)
    n3 = 3 * planes * 8
    res[0:n3] = dot(lhs[0:n3], smooth[0:256]) + dot(lhs[0:n3, 0:128], smooth[256:384])
    for c in range(3):
        for g in range(planes // 8):
            for r in range(8):
                ys[0, pl.ds(g * 64 + r, 8, stride=8), :] = res[pl.ds((c * planes + g * 8 + r) * 8, 8), :]
        for o in range(planes):
            out[c, o] = vel[c, o] + (8.0 * VOLUME / 24.0) * ys[0, pl.ds(o * 8, 8), :]


VM = pl.BlockSpec(memory_space=pltpu.VMEM)
SM = pl.BlockSpec(memory_space=pltpu.SMEM)


def own_part(planes, own):
    nx, nd, nf = planes + 18, planes + 16, planes + 8
    shape = jax.ShapeDtypeStruct
    return pl.pallas_call(
        functools.partial(own_kernel, planes),
        out_shape=(
            shape((12, nd * 8, 128), f32),
            shape((12, nf * 8, 128), f32),
            shape((12, nf * 8, 128), f32),
            shape((3, 12, nf * 8, 128), f32),
        ),
        in_specs=[VM],
        out_specs=(VM,) * 4,
        scratch_shapes=[
            pltpu.VMEM((256, 128), bf16),
            pltpu.VMEM((256, 128), bf16),
            pltpu.VMEM((256, 128), bf16),
            pltpu.VMEM((5, nx * 8, 128), f32),
            pltpu.VMEM((12, (nd + 1) * 8, 128), f32),
            pltpu.VMEM((2, nf * 8, 128), f32),
            pltpu.VMEM((max(1536, 3 * nf * 8), 256), bf16),
            pltpu.VMEM((1536, 128), f32),
            pltpu.VMEM((3 * nf * 8, 128), f32),
        ],
        compiler_params=pltpu.CompilerParams(vmem_limit_bytes=16 * 2**20),
        cost_estimate=pl.CostEstimate(flops=6 * 10**8, bytes_accessed=16 * 2**20, transcendentals=10**6),
        name="own",
    )(own.reshape(-1, 128))


def mate_part(planes, partner, offsets, mates, owned, vel):
    nx, nd, nf = planes + 18, planes + 16, planes + 8
    count = len(mates)
    return pl.pallas_call(
        functools.partial(mate_kernel, planes, count),
        out_shape=jax.ShapeDtypeStruct(vel.shape, f32),
        in_specs=[SM, SM] + [VM] * (count + 5),
        out_specs=VM,
        scratch_shapes=[
            pltpu.VMEM((256, 128), bf16),
            pltpu.VMEM((256, 128), bf16),
            pltpu.VMEM((384, 128), bf16),
            pltpu.VMEM((5, nx * 8, 128), f32),
            pltpu.VMEM((3, nx * 8 + 16, 128), f32),
            pltpu.VMEM((12, (nd + 1) * 8, 128), f32),
            pltpu.VMEM((12, nd * 8, 128), f32),
            pltpu.VMEM((3, nf * 8, 128), f32),
            pltpu.VMEM((max(1536, 3 * nf * 8), 256), bf16),
            pltpu.VMEM((1536, 128), f32),
            pltpu.VMEM((3 * nf * 8, 128), f32),
            pltpu.VMEM((3, nf * 8, 128), f32),
        ],
        compiler_params=pltpu.CompilerParams(vmem_limit_bytes=16 * 2**20),
        name="mate",
    )(partner, offsets, *[m.reshape(-1, 128) for m in mates], *owned, vel)


def advect_kernel(planes, image, vel, warp, down, up):
    lane = lax.broadcasted_iota(jnp.int32, (8, 128), 1)

    for z in range(planes):
        x = image[0, z].astype(f32)
        before = image[0, z - 1].astype(f32) if z > 0 else x
        after = image[0, z + 1].astype(f32) if z < planes - 1 else x
        sides = (
            (before, after),
            (jnp.where(row_inside(-1), pltpu.roll(x, 1, 0), 0.0), jnp.where(row_inside(1), pltpu.roll(x, 7, 0), 0.0)),
            (jnp.where(lane >= 1, pltpu.roll(x, 1, 1), 0.0), jnp.where(lane < 127, pltpu.roll(x, 127, 1), 0.0)),
        )
        moved = 0.0
        for c, (lo, hi) in enumerate(sides):
            v = vel[0, c, z]
            moved = moved + (jnp.maximum(v, 0.0) * (x - lo) + jnp.minimum(v, 0.0) * (hi - x))
        y = x - moved
        warp[z] = y
        if z == 0 or z == planes - 1:
            ref, v = (down, jnp.maximum(vel[0, 0, z], 0.0)) if z == 0 else (up, jnp.minimum(vel[0, 0, z], 0.0))
            for n, part in enumerate(split(y) + split(v) + (image[0, z],)):
                ref[8 + n] = part
        if 1 <= z <= 8:
            down[z - 1] = y.astype(bf16)
        if planes - 9 <= z < planes - 1:
            up[z - (planes - 9)] = y.astype(bf16)


def widen_kernel(planes, warp, below, above, image, vel, out):
    low, high = faces()
    ld = lambda ref, n: ref[n].astype(f32)
    first, last = image[0, 0].astype(f32), image[0, planes - 1].astype(f32)
    top = planes - 1
    for n in range(8):
        out[n] = (ld(below, n) * low).astype(bf16)
        out[planes + 10 + n] = (ld(above, n) * high).astype(bf16)
    out[8] = (low * ((ld(below, 8) + ld(below, 9)) - (ld(below, 10) + ld(below, 11)) * (first - ld(below, 12)))).astype(bf16)
    out[planes + 9] = (high * ((ld(above, 8) + ld(above, 9)) - (ld(above, 10) + ld(above, 11)) * (ld(above, 12) - last))).astype(bf16)
    for z in range(1, top):
        out[9 + z] = warp[z].astype(bf16)
    out[9] = (warp[0] - jnp.maximum(vel[0, 0, 0], 0.0) * (first - ld(below, 12))).astype(bf16)
    out[9 + top] = (warp[top] - jnp.minimum(vel[0, 0, top], 0.0) * (ld(above, 12) - last)).astype(bf16)


def shards(intensity, velocity, partner, offsets):
    planes = intensity.shape[1]
    slabs, brains = lax.axis_size("slab"), lax.axis_size("brain")
    edge = jax.ShapeDtypeStruct((EDGE, 8, 128), bf16)
    warp, down, up = pl.pallas_call(
        functools.partial(advect_kernel, planes),
        out_shape=(jax.ShapeDtypeStruct((planes, 8, 128), f32), edge, edge),
        in_specs=[VM, VM],
        out_specs=(VM,) * 3,
        compiler_params=pltpu.CompilerParams(vmem_limit_bytes=8 * 2**20),
        name="advect",
    )(intensity, velocity)
    below = lax.ppermute(up, "slab", [(n, n + 1) for n in range(slabs - 1)])
    above = lax.ppermute(down, "slab", [(n + 1, n) for n in range(slabs - 1)])
    own = pl.pallas_call(
        functools.partial(widen_kernel, planes),
        out_shape=jax.ShapeDtypeStruct((planes + 18, 8, 128), bf16),
        in_specs=[VM] * 5,
        out_specs=VM,
        compiler_params=pltpu.CompilerParams(vmem_limit_bytes=8 * 2**20),
        name="widen",
    )(warp, below, above, intensity, velocity)
    if brains == 4:
        mates = [lax.ppermute(own, "brain", [(n, n ^ k) for n in range(4)]) for k in (1, 2, 3)]
    else:
        gathered = lax.all_gather(own, "brain")
        mates = [lax.dynamic_index_in_dim(gathered, partner[lax.axis_index("brain")], 0, keepdims=False)]
    return mate_part(planes, partner, offsets, mates, own_part(planes, own), velocity[0])[None]


def solution(mesh):
    return jax.shard_map(
        shards,
        mesh=mesh,
        in_specs=(
            P(("groups", "brain"), "slab", None, None),
            P(("groups", "brain"), None, "slab", None, None),
            P("groups"),
            P("groups", None),
        ),
        out_specs=P(("groups", "brain"), None, "slab", None, None),
        check_vma=False,
    )
```

```python
import functools
import jax, jax.numpy as jnp, numpy as np
from jax import lax
from jax.experimental import pallas as pl
from jax.experimental.pallas import tpu as pltpu
from jax.sharding import PartitionSpec as P

PAIRS = tuple((i, j) for i in range(6) for j in range(i + 1, 6) if i // 2 != j // 2)
TAPS = tuple(float(v) for v in np.exp(-np.arange(-3, 4) ** 2 / 4.5) / np.exp(-np.arange(-3, 4) ** 2 / 4.5).sum())
f32, bf16 = jnp.float32, jnp.bfloat16
LOG2E = 1.4426950408889634
EDGE = 13
VOLUME = 729.0
UNROLL = 2
FLOOR = 1e-5 * VOLUME * VOLUME


def split(v):
    hi = v.astype(bf16)
    return hi, (v - hi.astype(f32)).astype(bf16)


def lanes():
    return (lax.broadcasted_iota(jnp.int32, (128, 128), 0), lax.broadcasted_iota(jnp.int32, (128, 128), 1))


def ones_where(cond):
    return jnp.where(cond, 1.0, 0.0).astype(bf16)


def halves(parts):
    return jnp.concatenate(split(jnp.concatenate(parts, axis=0)), axis=1)


def dot(a, b):
    return jnp.dot(a, b, preferred_element_type=f32)


def faces():
    slab = lax.axis_index("slab")
    one = jnp.float32(1.0)
    zero = jnp.float32(0.0)
    return jnp.where(slab > 0, one, zero), jnp.where(slab < lax.axis_size("slab") - 1, one, zero)


def row_inside(d):
    row = lax.broadcasted_iota(jnp.int32, (8, 128), 0)
    return (row + d >= 0) & (row + d < 8)


def describe(planes, xs, box3, tb, desc, low, high):
    nd = planes + 16
    ng = nd // 8

    def squares(g, carry):
        c1, c2 = carry
        scale = jnp.where(g == 0, low, jnp.where(g == ng - 1, high, 1.0))
        for i in range(8):
            s = g * 8 + i
            ld = lambda n, p: xs[n, pl.ds(pl.multiple_of(p * 8, 8), 8), :]
            near = [ld(0, s + 2), ld(0, s)] + [ld(j, s + 1) for j in (1, 2, 3, 4)]
            n1, n2 = [], []
            for k, (a, b) in enumerate(PAIRS):
                d = near[a] - near[b]
                q = d * d * scale
                tb[k, pl.ds(pl.multiple_of(s * 8, 8), 8), :] = c2[k] + q
                n2.append(c1[k] + q)
                n1.append(q)
            c1, c2 = n1, n2
        return c1, c2
    zero = [jnp.zeros((8, 128), f32)] * 12
    c1, c2 = lax.fori_loop(0, ng, squares, (zero, zero))
    for k in range(12):
        tb[k, pl.ds(nd * 8, 8), :] = c2[k]

    for g in range(ng):
        parts = []
        for r in range(8):
            for k in range(12):
                t = [tb[k, pl.ds(g * 64 + 8 + n, 8, stride=8), :] for n in (r - 1, r, r + 1) if 0 <= n < 8]
                parts.append(functools.reduce(jnp.add, t))
        box = dot(halves(parts), box3[...])
        for r in range(8):
            v = [box[(r * 12 + k) * 8:(r * 12 + k) * 8 + 8] for k in range(12)]
            total = functools.reduce(jnp.add, v)
            inv = (-LOG2E / 27.0) / (total * (1.0 / 324.0) + 0.1)
            for k in range(12):
                e = jnp.exp2(v[k] * inv)
                if g == 0:
                    e = e * low
                if g == ng - 1:
                    e = e * high
                desc[k, pl.ds(g * 64 + r, 8, stride=8), :] = e


def depth_sums(planes, value, ys, q):
    nd, nf = planes + 16, planes + 8
    d = [value(t) for t in range(nd)]
    for f in range(nf):
        if f % 16 == 0:
            s2 = [d[f + t] + d[f + t + 1] for t in (0, 2, 4, 6)]
            total = ((s2[0] + s2[1]) + (s2[2] + s2[3])) + d[f + 8]
        else:
            total = (total - d[f - 1]) + d[f + 8]
        ys[q, pl.ds(f * 8, 8), :] = total


def row_sums(ys, q, g):
    t = [ys[q, pl.ds(g * 64 + r, 8, stride=8), :] for r in range(8)]
    lo = (t[0] + t[1]) + (t[2] + t[3])
    hi = (t[4] + t[5]) + (t[6] + t[7])
    w0 = lo + t[4]
    w1 = w0 + t[5]
    w7 = hi + t[3]
    w6 = w7 + t[2]
    return [w0, w1, w1 + t[6], lo + hi, lo + hi, w6 + t[1], w6, w7]


def own_kernel(planes, own, desc, mean, slope, grads, box3, box9, grad, xs, tb, ys):
    nx, nd, nf = planes + 18, planes + 16, planes + 8
    low, high = faces()
    i, j = lanes()
    for h in (0, 128):
        box3[h:h + 128] = ones_where(jnp.abs(i - j) <= 1)
        box9[h:h + 128] = ones_where(jnp.abs(i - j) <= 4)
        grad[h:h + 128] = jnp.where(i == j + 1, 1.0, jnp.where(i == j - 1, -1.0, 0.0)).astype(bf16)
    x = own[...]
    xs[0] = x.astype(f32)
    xs[3] = dot(x, ones_where(i == j + 1))
    xs[4] = dot(x, ones_where(i == j - 1))

    def prep(p, _):
        at = pl.ds(pl.multiple_of(p * 8, 8), 8)
        v = xs[0, at, :]
        xs[1, at, :] = jnp.where(row_inside(1), pltpu.roll(v, 7, 0), 0.0)
        xs[2, at, :] = jnp.where(row_inside(-1), pltpu.roll(v, 1, 0), 0.0)
        return 0
    lax.fori_loop(0, nx, prep, 0, unroll=6)
    describe(planes, xs, box3, tb, desc, low, high)

    def channels(k, _):
        for h in range(UNROLL):
            one_channel(UNROLL * k + h, h)
        return 0

    def one_channel(k, h):
        ld = lambda t: desc[k, pl.ds(t * 8, 8), :]
        depth_sums(planes, ld, ys, 2 * h)
        depth_sums(planes, lambda t: ld(t) * ld(t), ys, 2 * h + 1)
        parts, centre = [], []
        for g in range(nf // 8):
            for q in range(2):
                parts += row_sums(ys, 2 * h + q, g)
            centre += [desc[k, pl.ds(g * 64 + 32 + r, 8, stride=8), :] for r in range(8)]
        sums = dot(halves(parts), box9[...])
        across = dot(halves(centre), grad[...])
        for g in range(nf // 8):
            a = centre[g * 8:g * 8 + 8]
            for r in range(8):
                at = pl.ds(g * 64 + r * 8, 8)
                mo, so = [sums[(g * 16 + q * 8 + r) * 8:(g * 16 + q * 8 + r) * 8 + 8] for q in range(2)]
                gc = across[(g * 8 + r) * 8:(g * 8 + r) * 8 + 8]
                inv = lax.rsqrt(VOLUME * so - mo * mo + FLOOR)
                gz = desc[k, pl.ds(g * 64 + 40 + r, 8, stride=8), :] - desc[k, pl.ds(g * 64 + 24 + r, 8, stride=8), :]
                gr = a[1] if r == 0 else -a[6] if r == 7 else a[r + 1] - a[r - 1]
                mean[k, at, :] = mo
                slope[k, at, :] = (inv * inv) * (VOLUME * a[r] - mo)
                for c, gg in enumerate((gz, gr, gc)):
                    grads[c, k, at, :] = gg * inv
    lax.fori_loop(0, 12 // UNROLL, channels, 0)


def mate_kernel(planes, count, partner, offsets, *refs):
    mates = refs[:count]
    adesc, mean, slope, grads, vel, out, box3, box9, smooth, xs, raw, tb, desc, ys, frc = refs[count:]
    nx, nd, nf = planes + 18, planes + 16, planes + 8
    low, high = faces()
    me = lax.axis_index("brain")
    mate = partner[me]
    dr = offsets[0, mate] - offsets[0, me]
    dc = offsets[1, mate] - offsets[1, me]
    i, j = lanes()
    weights = jnp.zeros((128, 128), f32)
    for d in range(4):
        weights = jnp.where(jnp.abs(i - j) == d, TAPS[3 + d], weights)
    whi, wlo = split(weights)
    for h in (0, 128):
        box3[h:h + 128] = ones_where(jnp.abs(i - j) <= 1)
        box9[h:h + 128] = ones_where(jnp.abs(i - j) <= 4)
        smooth[h:h + 128] = whi
    smooth[256:384] = wlo
    row = lax.broadcasted_iota(jnp.int32, (8, 128), 0)

    x = mates[0][...]
    for n in range(1, count):
        x = jnp.where((me ^ mate) == n + 1, mates[n][...], x)
    for n, d in ((0, 0), (1, 1), (2, -1)):
        take = ones_where((i == j + d + dc) & (j + d >= 0) & (j + d < 128))
        raw[n, pl.ds(8, nx * 8), :] = dot(x, take)

    def prep(p, _):
        at = pl.multiple_of(p * 8, 8)
        for n, b, d in ((0, 0, 0), (1, 0, 1), (2, 0, -1), (3, 1, 0), (4, 2, 0)):
            v = raw[b, pl.ds(at + 8 + dr + d, 8), :]
            xs[n, pl.ds(at, 8), :] = jnp.where(row_inside(d) & row_inside(d + dr), v, 0.0)
        return 0
    lax.fori_loop(0, nx, prep, 0, unroll=6)
    describe(planes, xs, box3, tb, desc, low, high)

    def channels(k, _):
        for h in range(UNROLL):
            one_channel(UNROLL * k + h, h)
        return 0

    def one_channel(k, h):
        lda = lambda t: adesc[k, pl.ds(t * 8, 8), :]
        ldb = lambda t: desc[k, pl.ds(t * 8, 8), :]
        depth_sums(planes, ldb, ys, 3 * h)
        depth_sums(planes, lambda t: ldb(t) * ldb(t), ys, 3 * h + 1)
        depth_sums(planes, lambda t: lda(t) * ldb(t), ys, 3 * h + 2)
        parts = []
        for g in range(nf // 8):
            for q in range(3):
                parts += row_sums(ys, 3 * h + q, g)
        sums = dot(halves(parts), box9[...])
        for g in range(nf // 8):
            for r in range(8):
                at = pl.ds(g * 64 + r * 8, 8)
                mm, sm, sc = [sums[(g * 24 + q * 8 + r) * 8:(g * 24 + q * 8 + r) * 8 + 8] for q in range(3)]
                b = desc[k, pl.ds(g * 64 + 32 + r, 8, stride=8), :]
                inv = lax.rsqrt(VOLUME * sm - mm * mm + FLOOR)
                cov = VOLUME * sc - mean[k, at, :] * mm
                coef = (VOLUME * b - mm - cov * slope[k, at, :]) * inv
                for c in range(3):
                    frc[c, at, :] = frc[c, at, :] + coef * grads[c, k, at, :]
    frc[...] = jnp.zeros_like(frc)
    lax.fori_loop(0, 12 // UNROLL, channels, 0)

    parts = []
    for c in range(3):
        for g in range(nf // 8):
            for r in range(8):
                v = frc[c, pl.ds(g * 64 + r * 8, 8), :]
                if g == 0:
                    v = jnp.where(row >= 4, v, v * low)
                if g == nf // 8 - 1:
                    v = jnp.where(row < 4, v, v * high)
                ys[0, pl.ds(g * 64 + r, 8, stride=8), :] = v
        for o in range(planes):
            p = [ys[0, pl.ds((o + 1 + n) * 8, 8), :] for n in range(7)]
            v = TAPS[3] * p[3]
            for n in range(3):
                v = v + TAPS[n] * (p[n] + p[6 - n])
            ys[1, pl.ds(o * 8, 8), :] = v
        for g in range(planes // 8):
            t = [ys[1, pl.ds(g * 64 + r, 8, stride=8), :] for r in range(8)]
            for r in range(8):
                v = TAPS[3] * t[r]
                for n in range(1, 4):
                    s = [t[q] for q in (r - n, r + n) if 0 <= q < 8]
                    v = v + TAPS[3 + n] * (s[0] + s[1] if len(s) == 2 else s[0])
                parts.append(v)
    both = halves(parts)
    res = dot(both, smooth[0:256]) + dot(both[:, 0:128], smooth[256:384])
    for c in range(3):
        for g in range(planes // 8):
            for r in range(8):
                n = ((c * planes + g * 8) + r) * 8
                ys[0, pl.ds(g * 64 + r, 8, stride=8), :] = res[n:n + 8]
        for o in range(planes):
            out[c, o] = vel[c, o] + (8.0 * VOLUME / 24.0) * ys[0, pl.ds(o * 8, 8), :]


VM = pl.BlockSpec(memory_space=pltpu.VMEM)
SM = pl.BlockSpec(memory_space=pltpu.SMEM)


def own_part(planes, own):
    nx, nd, nf = planes + 18, planes + 16, planes + 8
    shape = jax.ShapeDtypeStruct
    return pl.pallas_call(
        functools.partial(own_kernel, planes),
        out_shape=(
            shape((12, nd * 8, 128), f32),
            shape((12, nf * 8, 128), f32),
            shape((12, nf * 8, 128), f32),
            shape((3, 12, nf * 8, 128), f32),
        ),
        in_specs=[VM],
        out_specs=(VM,) * 4,
        scratch_shapes=[
            pltpu.VMEM((256, 128), bf16),
            pltpu.VMEM((256, 128), bf16),
            pltpu.VMEM((256, 128), bf16),
            pltpu.VMEM((5, nx * 8, 128), f32),
            pltpu.VMEM((12, (nd + 1) * 8, 128), f32),
            pltpu.VMEM((2 * UNROLL, nf * 8, 128), f32),
        ],
        compiler_params=pltpu.CompilerParams(vmem_limit_bytes=16 * 2**20),
        cost_estimate=pl.CostEstimate(flops=6 * 10**8, bytes_accessed=16 * 2**20, transcendentals=10**6),
        name="own",
    )(own.reshape(-1, 128))


def mate_part(planes, partner, offsets, mates, owned, vel):
    nx, nd, nf = planes + 18, planes + 16, planes + 8
    count = len(mates)
    return pl.pallas_call(
        functools.partial(mate_kernel, planes, count),
        out_shape=jax.ShapeDtypeStruct(vel.shape, f32),
        in_specs=[SM, SM] + [VM] * (count + 5),
        out_specs=VM,
        scratch_shapes=[
            pltpu.VMEM((256, 128), bf16),
            pltpu.VMEM((256, 128), bf16),
            pltpu.VMEM((384, 128), bf16),
            pltpu.VMEM((5, nx * 8, 128), f32),
            pltpu.VMEM((3, nx * 8 + 16, 128), f32),
            pltpu.VMEM((12, (nd + 1) * 8, 128), f32),
            pltpu.VMEM((12, nd * 8, 128), f32),
            pltpu.VMEM((3 * UNROLL, nf * 8, 128), f32),
            pltpu.VMEM((3, nf * 8, 128), f32),
        ],
        compiler_params=pltpu.CompilerParams(vmem_limit_bytes=16 * 2**20),
        name="mate",
    )(partner, offsets.T, *[m.reshape(-1, 128) for m in mates], *owned, vel)


def advect_kernel(planes, image_hbm, vel_hbm, warp, first, second, image, vel, down, up, sems):
    copies = [
        pltpu.make_async_copy(vel_hbm, vel, sems.at[0]),
        pltpu.make_async_copy(image_hbm, image, sems.at[1]),
    ]
    for copy in copies:
        copy.start()
    for copy in copies:
        copy.wait()
    lane = lax.broadcasted_iota(jnp.int32, (8, 128), 1)

    for z in range(planes):
        x = image[0, z].astype(f32)
        before = image[0, z - 1].astype(f32) if z > 0 else x
        after = image[0, z + 1].astype(f32) if z < planes - 1 else x
        sides = (
            (before, after),
            (jnp.where(row_inside(-1), pltpu.roll(x, 1, 0), 0.0), jnp.where(row_inside(1), pltpu.roll(x, 7, 0), 0.0)),
            (jnp.where(lane >= 1, pltpu.roll(x, 1, 1), 0.0), jnp.where(lane < 127, pltpu.roll(x, 127, 1), 0.0)),
        )
        moved = 0.0
        for c, (lo, hi) in enumerate(sides):
            v = vel[0, c, z]
            moved = moved + (jnp.maximum(v, 0.0) * (x - lo) + jnp.minimum(v, 0.0) * (hi - x))
        y = x - moved
        warp[z] = y
        if z == 0 or z == planes - 1:
            v = jnp.maximum(vel[0, 0, z], 0.0) if z == 0 else jnp.minimum(vel[0, 0, z], 0.0)
            edge = split(y) + split(v) + (image[0, z],)
            for n, part in enumerate(edge):
                (down if z == 0 else up)[8 + n] = part
        if 1 <= z <= 8:
            down[z - 1] = y.astype(bf16)
        if planes - 9 <= z < planes - 1:
            up[z - (planes - 9)] = y.astype(bf16)
    even = lax.rem(lax.axis_index("slab"), 2) == 0
    for n in range(EDGE):
        first[n] = jnp.where(even, up[n], down[n])
        second[n] = jnp.where(even, down[n], up[n])


def widen_kernel(planes, warp, sent1, sent2, got1, got2, out):
    low, high = faces()
    even = lax.rem(lax.axis_index("slab"), 2) == 0
    down, up, below, above = (sent2, sent1), (sent1, sent2), (got2, got1), (got1, got2)
    ld = lambda pair, n: jnp.where(even, pair[0][n], pair[1][n]).astype(f32)
    top = planes - 1
    first, last = ld(down, 12), ld(up, 12)
    for n in range(8):
        out[n] = (ld(below, n) * low).astype(bf16)
        out[planes + 10 + n] = (ld(above, n) * high).astype(bf16)
    out[8] = (low * ((ld(below, 8) + ld(below, 9)) - (ld(below, 10) + ld(below, 11)) * (first - ld(below, 12)))).astype(bf16)
    out[planes + 9] = (high * ((ld(above, 8) + ld(above, 9)) - (ld(above, 10) + ld(above, 11)) * (ld(above, 12) - last))).astype(bf16)
    for z in range(1, top):
        out[9 + z] = warp[z].astype(bf16)
    out[9] = (warp[0] - (ld(down, 10) + ld(down, 11)) * (first - ld(below, 12))).astype(bf16)
    out[9 + top] = (warp[top] - (ld(up, 10) + ld(up, 11)) * (ld(above, 12) - last)).astype(bf16)


def shards(intensity, velocity, partner, offsets):
    planes = intensity.shape[1]
    slabs, brains = lax.axis_size("slab"), lax.axis_size("brain")
    edge = jax.ShapeDtypeStruct((EDGE, 8, 128), bf16)
    warp, first, second = pl.pallas_call(
        functools.partial(advect_kernel, planes),
        out_shape=(jax.ShapeDtypeStruct((planes, 8, 128), f32), edge, edge),
        in_specs=[pl.BlockSpec(memory_space=pltpu.HBM)] * 2,
        out_specs=(VM,) * 3,
        scratch_shapes=[
            pltpu.VMEM(intensity.shape, bf16),
            pltpu.VMEM(velocity.shape, f32),
            pltpu.VMEM(edge.shape, bf16),
            pltpu.VMEM(edge.shape, bf16),
            pltpu.SemaphoreType.DMA((2,)),
        ],
        compiler_params=pltpu.CompilerParams(vmem_limit_bytes=8 * 2**20),
        name="advect",
    )(intensity, velocity)
    odd_pairs = [(n, n + 1) for n in range(1, slabs - 1, 2)]
    even_pairs = [(n, n + 1) for n in range(0, slabs - 1, 2)]
    both_ways = lambda pairs: pairs + [(b, a) for a, b in pairs]
    from_odd = lax.ppermute(second, "slab", both_ways(odd_pairs))
    from_even = lax.ppermute(first, "slab", both_ways(even_pairs))
    own = pl.pallas_call(
        functools.partial(widen_kernel, planes),
        out_shape=jax.ShapeDtypeStruct((planes + 18, 8, 128), bf16),
        in_specs=[VM] * 5,
        out_specs=VM,
        compiler_params=pltpu.CompilerParams(vmem_limit_bytes=8 * 2**20),
        name="widen",
    )(warp, first, second, from_even, from_odd)
    if brains == 4:
        mates = [lax.ppermute(own, "brain", [(n, n ^ k) for n in range(4)]) for k in (1, 2, 3)]
    else:
        gathered = lax.all_gather(own, "brain")
        mates = [lax.dynamic_index_in_dim(gathered, partner[lax.axis_index("brain")], 0, keepdims=False)]
    return mate_part(planes, partner, offsets, mates, own_part(planes, own), velocity[0])[None]


def solution(mesh):
    return jax.shard_map(
        shards,
        mesh=mesh,
        in_specs=(
            P(("groups", "brain"), "slab", None, None),
            P(("groups", "brain"), None, "slab", None, None),
            P("groups"),
            P("groups", None),
        ),
        out_specs=P(("groups", "brain"), None, "slab", None, None),
        check_vma=False,
    )
```

```python
import functools
import jax, jax.numpy as jnp, numpy as np
from jax import lax
from jax.experimental import pallas as pl
from jax.experimental.pallas import tpu as pltpu
from jax.sharding import PartitionSpec as P

PAIRS = tuple((i, j) for i in range(6) for j in range(i + 1, 6) if i // 2 != j // 2)
TAPS = tuple(float(v) for v in np.exp(-np.arange(-3, 4) ** 2 / 4.5) / np.exp(-np.arange(-3, 4) ** 2 / 4.5).sum())
f32, bf16 = jnp.float32, jnp.bfloat16
LOG2E = 1.4426950408889634
EDGE = 13
VOLUME = 729.0
UNROLL = 2
FLOOR = 1e-5 * VOLUME * VOLUME


def split(v):
    hi = v.astype(bf16)
    return hi, (v - hi.astype(f32)).astype(bf16)


def lanes():
    return (lax.broadcasted_iota(jnp.int32, (128, 128), 0), lax.broadcasted_iota(jnp.int32, (128, 128), 1))


def ones_where(cond):
    return jnp.where(cond, 1.0, 0.0).astype(bf16)


def halves(parts):
    return jnp.concatenate(split(jnp.concatenate(parts, axis=0)), axis=1)


def dot(a, b):
    return jnp.dot(a, b, preferred_element_type=f32)


def faces():
    slab = lax.axis_index("slab")
    one = jnp.float32(1.0)
    zero = jnp.float32(0.0)
    return jnp.where(slab > 0, one, zero), jnp.where(slab < lax.axis_size("slab") - 1, one, zero)


def row_inside(d):
    row = lax.broadcasted_iota(jnp.int32, (8, 128), 0)
    return (row + d >= 0) & (row + d < 8)


def describe(planes, xs, box3, tb, desc, low, high):
    nd = planes + 16
    ng = nd // 8

    def squares(g, carry, scale=None):
        c1, c2 = carry
        for i in range(8):
            s = g * 8 + i
            ld = lambda n, p: xs[n, pl.ds(pl.multiple_of(p * 8, 8), 8), :]
            near = [ld(0, s + 2), ld(0, s)] + [ld(j, s + 1) for j in (1, 2, 3, 4)]
            n1, n2 = [], []
            done = []
            for k, (a, b) in enumerate(PAIRS):
                d = near[a] - near[b]
                q = d * d
                if scale is not None:
                    q = q * scale
                done.append(c2[k] + q)
                n2.append(c1[k] + q)
                n1.append(q)
            put(s, done)
            c1, c2 = n1, n2
        return c1, c2

    def put(s, done):
        at = pl.ds(s * 8 if isinstance(s, int) else pl.multiple_of(s * 8, 8), 8)
        for k in range(12):
            tb[k, at, :] = done[k]
        while len(done) > 1:
            done = [done[n] + done[n + 1] for n in range(0, len(done) - 1, 2)] + done[len(done) // 2 * 2:]
        tb[12, at, :] = done[0]

    zero = [jnp.zeros((8, 128), f32)] * 12
    carry = squares(0, (zero, zero), low)
    carry = lax.fori_loop(1, ng - 1, squares, carry)
    c1, c2 = squares(ng - 1, carry, high)
    put(nd, c2)

    for g in range(ng):
        parts = []
        for k in (12,) + tuple(range(12)):
            t = [tb[k, pl.ds(g * 64 + 8 + r, 8, stride=8), :] for r in range(8)]
            p = [t[r] + t[r + 1] for r in range(7)]
            parts += [p[0]] + [p[r - 1] + t[r + 1] for r in range(1, 7)] + [p[6]]
        box = dot(halves(parts), box3[...])
        inv = [(-LOG2E / 27.0) / (box[r * 8:r * 8 + 8] * (1.0 / 324.0) + 0.1) for r in range(8)]
        for k in range(12):
            for r in range(8):
                n = (k + 1) * 64 + r * 8
                e = jnp.exp2(box[n:n + 8] * inv[r])
                if g == 0:
                    e = e * low
                if g == ng - 1:
                    e = e * high
                desc[k, pl.ds(g * 64 + r, 8, stride=8), :] = e


def depth_sums(planes, value, ys, q):
    nd, nf = planes + 16, planes + 8
    d = [value(t) for t in range(nd)]
    for f in range(nf):
        if f % 16 == 0:
            s2 = [d[f + t] + d[f + t + 1] for t in (0, 2, 4, 6)]
            total = ((s2[0] + s2[1]) + (s2[2] + s2[3])) + d[f + 8]
        else:
            total = (total - d[f - 1]) + d[f + 8]
        ys[q, pl.ds(f * 8, 8), :] = total


def row_sums(ys, q, g):
    t = [ys[q, pl.ds(g * 64 + r, 8, stride=8), :] for r in range(8)]
    lo = (t[0] + t[1]) + (t[2] + t[3])
    hi = (t[4] + t[5]) + (t[6] + t[7])
    w0 = lo + t[4]
    w1 = w0 + t[5]
    w7 = hi + t[3]
    w6 = w7 + t[2]
    return [w0, w1, w1 + t[6], lo + hi, lo + hi, w6 + t[1], w6, w7]


def own_kernel(planes, own, desc, mean, slope, grads, box3, box9, grad, xs, tb, ys):
    nx, nd, nf = planes + 18, planes + 16, planes + 8
    low, high = faces()
    i, j = lanes()
    for h in (0, 128):
        box3[h:h + 128] = ones_where(jnp.abs(i - j) <= 1)
        box9[h:h + 128] = ones_where(jnp.abs(i - j) <= 4)
        grad[h:h + 128] = jnp.where(i == j + 1, 1.0, jnp.where(i == j - 1, -1.0, 0.0)).astype(bf16)
    x = own[...]
    xs[0] = x.astype(f32)
    xs[3] = dot(x, ones_where(i == j + 1))
    xs[4] = dot(x, ones_where(i == j - 1))

    def prep(p, _):
        at = pl.ds(pl.multiple_of(p * 8, 8), 8)
        v = xs[0, at, :]
        xs[1, at, :] = jnp.where(row_inside(1), pltpu.roll(v, 7, 0), 0.0)
        xs[2, at, :] = jnp.where(row_inside(-1), pltpu.roll(v, 1, 0), 0.0)
        return 0
    lax.fori_loop(0, nx, prep, 0, unroll=6)
    describe(planes, xs, box3, tb, desc, low, high)

    def channels(k, _):
        for h in range(UNROLL):
            one_channel(UNROLL * k + h, h)
        return 0

    def one_channel(k, h):
        ld = lambda t: desc[k, pl.ds(t * 8, 8), :]
        depth_sums(planes, ld, ys, 2 * h)
        depth_sums(planes, lambda t: ld(t) * ld(t), ys, 2 * h + 1)
        parts, centre = [], []
        for g in range(nf // 8):
            for q in range(2):
                parts += row_sums(ys, 2 * h + q, g)
            centre += [desc[k, pl.ds(g * 64 + 32 + r, 8, stride=8), :] for r in range(8)]
        sums = dot(halves(parts), box9[...])
        across = dot(halves(centre), grad[...])
        for g in range(nf // 8):
            a = centre[g * 8:g * 8 + 8]
            for r in range(8):
                at = pl.ds(g * 64 + r * 8, 8)
                mo, so = [sums[(g * 16 + q * 8 + r) * 8:(g * 16 + q * 8 + r) * 8 + 8] for q in range(2)]
                gc = across[(g * 8 + r) * 8:(g * 8 + r) * 8 + 8]
                inv = lax.rsqrt(VOLUME * so - mo * mo + FLOOR)
                gz = desc[k, pl.ds(g * 64 + 40 + r, 8, stride=8), :] - desc[k, pl.ds(g * 64 + 24 + r, 8, stride=8), :]
                gr = a[1] if r == 0 else -a[6] if r == 7 else a[r + 1] - a[r - 1]
                mean[k, at, :] = mo
                slope[k, at, :] = (inv * inv) * (VOLUME * a[r] - mo)
                for c, gg in enumerate((gz, gr, gc)):
                    grads[c, k, at, :] = gg * inv
    lax.fori_loop(0, 12 // UNROLL, channels, 0)


def mate_kernel(planes, count, *refs):
    mates = refs[:count]
    meta, adesc, mean, slope, grads, vel, out, box3, box9, smooth, xs, raw, tb, desc, ys, frc = refs[count:]
    nx, nd, nf = planes + 18, planes + 16, planes + 8
    low, high = faces()
    which, dc = meta[0:1, :], meta[16:17, :]
    dr = jnp.max(meta[8:16, :])
    i, j = lanes()
    weights = jnp.zeros((128, 128), f32)
    for d in range(4):
        weights = jnp.where(jnp.abs(i - j) == d, TAPS[3 + d], weights)
    whi, wlo = split(weights)
    for h in (0, 128):
        box3[h:h + 128] = ones_where(jnp.abs(i - j) <= 1)
        box9[h:h + 128] = ones_where(jnp.abs(i - j) <= 4)
        smooth[h:h + 128] = whi
    smooth[256:384] = wlo
    row = lax.broadcasted_iota(jnp.int32, (8, 128), 0)

    x = mates[0][...]
    for n in range(1, count):
        x = jnp.where(which == n + 1, mates[n][...], x)
    for n, d in ((0, 0), (1, 1), (2, -1)):
        take = ones_where((i == j + d + dc) & (j + d >= 0) & (j + d < 128))
        raw[n, pl.ds(8, nx * 8), :] = dot(x, take)

    def prep(p, _):
        at = pl.multiple_of(p * 8, 8)
        for n, b, d in ((0, 0, 0), (1, 0, 1), (2, 0, -1), (3, 1, 0), (4, 2, 0)):
            v = raw[b, pl.ds(at + 8 + dr + d, 8), :]
            xs[n, pl.ds(at, 8), :] = jnp.where(row_inside(d) & row_inside(d + dr), v, 0.0)
        return 0
    lax.fori_loop(0, nx, prep, 0, unroll=6)
    describe(planes, xs, box3, tb, desc, low, high)

    def channels(step, _):
        ks = [UNROLL * step + h for h in range(UNROLL)]
        sums = []
        for h, k in enumerate(ks):
            lda = lambda t: adesc[k, pl.ds(t * 8, 8), :]
            ldb = lambda t: desc[k, pl.ds(t * 8, 8), :]
            depth_sums(planes, ldb, ys, 3 * h)
            depth_sums(planes, lambda t: ldb(t) * ldb(t), ys, 3 * h + 1)
            depth_sums(planes, lambda t: lda(t) * ldb(t), ys, 3 * h + 2)
            parts = []
            for g in range(nf // 8):
                for q in range(3):
                    parts += row_sums(ys, 3 * h + q, g)
            sums.append(dot(halves(parts), box9[...]))
        for g in range(nf // 8):
            for r in range(8):
                at = pl.ds(g * 64 + r * 8, 8)
                acc = [frc[c, at, :] for c in range(3)]
                for h, k in enumerate(ks):
                    mm, sm, sc = [sums[h][(g * 24 + q * 8 + r) * 8:(g * 24 + q * 8 + r) * 8 + 8] for q in range(3)]
                    b = desc[k, pl.ds(g * 64 + 32 + r, 8, stride=8), :]
                    inv = lax.rsqrt(VOLUME * sm - mm * mm + FLOOR)
                    cov = VOLUME * sc - mean[k, at, :] * mm
                    coef = (VOLUME * b - mm - cov * slope[k, at, :]) * inv
                    acc = [acc[c] + coef * grads[c, k, at, :] for c in range(3)]
                for c in range(3):
                    frc[c, at, :] = acc[c]
        return 0
    frc[...] = jnp.zeros_like(frc)
    lax.fori_loop(0, 12 // UNROLL, channels, 0)

    parts = []
    for c in range(3):
        for g in range(nf // 8):
            for r in range(8):
                v = frc[c, pl.ds(g * 64 + r * 8, 8), :]
                if g == 0:
                    v = jnp.where(row >= 4, v, v * low)
                if g == nf // 8 - 1:
                    v = jnp.where(row < 4, v, v * high)
                ys[0, pl.ds(g * 64 + r, 8, stride=8), :] = v
        for o in range(planes):
            p = [ys[0, pl.ds((o + 1 + n) * 8, 8), :] for n in range(7)]
            v = TAPS[3] * p[3]
            for n in range(3):
                v = v + TAPS[n] * (p[n] + p[6 - n])
            ys[1, pl.ds(o * 8, 8), :] = v
        for g in range(planes // 8):
            t = [ys[1, pl.ds(g * 64 + r, 8, stride=8), :] for r in range(8)]
            for r in range(8):
                v = TAPS[3] * t[r]
                for n in range(1, 4):
                    s = [t[q] for q in (r - n, r + n) if 0 <= q < 8]
                    v = v + TAPS[3 + n] * (s[0] + s[1] if len(s) == 2 else s[0])
                parts.append(v)
    both = halves(parts)
    res = dot(both, smooth[0:256]) + dot(both[:, 0:128], smooth[256:384])
    for c in range(3):
        for g in range(planes // 8):
            for r in range(8):
                n = ((c * planes + g * 8) + r) * 8
                ys[0, pl.ds(g * 64 + r, 8, stride=8), :] = res[n:n + 8]
        for o in range(planes):
            out[c, o] = vel[c, o] + (8.0 * VOLUME / 24.0) * ys[0, pl.ds(o * 8, 8), :]


VM = pl.BlockSpec(memory_space=pltpu.VMEM)
HBM = pl.BlockSpec(memory_space=pltpu.HBM)


def own_part(planes, own):
    nx, nd, nf = planes + 18, planes + 16, planes + 8
    shape = jax.ShapeDtypeStruct
    return pl.pallas_call(
        functools.partial(own_kernel, planes),
        out_shape=(
            shape((12, nd * 8, 128), f32),
            shape((12, nf * 8, 128), f32),
            shape((12, nf * 8, 128), f32),
            shape((3, 12, nf * 8, 128), f32),
        ),
        in_specs=[VM],
        out_specs=(VM,) * 4,
        scratch_shapes=[
            pltpu.VMEM((256, 128), bf16),
            pltpu.VMEM((256, 128), bf16),
            pltpu.VMEM((256, 128), bf16),
            pltpu.VMEM((5, nx * 8, 128), f32),
            pltpu.VMEM((13, (nd + 1) * 8, 128), f32),
            pltpu.VMEM((2 * UNROLL, nf * 8, 128), f32),
        ],
        compiler_params=pltpu.CompilerParams(vmem_limit_bytes=16 * 2**20),
        cost_estimate=pl.CostEstimate(flops=6 * 10**8, bytes_accessed=16 * 2**20, transcendentals=10**6),
        name="own",
    )(own.reshape(-1, 128))


def mate_part(planes, mates, meta, owned, vel):
    nx, nd, nf = planes + 18, planes + 16, planes + 8
    count = len(mates)
    return pl.pallas_call(
        functools.partial(mate_kernel, planes, count),
        out_shape=jax.ShapeDtypeStruct(vel.shape, f32),
        in_specs=[VM] * (count + 6),
        out_specs=VM,
        scratch_shapes=[
            pltpu.VMEM((256, 128), bf16),
            pltpu.VMEM((256, 128), bf16),
            pltpu.VMEM((384, 128), bf16),
            pltpu.VMEM((5, nx * 8, 128), f32),
            pltpu.VMEM((3, nx * 8 + 16, 128), f32),
            pltpu.VMEM((13, (nd + 1) * 8, 128), f32),
            pltpu.VMEM((12, nd * 8, 128), f32),
            pltpu.VMEM((3 * UNROLL, nf * 8, 128), f32),
            pltpu.VMEM((3, nf * 8, 128), f32),
        ],
        compiler_params=pltpu.CompilerParams(vmem_limit_bytes=16 * 2**20),
        name="mate",
    )(*[m.reshape(-1, 128) for m in mates], meta, *owned, vel)


def advect_kernel(planes, image_hbm, vel_hbm, partner_hbm, offsets_hbm, warp, first, second, meta, image, vel, down, up, partner, offsets, sems):
    copies = [
        pltpu.make_async_copy(vel_hbm, vel, sems.at[0]),
        pltpu.make_async_copy(image_hbm, image, sems.at[1]),
        pltpu.make_async_copy(partner_hbm, partner, sems.at[2]),
        pltpu.make_async_copy(offsets_hbm, offsets, sems.at[3]),
    ]
    for copy in copies:
        copy.start()
    for copy in copies:
        copy.wait()
    lane = lax.broadcasted_iota(jnp.int32, (8, 128), 1)

    for z in range(planes):
        x = image[0, z].astype(f32)
        before = image[0, z - 1].astype(f32) if z > 0 else x
        after = image[0, z + 1].astype(f32) if z < planes - 1 else x
        sides = (
            (before, after),
            (jnp.where(row_inside(-1), pltpu.roll(x, 1, 0), 0.0), jnp.where(row_inside(1), pltpu.roll(x, 7, 0), 0.0)),
            (jnp.where(lane >= 1, pltpu.roll(x, 1, 1), 0.0), jnp.where(lane < 127, pltpu.roll(x, 127, 1), 0.0)),
        )
        moved = 0.0
        for c, (lo, hi) in enumerate(sides):
            v = vel[0, c, z]
            moved = moved + (jnp.maximum(v, 0.0) * (x - lo) + jnp.minimum(v, 0.0) * (hi - x))
        y = x - moved
        warp[z] = y
        if z == 0 or z == planes - 1:
            v = jnp.maximum(vel[0, 0, z], 0.0) if z == 0 else jnp.minimum(vel[0, 0, z], 0.0)
            edge = split(y) + split(v) + (image[0, z],)
            for n, part in enumerate(edge):
                (down if z == 0 else up)[8 + n] = part
        if 1 <= z <= 8:
            down[z - 1] = y.astype(bf16)
        if planes - 9 <= z < planes - 1:
            up[z - (planes - 9)] = y.astype(bf16)
    me = lax.axis_index("brain")
    mate = partner[me]
    for n, value in enumerate((me ^ mate, offsets[0, mate] - offsets[0, me], offsets[1, mate] - offsets[1, me])):
        meta[n * 8:n * 8 + 8, :] = jnp.full((8, 128), value, jnp.int32)
    even = lax.rem(lax.axis_index("slab"), 2) == 0
    for n in range(EDGE):
        first[n] = jnp.where(even, up[n], down[n])
        second[n] = jnp.where(even, down[n], up[n])


def widen_kernel(planes, warp, sent1, sent2, got1, got2, out):
    low, high = faces()
    even = lax.rem(lax.axis_index("slab"), 2) == 0
    down, up, below, above = (sent2, sent1), (sent1, sent2), (got2, got1), (got1, got2)
    ld = lambda pair, n: jnp.where(even, pair[0][n], pair[1][n]).astype(f32)
    top = planes - 1
    first, last = ld(down, 12), ld(up, 12)
    for n in range(8):
        out[n] = (ld(below, n) * low).astype(bf16)
        out[planes + 10 + n] = (ld(above, n) * high).astype(bf16)
    out[8] = (low * ((ld(below, 8) + ld(below, 9)) - (ld(below, 10) + ld(below, 11)) * (first - ld(below, 12)))).astype(bf16)
    out[planes + 9] = (high * ((ld(above, 8) + ld(above, 9)) - (ld(above, 10) + ld(above, 11)) * (ld(above, 12) - last))).astype(bf16)
    for z in range(1, top):
        out[9 + z] = warp[z].astype(bf16)
    out[9] = (warp[0] - (ld(down, 10) + ld(down, 11)) * (first - ld(below, 12))).astype(bf16)
    out[9 + top] = (warp[top] - (ld(up, 10) + ld(up, 11)) * (ld(above, 12) - last)).astype(bf16)


def shards(intensity, velocity, partner, offsets):
    planes = intensity.shape[1]
    slabs, brains = lax.axis_size("slab"), lax.axis_size("brain")
    edge = jax.ShapeDtypeStruct((EDGE, 8, 128), bf16)
    warp, first, second, meta = pl.pallas_call(
        functools.partial(advect_kernel, planes),
        out_shape=(jax.ShapeDtypeStruct((planes, 8, 128), f32), edge, edge, jax.ShapeDtypeStruct((24, 128), jnp.int32)),
        in_specs=[HBM] * 4,
        out_specs=(VM,) * 4,
        scratch_shapes=[
            pltpu.VMEM(intensity.shape, bf16),
            pltpu.VMEM(velocity.shape, f32),
            pltpu.VMEM(edge.shape, bf16),
            pltpu.VMEM(edge.shape, bf16),
            pltpu.SMEM(partner.shape, jnp.int32),
            pltpu.SMEM(offsets.shape[::-1], jnp.int32),
            pltpu.SemaphoreType.DMA((4,)),
        ],
        compiler_params=pltpu.CompilerParams(vmem_limit_bytes=8 * 2**20),
        name="advect",
    )(*[pltpu.with_memory_space_constraint(v, pltpu.HBM) for v in (intensity, velocity, partner, offsets.T)])
    odd_pairs = [(n, n + 1) for n in range(1, slabs - 1, 2)]
    even_pairs = [(n, n + 1) for n in range(0, slabs - 1, 2)]
    both_ways = lambda pairs: pairs + [(b, a) for a, b in pairs]
    from_odd = lax.ppermute(second, "slab", both_ways(odd_pairs))
    from_even = lax.ppermute(first, "slab", both_ways(even_pairs))
    own = pl.pallas_call(
        functools.partial(widen_kernel, planes),
        out_shape=jax.ShapeDtypeStruct((planes + 18, 8, 128), bf16),
        in_specs=[VM] * 5,
        out_specs=VM,
        compiler_params=pltpu.CompilerParams(vmem_limit_bytes=8 * 2**20),
        name="widen",
    )(warp, first, second, from_even, from_odd)
    if brains == 4:
        mates = [lax.ppermute(own, "brain", [(n, n ^ k) for n in range(4)]) for k in (1, 2, 3)]
    else:
        gathered = lax.all_gather(own, "brain")
        mates = [lax.dynamic_index_in_dim(gathered, partner[lax.axis_index("brain")], 0, keepdims=False)]
    return mate_part(planes, mates, meta, own_part(planes, own), velocity[0])[None]


def solution(mesh):
    return jax.shard_map(
        shards,
        mesh=mesh,
        in_specs=(
            P(("groups", "brain"), "slab", None, None),
            P(("groups", "brain"), None, "slab", None, None),
            P("groups"),
            P("groups", None),
        ),
        out_specs=P(("groups", "brain"), None, "slab", None, None),
        check_vma=False,
    )
```

```python
import functools
import jax, jax.numpy as jnp, numpy as np
from jax import lax
from jax.experimental import pallas as pl
from jax.experimental.pallas import tpu as pltpu
from jax.sharding import PartitionSpec as P

PAIRS = tuple((i, j) for i in range(6) for j in range(i + 1, 6) if i // 2 != j // 2)
TAPS = tuple(float(v) for v in np.exp(-np.arange(-3, 4) ** 2 / 4.5) / np.exp(-np.arange(-3, 4) ** 2 / 4.5).sum())
f32, bf16 = jnp.float32, jnp.bfloat16
LOG2E = 1.4426950408889634
EDGE = 13
VOLUME = 729.0
UNROLL = 2
PITCH = 9
SPARE = 16
FLOOR = 1e-5 * VOLUME * VOLUME


def split(v):
    hi = v.astype(bf16)
    return hi, (v - hi.astype(f32)).astype(bf16)


def lanes():
    return (lax.broadcasted_iota(jnp.int32, (128, 128), 0), lax.broadcasted_iota(jnp.int32, (128, 128), 1))


def ones_where(cond):
    return jnp.where(cond, 1.0, 0.0).astype(bf16)


def halves(parts):
    return jnp.concatenate(split(jnp.concatenate(parts, axis=0)), axis=1)


def dot(a, b):
    return jnp.dot(a, b, preferred_element_type=f32)


def faces():
    slab = lax.axis_index("slab")
    one = jnp.float32(1.0)
    zero = jnp.float32(0.0)
    return jnp.where(slab > 0, one, zero), jnp.where(slab < lax.axis_size("slab") - 1, one, zero)


def row_inside(d):
    row = lax.broadcasted_iota(jnp.int32, (8, 128), 0)
    return (row + d >= 0) & (row + d < 8)


def describe(planes, xs, box3, tb, desc, low, high):
    nd = planes + 16
    ng = nd // 8

    def squares(g, carry, scale=None):
        c1, c2 = carry
        for i in range(8):
            s = g * 8 + i
            ld = lambda n, p: xs[n, pl.ds(pl.multiple_of(p * 8, 8), 8), :]
            near = [ld(0, s + 2), ld(0, s)] + [ld(j, s + 1) for j in (1, 2, 3, 4)]
            n1, n2 = [], []
            done = []
            for k, (a, b) in enumerate(PAIRS):
                d = near[a] - near[b]
                q = d * d
                if scale is not None:
                    q = q * scale
                done.append(c2[k] + q)
                n2.append(c1[k] + q)
                n1.append(q)
            put(s, done)
            c1, c2 = n1, n2
        return c1, c2

    def put(s, done):
        at = pl.ds(s * PITCH, 8)
        for k in range(12):
            tb[k, at, :] = done[k]
        while len(done) > 1:
            done = [done[n] + done[n + 1] for n in range(0, len(done) - 1, 2)] + done[len(done) // 2 * 2:]
        tb[12, at, :] = done[0]

    zero = [jnp.zeros((8, 128), f32)] * 12
    carry = squares(0, (zero, zero), low)
    carry = lax.fori_loop(1, ng - 1, squares, carry)
    c1, c2 = squares(ng - 1, carry, high)
    put(nd, c2)

    for g in range(ng):
        parts = []
        for k in (12,) + tuple(range(12)):
            t = [tb[k, pl.ds((g * 8 + 1) * PITCH + r, 8, stride=PITCH), :] for r in range(8)]
            p = [t[r] + t[r + 1] for r in range(7)]
            parts += [p[0]] + [p[r - 1] + t[r + 1] for r in range(1, 7)] + [p[6]]
        box = dot(halves(parts), box3[...])
        inv = [(-LOG2E / 27.0) / (box[r * 8:r * 8 + 8] * (1.0 / 324.0) + 0.1) for r in range(8)]
        for k in range(12):
            for r in range(8):
                n = (k + 1) * 64 + r * 8
                e = jnp.exp2(box[n:n + 8] * inv[r])
                if g == 0:
                    e = e * low
                if g == ng - 1:
                    e = e * high
                desc[k, pl.ds(g * 8 * PITCH + r, 8, stride=PITCH), :] = e


def depth_sums(planes, value, ys, q):
    nd, nf = planes + 16, planes + 8
    d = [value(t) for t in range(nd)]
    for f in range(nf):
        if f % 16 == 0:
            s2 = [d[f + t] + d[f + t + 1] for t in (0, 2, 4, 6)]
            total = ((s2[0] + s2[1]) + (s2[2] + s2[3])) + d[f + 8]
        else:
            total = (total - d[f - 1]) + d[f + 8]
        ys[q, pl.ds(f * PITCH, 8), :] = total


def row_sums(ys, q, g):
    t = [ys[q, pl.ds(g * 8 * PITCH + r, 8, stride=PITCH), :] for r in range(8)]
    lo = (t[0] + t[1]) + (t[2] + t[3])
    hi = (t[4] + t[5]) + (t[6] + t[7])
    w0 = lo + t[4]
    w1 = w0 + t[5]
    w7 = hi + t[3]
    w6 = w7 + t[2]
    return [w0, w1, w1 + t[6], lo + hi, lo + hi, w6 + t[1], w6, w7]


def own_kernel(planes, own, desc, mean, slope, grads, box3, box9, grad, xs, tb, ys):
    nx, nd, nf = planes + 18, planes + 16, planes + 8
    low, high = faces()
    i, j = lanes()
    for h in (0, 128):
        box3[h:h + 128] = ones_where(jnp.abs(i - j) <= 1)
        box9[h:h + 128] = ones_where(jnp.abs(i - j) <= 4)
        grad[h:h + 128] = jnp.where(i == j + 1, 1.0, jnp.where(i == j - 1, -1.0, 0.0)).astype(bf16)
    x = own[...]
    xs[0] = x.astype(f32)
    xs[3] = dot(x, ones_where(i == j + 1))
    xs[4] = dot(x, ones_where(i == j - 1))

    def prep(p, _):
        at = pl.ds(pl.multiple_of(p * 8, 8), 8)
        v = xs[0, at, :]
        xs[1, at, :] = jnp.where(row_inside(1), pltpu.roll(v, 7, 0), 0.0)
        xs[2, at, :] = jnp.where(row_inside(-1), pltpu.roll(v, 1, 0), 0.0)
        return 0
    lax.fori_loop(0, nx, prep, 0, unroll=6)
    describe(planes, xs, box3, tb, desc, low, high)

    def channels(k, _):
        for h in range(UNROLL):
            one_channel(UNROLL * k + h, h)
        return 0

    def one_channel(k, h):
        ld = lambda t: desc[k, pl.ds(t * PITCH, 8), :]
        depth_sums(planes, ld, ys, 2 * h)
        depth_sums(planes, lambda t: ld(t) * ld(t), ys, 2 * h + 1)
        parts, centre = [], []
        for g in range(nf // 8):
            for q in range(2):
                parts += row_sums(ys, 2 * h + q, g)
            centre += [desc[k, pl.ds((g * 8 + 4) * PITCH + r, 8, stride=PITCH), :] for r in range(8)]
        sums = dot(halves(parts), box9[...])
        across = dot(halves(centre), grad[...])
        for g in range(nf // 8):
            a = centre[g * 8:g * 8 + 8]
            for r in range(8):
                at = pl.ds(g * 64 + r * 8, 8)
                mo, so = [sums[(g * 16 + q * 8 + r) * 8:(g * 16 + q * 8 + r) * 8 + 8] for q in range(2)]
                gc = across[(g * 8 + r) * 8:(g * 8 + r) * 8 + 8]
                inv = lax.rsqrt(VOLUME * so - mo * mo + FLOOR)
                gz = desc[k, pl.ds((g * 8 + 5) * PITCH + r, 8, stride=PITCH), :] - desc[k, pl.ds((g * 8 + 3) * PITCH + r, 8, stride=PITCH), :]
                gr = a[1] if r == 0 else -a[6] if r == 7 else a[r + 1] - a[r - 1]
                mean[k, at, :] = mo
                slope[k, at, :] = (inv * inv) * (VOLUME * a[r] - mo)
                for c, gg in enumerate((gz, gr, gc)):
                    grads[c, k, at, :] = gg * inv
    lax.fori_loop(0, 12 // UNROLL, channels, 0)


def mate_kernel(planes, count, *refs):
    mates = refs[:count]
    meta, adesc, mean, slope, grads, vel, out, box3, box9, smooth, xs, raw, tb, desc, ys, frc = refs[count:]
    nx, nd, nf = planes + 18, planes + 16, planes + 8
    low, high = faces()
    which, dc = meta[0:1, :], meta[16:17, :]
    dr = jnp.max(meta[8:16, :])
    i, j = lanes()
    weights = jnp.zeros((128, 128), f32)
    for d in range(4):
        weights = jnp.where(jnp.abs(i - j) == d, TAPS[3 + d], weights)
    whi, wlo = split(weights)
    for h in (0, 128):
        box3[h:h + 128] = ones_where(jnp.abs(i - j) <= 1)
        box9[h:h + 128] = ones_where(jnp.abs(i - j) <= 4)
        smooth[h:h + 128] = whi
    smooth[256:384] = wlo
    row = lax.broadcasted_iota(jnp.int32, (8, 128), 0)

    x = mates[0][...]
    for n in range(1, count):
        x = jnp.where(which == n + 1, mates[n][...], x)
    for n, d in ((0, 0), (1, 1), (2, -1)):
        take = ones_where((i == j + d + dc) & (j + d >= 0) & (j + d < 128))
        raw[n, pl.ds(8, nx * 8), :] = dot(x, take)

    def prep(p, _):
        at = pl.multiple_of(p * 8, 8)
        for n, b, d in ((0, 0, 0), (1, 0, 1), (2, 0, -1), (3, 1, 0), (4, 2, 0)):
            v = raw[b, pl.ds(at + 8 + dr + d, 8), :]
            xs[n, pl.ds(at, 8), :] = jnp.where(row_inside(d) & row_inside(d + dr), v, 0.0)
        return 0
    lax.fori_loop(0, nx, prep, 0, unroll=6)
    describe(planes, xs, box3, tb, desc, low, high)

    def channels(step, _):
        ks = [UNROLL * step + h for h in range(UNROLL)]
        sums = []
        for h, k in enumerate(ks):
            lda = lambda t: adesc[k, pl.ds(t * PITCH, 8), :]
            ldb = lambda t: desc[k, pl.ds(t * PITCH, 8), :]
            depth_sums(planes, ldb, ys, 3 * h)
            depth_sums(planes, lambda t: ldb(t) * ldb(t), ys, 3 * h + 1)
            depth_sums(planes, lambda t: lda(t) * ldb(t), ys, 3 * h + 2)
            parts = []
            for g in range(nf // 8):
                for q in range(3):
                    parts += row_sums(ys, 3 * h + q, g)
            sums.append(dot(halves(parts), box9[...]))
        for g in range(nf // 8):
            for r in range(8):
                at = pl.ds(g * 64 + r * 8, 8)
                acc = [frc[c, at, :] for c in range(3)]
                for h, k in enumerate(ks):
                    mm, sm, sc = [sums[h][(g * 24 + q * 8 + r) * 8:(g * 24 + q * 8 + r) * 8 + 8] for q in range(3)]
                    b = desc[k, pl.ds((g * 8 + 4) * PITCH + r, 8, stride=PITCH), :]
                    inv = lax.rsqrt(VOLUME * sm - mm * mm + FLOOR)
                    cov = VOLUME * sc - mean[k, at, :] * mm
                    coef = (VOLUME * b - mm - cov * slope[k, at, :]) * inv
                    acc = [acc[c] + coef * grads[c, k, at, :] for c in range(3)]
                for c in range(3):
                    frc[c, at, :] = acc[c]
        return 0
    frc[...] = jnp.zeros_like(frc)
    lax.fori_loop(0, 12 // UNROLL, channels, 0)

    parts = []
    for c in range(3):
        for g in range(nf // 8):
            for r in range(8):
                v = frc[c, pl.ds(g * 64 + r * 8, 8), :]
                if g == 0:
                    v = jnp.where(row >= 4, v, v * low)
                if g == nf // 8 - 1:
                    v = jnp.where(row < 4, v, v * high)
                ys[0, pl.ds(g * 8 * PITCH + r, 8, stride=PITCH), :] = v
        for o in range(planes):
            p = [ys[0, pl.ds((o + 1 + n) * PITCH, 8), :] for n in range(7)]
            v = TAPS[3] * p[3]
            for n in range(3):
                v = v + TAPS[n] * (p[n] + p[6 - n])
            ys[1, pl.ds(o * PITCH, 8), :] = v
        for g in range(planes // 8):
            t = [ys[1, pl.ds(g * 8 * PITCH + r, 8, stride=PITCH), :] for r in range(8)]
            for r in range(8):
                v = TAPS[3] * t[r]
                for n in range(1, 4):
                    s = [t[q] for q in (r - n, r + n) if 0 <= q < 8]
                    v = v + TAPS[3 + n] * (s[0] + s[1] if len(s) == 2 else s[0])
                parts.append(v)
    both = halves(parts)
    res = dot(both, smooth[0:256]) + dot(both[:, 0:128], smooth[256:384])
    for c in range(3):
        for g in range(planes // 8):
            for r in range(8):
                n = ((c * planes + g * 8) + r) * 8
                ys[0, pl.ds(g * 8 * PITCH + r, 8, stride=PITCH), :] = res[n:n + 8]
        for o in range(planes):
            out[c, o] = vel[c, o] + (8.0 * VOLUME / 24.0) * ys[0, pl.ds(o * PITCH, 8), :]


VM = pl.BlockSpec(memory_space=pltpu.VMEM)
HBM = pl.BlockSpec(memory_space=pltpu.HBM)


def own_part(planes, own):
    nx, nd, nf = planes + 18, planes + 16, planes + 8
    shape = jax.ShapeDtypeStruct
    return pl.pallas_call(
        functools.partial(own_kernel, planes),
        out_shape=(
            shape((12, nd * PITCH + SPARE, 128), f32),
            shape((12, nf * 8, 128), f32),
            shape((12, nf * 8, 128), f32),
            shape((3, 12, nf * 8, 128), f32),
        ),
        in_specs=[VM],
        out_specs=(VM,) * 4,
        scratch_shapes=[
            pltpu.VMEM((256, 128), bf16),
            pltpu.VMEM((256, 128), bf16),
            pltpu.VMEM((256, 128), bf16),
            pltpu.VMEM((5, nx * 8, 128), f32),
            pltpu.VMEM((13, (nd + 1) * PITCH + SPARE, 128), f32),
            pltpu.VMEM((2 * UNROLL, nf * PITCH + SPARE, 128), f32),
        ],
        compiler_params=pltpu.CompilerParams(vmem_limit_bytes=16 * 2**20),
        cost_estimate=pl.CostEstimate(flops=6 * 10**8, bytes_accessed=16 * 2**20, transcendentals=10**6),
        name="own",
    )(own.reshape(-1, 128))


def mate_part(planes, mates, meta, owned, vel):
    nx, nd, nf = planes + 18, planes + 16, planes + 8
    count = len(mates)
    return pl.pallas_call(
        functools.partial(mate_kernel, planes, count),
        out_shape=jax.ShapeDtypeStruct(vel.shape, f32),
        in_specs=[VM] * (count + 6),
        out_specs=VM,
        scratch_shapes=[
            pltpu.VMEM((256, 128), bf16),
            pltpu.VMEM((256, 128), bf16),
            pltpu.VMEM((384, 128), bf16),
            pltpu.VMEM((5, nx * 8, 128), f32),
            pltpu.VMEM((3, nx * 8 + 16, 128), f32),
            pltpu.VMEM((13, (nd + 1) * PITCH + SPARE, 128), f32),
            pltpu.VMEM((12, nd * PITCH + SPARE, 128), f32),
            pltpu.VMEM((3 * UNROLL, nf * PITCH + SPARE, 128), f32),
            pltpu.VMEM((3, nf * 8, 128), f32),
        ],
        compiler_params=pltpu.CompilerParams(vmem_limit_bytes=16 * 2**20),
        name="mate",
    )(*[m.reshape(-1, 128) for m in mates], meta, *owned, vel)


def advect_kernel(planes, image_hbm, vel_hbm, partner_hbm, offsets_hbm, warp, first, second, meta, image, vel, down, up, partner, offsets, sems):
    copies = [
        pltpu.make_async_copy(vel_hbm, vel, sems.at[0]),
        pltpu.make_async_copy(image_hbm, image, sems.at[1]),
        pltpu.make_async_copy(partner_hbm, partner, sems.at[2]),
        pltpu.make_async_copy(offsets_hbm, offsets, sems.at[3]),
    ]
    for copy in copies:
        copy.start()
    for copy in copies:
        copy.wait()
    lane = lax.broadcasted_iota(jnp.int32, (8, 128), 1)

    for z in range(planes):
        x = image[0, z].astype(f32)
        before = image[0, z - 1].astype(f32) if z > 0 else x
        after = image[0, z + 1].astype(f32) if z < planes - 1 else x
        sides = (
            (before, after),
            (jnp.where(row_inside(-1), pltpu.roll(x, 1, 0), 0.0), jnp.where(row_inside(1), pltpu.roll(x, 7, 0), 0.0)),
            (jnp.where(lane >= 1, pltpu.roll(x, 1, 1), 0.0), jnp.where(lane < 127, pltpu.roll(x, 127, 1), 0.0)),
        )
        moved = 0.0
        for c, (lo, hi) in enumerate(sides):
            v = vel[0, c, z]
            moved = moved + (jnp.maximum(v, 0.0) * (x - lo) + jnp.minimum(v, 0.0) * (hi - x))
        y = x - moved
        warp[z] = y
        if z == 0 or z == planes - 1:
            v = jnp.maximum(vel[0, 0, z], 0.0) if z == 0 else jnp.minimum(vel[0, 0, z], 0.0)
            edge = split(y) + split(v) + (image[0, z],)
            for n, part in enumerate(edge):
                (down if z == 0 else up)[8 + n] = part
        if 1 <= z <= 8:
            down[z - 1] = y.astype(bf16)
        if planes - 9 <= z < planes - 1:
            up[z - (planes - 9)] = y.astype(bf16)
    me = lax.axis_index("brain")
    mate = partner[me]
    for n, value in enumerate((me ^ mate, offsets[0, mate] - offsets[0, me], offsets[1, mate] - offsets[1, me])):
        meta[n * 8:n * 8 + 8, :] = jnp.full((8, 128), value, jnp.int32)
    even = lax.rem(lax.axis_index("slab"), 2) == 0
    for n in range(EDGE):
        first[n] = jnp.where(even, up[n], down[n])
        second[n] = jnp.where(even, down[n], up[n])


def widen_kernel(planes, warp, sent1, sent2, got1, got2, out):
    low, high = faces()
    even = lax.rem(lax.axis_index("slab"), 2) == 0
    down, up, below, above = (sent2, sent1), (sent1, sent2), (got2, got1), (got1, got2)
    ld = lambda pair, n: jnp.where(even, pair[0][n], pair[1][n]).astype(f32)
    top = planes - 1
    first, last = ld(down, 12), ld(up, 12)
    for n in range(8):
        out[n] = (ld(below, n) * low).astype(bf16)
        out[planes + 10 + n] = (ld(above, n) * high).astype(bf16)
    out[8] = (low * ((ld(below, 8) + ld(below, 9)) - (ld(below, 10) + ld(below, 11)) * (first - ld(below, 12)))).astype(bf16)
    out[planes + 9] = (high * ((ld(above, 8) + ld(above, 9)) - (ld(above, 10) + ld(above, 11)) * (ld(above, 12) - last))).astype(bf16)
    for z in range(1, top):
        out[9 + z] = warp[z].astype(bf16)
    out[9] = (warp[0] - (ld(down, 10) + ld(down, 11)) * (first - ld(below, 12))).astype(bf16)
    out[9 + top] = (warp[top] - (ld(up, 10) + ld(up, 11)) * (ld(above, 12) - last)).astype(bf16)


def shards(intensity, velocity, partner, offsets):
    planes = intensity.shape[1]
    slabs, brains = lax.axis_size("slab"), lax.axis_size("brain")
    edge = jax.ShapeDtypeStruct((EDGE, 8, 128), bf16)
    warp, first, second, meta = pl.pallas_call(
        functools.partial(advect_kernel, planes),
        out_shape=(jax.ShapeDtypeStruct((planes, 8, 128), f32), edge, edge, jax.ShapeDtypeStruct((24, 128), jnp.int32)),
        in_specs=[HBM] * 4,
        out_specs=(VM,) * 4,
        scratch_shapes=[
            pltpu.VMEM(intensity.shape, bf16),
            pltpu.VMEM(velocity.shape, f32),
            pltpu.VMEM(edge.shape, bf16),
            pltpu.VMEM(edge.shape, bf16),
            pltpu.SMEM(partner.shape, jnp.int32),
            pltpu.SMEM(offsets.shape[::-1], jnp.int32),
            pltpu.SemaphoreType.DMA((4,)),
        ],
        compiler_params=pltpu.CompilerParams(vmem_limit_bytes=8 * 2**20),
        name="advect",
    )(*[pltpu.with_memory_space_constraint(v, pltpu.HBM) for v in (intensity, velocity, partner, offsets.T)])
    odd_pairs = [(n, n + 1) for n in range(1, slabs - 1, 2)]
    even_pairs = [(n, n + 1) for n in range(0, slabs - 1, 2)]
    both_ways = lambda pairs: pairs + [(b, a) for a, b in pairs]
    from_odd = lax.ppermute(second, "slab", both_ways(odd_pairs))
    from_even = lax.ppermute(first, "slab", both_ways(even_pairs))
    own = pl.pallas_call(
        functools.partial(widen_kernel, planes),
        out_shape=jax.ShapeDtypeStruct((planes + 18, 8, 128), bf16),
        in_specs=[VM] * 5,
        out_specs=VM,
        compiler_params=pltpu.CompilerParams(vmem_limit_bytes=8 * 2**20),
        name="widen",
    )(warp, first, second, from_even, from_odd)
    if brains == 4:
        mates = [lax.ppermute(own, "brain", [(n, n ^ k) for n in range(4)]) for k in (1, 2, 3)]
    else:
        gathered = lax.all_gather(own, "brain")
        mates = [lax.dynamic_index_in_dim(gathered, partner[lax.axis_index("brain")], 0, keepdims=False)]
    return mate_part(planes, mates, meta, own_part(planes, own), velocity[0])[None]


def solution(mesh):
    return jax.shard_map(
        shards,
        mesh=mesh,
        in_specs=(
            P(("groups", "brain"), "slab", None, None),
            P(("groups", "brain"), None, "slab", None, None),
            P("groups"),
            P("groups", None),
        ),
        out_specs=P(("groups", "brain"), None, "slab", None, None),
        check_vma=False,
    )
```

```python
import functools
import jax, jax.numpy as jnp, numpy as np
from jax import lax
from jax.experimental import pallas as pl
from jax.experimental.pallas import tpu as pltpu
from jax.sharding import PartitionSpec as P

PAIRS = tuple((i, j) for i in range(6) for j in range(i + 1, 6) if i // 2 != j // 2)
TAPS = tuple(float(v) for v in np.exp(-np.arange(-3, 4) ** 2 / 4.5) / np.exp(-np.arange(-3, 4) ** 2 / 4.5).sum())
f32, bf16 = jnp.float32, jnp.bfloat16
LOG2E = 1.4426950408889634
EDGE = 13
VOLUME = 729.0
UNROLL = 2
PITCH = 9
SPARE = 16
FLOOR = 1e-5 * VOLUME * VOLUME


def split(v):
    hi = v.astype(bf16)
    return hi, (v - hi.astype(f32)).astype(bf16)


def lanes():
    return (lax.broadcasted_iota(jnp.int32, (128, 128), 0), lax.broadcasted_iota(jnp.int32, (128, 128), 1))


def ones_where(cond):
    return jnp.where(cond, 1.0, 0.0).astype(bf16)


def halves(parts):
    return jnp.concatenate(split(jnp.concatenate(parts, axis=0)), axis=1)


def dot(a, b):
    return jnp.dot(a, b, preferred_element_type=f32)


def faces():
    slab = lax.axis_index("slab")
    one = jnp.float32(1.0)
    zero = jnp.float32(0.0)
    return jnp.where(slab > 0, one, zero), jnp.where(slab < lax.axis_size("slab") - 1, one, zero)


def row_inside(d):
    row = lax.broadcasted_iota(jnp.int32, (8, 128), 0)
    return (row + d >= 0) & (row + d < 8)


def describe(planes, xs, box3, tb, desc, low, high):
    nd = planes + 16
    ng = nd // 8

    def squares(g, carry, scale=None):
        c1, c2 = carry
        for i in range(8):
            s = g * 8 + i
            ld = lambda n, p: xs[n, pl.ds(pl.multiple_of(p * 8, 8), 8), :]
            near = [ld(0, s + 2), ld(0, s)] + [ld(j, s + 1) for j in (1, 2, 3, 4)]
            n1, n2 = [], []
            done = []
            for k, (a, b) in enumerate(PAIRS):
                d = near[a] - near[b]
                q = d * d
                if scale is not None:
                    q = q * scale
                done.append(c2[k] + q)
                n2.append(c1[k] + q)
                n1.append(q)
            put(s, done)
            c1, c2 = n1, n2
        return c1, c2

    def put(s, done):
        at = pl.ds(s * PITCH, 8)
        for k in range(12):
            tb[k, at, :] = done[k]
        while len(done) > 1:
            done = [done[n] + done[n + 1] for n in range(0, len(done) - 1, 2)] + done[len(done) // 2 * 2:]
        tb[12, at, :] = done[0]

    zero = [jnp.zeros((8, 128), f32)] * 12
    carry = squares(0, (zero, zero), low)
    carry = lax.fori_loop(1, ng - 1, squares, carry)
    c1, c2 = squares(ng - 1, carry, high)
    put(nd, c2)

    for g in range(ng):
        parts = []
        for k in (12,) + tuple(range(12)):
            t = [tb[k, pl.ds((g * 8 + 1) * PITCH + r, 8, stride=PITCH), :] for r in range(8)]
            p = [t[r] + t[r + 1] for r in range(7)]
            parts += [p[0]] + [p[r - 1] + t[r + 1] for r in range(1, 7)] + [p[6]]
        box = dot(halves(parts), box3[...])
        inv = [(-LOG2E / 27.0) / (box[r * 8:r * 8 + 8] * (1.0 / 324.0) + 0.1) for r in range(8)]
        for k in range(12):
            for r in range(8):
                n = (k + 1) * 64 + r * 8
                e = jnp.exp2(box[n:n + 8] * inv[r])
                if g == 0:
                    e = e * low
                if g == ng - 1:
                    e = e * high
                desc[k, pl.ds(g * 8 * PITCH + r, 8, stride=PITCH), :] = e


def depth_sums(planes, value, ys, q):
    nd, nf = planes + 16, planes + 8
    d = [value(t) for t in range(nd)]
    for f in range(nf):
        if f % 16 == 0:
            s2 = [d[f + t] + d[f + t + 1] for t in (0, 2, 4, 6)]
            total = ((s2[0] + s2[1]) + (s2[2] + s2[3])) + d[f + 8]
        else:
            total = (total - d[f - 1]) + d[f + 8]
        ys[q, pl.ds(f * PITCH, 8), :] = total


def row_sums(ys, q, g):
    t = [ys[q, pl.ds(g * 8 * PITCH + r, 8, stride=PITCH), :] for r in range(8)]
    lo = (t[0] + t[1]) + (t[2] + t[3])
    hi = (t[4] + t[5]) + (t[6] + t[7])
    w0 = lo + t[4]
    w1 = w0 + t[5]
    w7 = hi + t[3]
    w6 = w7 + t[2]
    return [w0, w1, w1 + t[6], lo + hi, lo + hi, w6 + t[1], w6, w7]


def own_kernel(planes, own, desc, mean, slope, grads, box3, box9, grad, xs, tb, ys):
    nx, nd, nf = planes + 18, planes + 16, planes + 8
    low, high = faces()
    i, j = lanes()
    for h in (0, 128):
        box3[h:h + 128] = ones_where(jnp.abs(i - j) <= 1)
        box9[h:h + 128] = ones_where(jnp.abs(i - j) <= 4)
        grad[h:h + 128] = jnp.where(i == j + 1, 1.0, jnp.where(i == j - 1, -1.0, 0.0)).astype(bf16)
    x = own[...]
    xs[0] = x.astype(f32)
    xs[3] = dot(x, ones_where(i == j + 1))
    xs[4] = dot(x, ones_where(i == j - 1))

    def prep(p, _):
        at = pl.ds(pl.multiple_of(p * 8, 8), 8)
        v = xs[0, at, :]
        xs[1, at, :] = jnp.where(row_inside(1), pltpu.roll(v, 7, 0), 0.0)
        xs[2, at, :] = jnp.where(row_inside(-1), pltpu.roll(v, 1, 0), 0.0)
        return 0
    lax.fori_loop(0, nx, prep, 0, unroll=6)
    describe(planes, xs, box3, tb, desc, low, high)

    def channels(k, _):
        for h in range(UNROLL):
            one_channel(UNROLL * k + h, h)
        return 0

    def one_channel(k, h):
        ld = lambda t: desc[k, pl.ds(t * PITCH, 8), :]
        depth_sums(planes, ld, ys, 2 * h)
        depth_sums(planes, lambda t: ld(t) * ld(t), ys, 2 * h + 1)
        parts, centre = [], []
        for g in range(nf // 8):
            for q in range(2):
                parts += row_sums(ys, 2 * h + q, g)
            centre += [desc[k, pl.ds((g * 8 + 4) * PITCH + r, 8, stride=PITCH), :] for r in range(8)]
        sums = dot(halves(parts), box9[...])
        across = dot(halves(centre), grad[...])
        for g in range(nf // 8):
            a = centre[g * 8:g * 8 + 8]
            for r in range(8):
                at = pl.ds(g * 64 + r * 8, 8)
                mo, so = [sums[(g * 16 + q * 8 + r) * 8:(g * 16 + q * 8 + r) * 8 + 8] for q in range(2)]
                gc = across[(g * 8 + r) * 8:(g * 8 + r) * 8 + 8]
                inv = lax.rsqrt(VOLUME * so - mo * mo + FLOOR)
                gz = desc[k, pl.ds((g * 8 + 5) * PITCH + r, 8, stride=PITCH), :] - desc[k, pl.ds((g * 8 + 3) * PITCH + r, 8, stride=PITCH), :]
                gr = a[1] if r == 0 else -a[6] if r == 7 else a[r + 1] - a[r - 1]
                mean[k, at, :] = mo
                slope[k, at, :] = (inv * inv) * (VOLUME * a[r] - mo)
                for c, gg in enumerate((gz, gr, gc)):
                    grads[c, k, at, :] = gg * inv
    lax.fori_loop(0, 12 // UNROLL, channels, 0)


def mate_kernel(planes, count, *refs):
    inner, outer = refs[:count], refs[count:2 * count]
    meta, adesc, mean, slope, grads, vel, out, box3, box9, smooth, xs, raw, tb, desc, ys, frc = refs[2 * count:]
    nx, nd, nf = planes + 18, planes + 16, planes + 8
    low, high = faces()
    which, dc = meta[0:1, :], meta[16:17, :]
    dr = jnp.max(meta[8:16, :])
    i, j = lanes()
    weights = jnp.zeros((128, 128), f32)
    for d in range(4):
        weights = jnp.where(jnp.abs(i - j) == d, TAPS[3 + d], weights)
    whi, wlo = split(weights)
    for h in (0, 128):
        box3[h:h + 128] = ones_where(jnp.abs(i - j) <= 1)
        box9[h:h + 128] = ones_where(jnp.abs(i - j) <= 4)
        smooth[h:h + 128] = whi
    smooth[256:384] = wlo
    row = lax.broadcasted_iota(jnp.int32, (8, 128), 0)

    x, y = inner[0][...], outer[0][...]
    for n in range(1, count):
        x = jnp.where(which == n + 1, inner[n][...], x)
        y = jnp.where(which == n + 1, outer[n][...], y)
    x = jnp.concatenate([y[0:80], x, y[80:160]], axis=0)
    for n, d in ((0, 0), (1, 1), (2, -1)):
        take = ones_where((i == j + d + dc) & (j + d >= 0) & (j + d < 128))
        raw[n, pl.ds(8, nx * 8), :] = dot(x, take)

    def prep(p, _):
        at = pl.multiple_of(p * 8, 8)
        for n, b, d in ((0, 0, 0), (1, 0, 1), (2, 0, -1), (3, 1, 0), (4, 2, 0)):
            v = raw[b, pl.ds(at + 8 + dr + d, 8), :]
            xs[n, pl.ds(at, 8), :] = jnp.where(row_inside(d) & row_inside(d + dr), v, 0.0)
        return 0
    lax.fori_loop(0, nx, prep, 0, unroll=6)
    describe(planes, xs, box3, tb, desc, low, high)

    def channels(step, _):
        ks = [UNROLL * step + h for h in range(UNROLL)]
        sums = []
        for h, k in enumerate(ks):
            lda = lambda t: adesc[k, pl.ds(t * PITCH, 8), :]
            ldb = lambda t: desc[k, pl.ds(t * PITCH, 8), :]
            depth_sums(planes, ldb, ys, 3 * h)
            depth_sums(planes, lambda t: ldb(t) * ldb(t), ys, 3 * h + 1)
            depth_sums(planes, lambda t: lda(t) * ldb(t), ys, 3 * h + 2)
            parts = []
            for g in range(nf // 8):
                for q in range(3):
                    parts += row_sums(ys, 3 * h + q, g)
            sums.append(dot(halves(parts), box9[...]))
        for g in range(nf // 8):
            for r in range(8):
                at = pl.ds(g * 64 + r * 8, 8)
                acc = [frc[c, at, :] for c in range(3)]
                for h, k in enumerate(ks):
                    mm, sm, sc = [sums[h][(g * 24 + q * 8 + r) * 8:(g * 24 + q * 8 + r) * 8 + 8] for q in range(3)]
                    b = desc[k, pl.ds((g * 8 + 4) * PITCH + r, 8, stride=PITCH), :]
                    inv = lax.rsqrt(VOLUME * sm - mm * mm + FLOOR)
                    cov = VOLUME * sc - mean[k, at, :] * mm
                    coef = (VOLUME * b - mm - cov * slope[k, at, :]) * inv
                    acc = [acc[c] + coef * grads[c, k, at, :] for c in range(3)]
                for c in range(3):
                    frc[c, at, :] = acc[c]
        return 0
    frc[...] = jnp.zeros_like(frc)
    lax.fori_loop(0, 12 // UNROLL, channels, 0)

    parts = []
    for c in range(3):
        for g in range(nf // 8):
            for r in range(8):
                v = frc[c, pl.ds(g * 64 + r * 8, 8), :]
                if g == 0:
                    v = jnp.where(row >= 4, v, v * low)
                if g == nf // 8 - 1:
                    v = jnp.where(row < 4, v, v * high)
                ys[0, pl.ds(g * 8 * PITCH + r, 8, stride=PITCH), :] = v
        for o in range(planes):
            p = [ys[0, pl.ds((o + 1 + n) * PITCH, 8), :] for n in range(7)]
            v = TAPS[3] * p[3]
            for n in range(3):
                v = v + TAPS[n] * (p[n] + p[6 - n])
            ys[1, pl.ds(o * PITCH, 8), :] = v
        for g in range(planes // 8):
            t = [ys[1, pl.ds(g * 8 * PITCH + r, 8, stride=PITCH), :] for r in range(8)]
            for r in range(8):
                v = TAPS[3] * t[r]
                for n in range(1, 4):
                    s = [t[q] for q in (r - n, r + n) if 0 <= q < 8]
                    v = v + TAPS[3 + n] * (s[0] + s[1] if len(s) == 2 else s[0])
                parts.append(v)
    both = halves(parts)
    res = dot(both, smooth[0:256]) + dot(both[:, 0:128], smooth[256:384])
    for c in range(3):
        for g in range(planes // 8):
            for r in range(8):
                n = ((c * planes + g * 8) + r) * 8
                ys[0, pl.ds(g * 8 * PITCH + r, 8, stride=PITCH), :] = res[n:n + 8]
        for o in range(planes):
            out[c, o] = vel[c, o] + (8.0 * VOLUME / 24.0) * ys[0, pl.ds(o * PITCH, 8), :]


VM = pl.BlockSpec(memory_space=pltpu.VMEM)
HBM = pl.BlockSpec(memory_space=pltpu.HBM)


def own_part(planes, own):
    nx, nd, nf = planes + 18, planes + 16, planes + 8
    shape = jax.ShapeDtypeStruct
    return pl.pallas_call(
        functools.partial(own_kernel, planes),
        out_shape=(
            shape((12, nd * PITCH + SPARE, 128), f32),
            shape((12, nf * 8, 128), f32),
            shape((12, nf * 8, 128), f32),
            shape((3, 12, nf * 8, 128), f32),
        ),
        in_specs=[VM],
        out_specs=(VM,) * 4,
        scratch_shapes=[
            pltpu.VMEM((256, 128), bf16),
            pltpu.VMEM((256, 128), bf16),
            pltpu.VMEM((256, 128), bf16),
            pltpu.VMEM((5, nx * 8, 128), f32),
            pltpu.VMEM((13, (nd + 1) * PITCH + SPARE, 128), f32),
            pltpu.VMEM((2 * UNROLL, nf * PITCH + SPARE, 128), f32),
        ],
        compiler_params=pltpu.CompilerParams(vmem_limit_bytes=16 * 2**20),
        cost_estimate=pl.CostEstimate(flops=6 * 10**8, bytes_accessed=16 * 2**20, transcendentals=10**6),
        name="own",
    )(own.reshape(-1, 128))


def mate_part(planes, inner, outer, meta, owned, vel):
    nx, nd, nf = planes + 18, planes + 16, planes + 8
    count = len(inner)
    return pl.pallas_call(
        functools.partial(mate_kernel, planes, count),
        out_shape=jax.ShapeDtypeStruct(vel.shape, f32),
        in_specs=[VM] * (2 * count + 6),
        out_specs=VM,
        scratch_shapes=[
            pltpu.VMEM((256, 128), bf16),
            pltpu.VMEM((256, 128), bf16),
            pltpu.VMEM((384, 128), bf16),
            pltpu.VMEM((5, nx * 8, 128), f32),
            pltpu.VMEM((3, nx * 8 + 16, 128), f32),
            pltpu.VMEM((13, (nd + 1) * PITCH + SPARE, 128), f32),
            pltpu.VMEM((12, nd * PITCH + SPARE, 128), f32),
            pltpu.VMEM((3 * UNROLL, nf * PITCH + SPARE, 128), f32),
            pltpu.VMEM((3, nf * 8, 128), f32),
        ],
        compiler_params=pltpu.CompilerParams(vmem_limit_bytes=16 * 2**20),
        name="mate",
    )(*[m.reshape(-1, 128) for m in inner + outer], meta, *owned, vel)


def advect_kernel(planes, image_hbm, vel_hbm, partner_hbm, offsets_hbm, warp, inner, first, second, meta, image, vel, down, up, partner, offsets, sems):
    copies = [
        pltpu.make_async_copy(vel_hbm, vel, sems.at[0]),
        pltpu.make_async_copy(image_hbm, image, sems.at[1]),
        pltpu.make_async_copy(partner_hbm, partner, sems.at[2]),
        pltpu.make_async_copy(offsets_hbm, offsets, sems.at[3]),
    ]
    for copy in copies:
        copy.start()
    for copy in copies:
        copy.wait()
    lane = lax.broadcasted_iota(jnp.int32, (8, 128), 1)

    for z in range(planes):
        x = image[0, z].astype(f32)
        before = image[0, z - 1].astype(f32) if z > 0 else x
        after = image[0, z + 1].astype(f32) if z < planes - 1 else x
        sides = (
            (before, after),
            (jnp.where(row_inside(-1), pltpu.roll(x, 1, 0), 0.0), jnp.where(row_inside(1), pltpu.roll(x, 7, 0), 0.0)),
            (jnp.where(lane >= 1, pltpu.roll(x, 1, 1), 0.0), jnp.where(lane < 127, pltpu.roll(x, 127, 1), 0.0)),
        )
        moved = 0.0
        for c, (lo, hi) in enumerate(sides):
            v = vel[0, c, z]
            moved = moved + (jnp.maximum(v, 0.0) * (x - lo) + jnp.minimum(v, 0.0) * (hi - x))
        y = x - moved
        warp[z] = y
        if z == 0 or z == planes - 1:
            v = jnp.maximum(vel[0, 0, z], 0.0) if z == 0 else jnp.minimum(vel[0, 0, z], 0.0)
            edge = split(y) + split(v) + (image[0, z],)
            for n, part in enumerate(edge):
                (down if z == 0 else up)[8 + n] = part
        else:
            inner[z - 1] = y.astype(bf16)
        if 1 <= z <= 8:
            down[z - 1] = y.astype(bf16)
        if planes - 9 <= z < planes - 1:
            up[z - (planes - 9)] = y.astype(bf16)
    me = lax.axis_index("brain")
    mate = partner[me]
    for n, value in enumerate((me ^ mate, offsets[0, mate] - offsets[0, me], offsets[1, mate] - offsets[1, me])):
        meta[n * 8:n * 8 + 8, :] = jnp.full((8, 128), value, jnp.int32)
    even = lax.rem(lax.axis_index("slab"), 2) == 0
    for n in range(EDGE):
        first[n] = jnp.where(even, up[n], down[n])
        second[n] = jnp.where(even, down[n], up[n])


def widen_kernel(planes, warp, sent1, sent2, got1, got2, out, outer):
    low, high = faces()
    even = lax.rem(lax.axis_index("slab"), 2) == 0
    down, up, below, above = (sent2, sent1), (sent1, sent2), (got2, got1), (got1, got2)
    ld = lambda pair, n: jnp.where(even, pair[0][n], pair[1][n]).astype(f32)
    top = planes - 1
    first, last = ld(down, 12), ld(up, 12)
    for n in range(8):
        out[n] = (ld(below, n) * low).astype(bf16)
        out[planes + 10 + n] = (ld(above, n) * high).astype(bf16)
    out[8] = (low * ((ld(below, 8) + ld(below, 9)) - (ld(below, 10) + ld(below, 11)) * (first - ld(below, 12)))).astype(bf16)
    out[planes + 9] = (high * ((ld(above, 8) + ld(above, 9)) - (ld(above, 10) + ld(above, 11)) * (ld(above, 12) - last))).astype(bf16)
    for z in range(1, top):
        out[9 + z] = warp[z].astype(bf16)
    out[9] = (warp[0] - (ld(down, 10) + ld(down, 11)) * (first - ld(below, 12))).astype(bf16)
    out[9 + top] = (warp[top] - (ld(up, 10) + ld(up, 11)) * (ld(above, 12) - last)).astype(bf16)

    for n in range(10):
        outer[n] = out[n]
        outer[10 + n] = out[planes + 8 + n]


def from_brains(x, partner):
    if lax.axis_size("brain") == 4:
        return [lax.ppermute(x, "brain", [(n, n ^ k) for n in range(4)]) for k in (1, 2, 3)]
    gathered = lax.all_gather(x, "brain")
    return [lax.dynamic_index_in_dim(gathered, partner[lax.axis_index("brain")], 0, keepdims=False)]


def shards(intensity, velocity, partner, offsets):
    planes = intensity.shape[1]
    slabs, brains = lax.axis_size("slab"), lax.axis_size("brain")
    edge = jax.ShapeDtypeStruct((EDGE, 8, 128), bf16)
    warp, inner, first, second, meta = pl.pallas_call(
        functools.partial(advect_kernel, planes),
        out_shape=(jax.ShapeDtypeStruct((planes, 8, 128), f32), jax.ShapeDtypeStruct((planes - 2, 8, 128), bf16), edge, edge, jax.ShapeDtypeStruct((24, 128), jnp.int32)),
        in_specs=[HBM] * 4,
        out_specs=(VM,) * 5,
        scratch_shapes=[
            pltpu.VMEM(intensity.shape, bf16),
            pltpu.VMEM(velocity.shape, f32),
            pltpu.VMEM(edge.shape, bf16),
            pltpu.VMEM(edge.shape, bf16),
            pltpu.SMEM(partner.shape, jnp.int32),
            pltpu.SMEM(offsets.shape[::-1], jnp.int32),
            pltpu.SemaphoreType.DMA((4,)),
        ],
        compiler_params=pltpu.CompilerParams(vmem_limit_bytes=8 * 2**20),
        name="advect",
    )(*[pltpu.with_memory_space_constraint(v, pltpu.HBM) for v in (intensity, velocity, partner, offsets.T)])
    odd_pairs = [(n, n + 1) for n in range(1, slabs - 1, 2)]
    even_pairs = [(n, n + 1) for n in range(0, slabs - 1, 2)]
    both_ways = lambda pairs: pairs + [(b, a) for a, b in pairs]
    from_odd = lax.ppermute(second, "slab", both_ways(odd_pairs))
    from_even = lax.ppermute(first, "slab", both_ways(even_pairs))
    inners = from_brains(inner, partner)
    own, outer = pl.pallas_call(
        functools.partial(widen_kernel, planes),
        out_shape=(jax.ShapeDtypeStruct((planes + 18, 8, 128), bf16), jax.ShapeDtypeStruct((20, 8, 128), bf16)),
        in_specs=[VM] * 5,
        out_specs=(VM,) * 2,
        compiler_params=pltpu.CompilerParams(vmem_limit_bytes=8 * 2**20),
        name="widen",
    )(warp, first, second, from_even, from_odd)
    outers = from_brains(outer, partner)
    return mate_part(planes, inners, outers, meta, own_part(planes, own), velocity[0])[None]


def solution(mesh):
    return jax.shard_map(
        shards,
        mesh=mesh,
        in_specs=(
            P(("groups", "brain"), "slab", None, None),
            P(("groups", "brain"), None, "slab", None, None),
            P("groups"),
            P("groups", None),
        ),
        out_specs=P(("groups", "brain"), None, "slab", None, None),
        check_vma=False,
    )
```

```python
import functools
import jax, jax.numpy as jnp, numpy as np
from jax import lax
from jax.experimental import pallas as pl
from jax.experimental.pallas import tpu as pltpu
from jax.sharding import PartitionSpec as P

PAIRS = tuple((i, j) for i in range(6) for j in range(i + 1, 6) if i // 2 != j // 2)
TAPS = tuple(float(v) for v in np.exp(-np.arange(-3, 4) ** 2 / 4.5) / np.exp(-np.arange(-3, 4) ** 2 / 4.5).sum())
f32, bf16 = jnp.float32, jnp.bfloat16
LOG2E = 1.4426950408889634
EDGE = 13
VOLUME = 729.0
UNROLL = 2
PITCH = 9
SPARE = 16
FLOOR = 1e-5 * VOLUME * VOLUME


def split(v):
    hi = v.astype(bf16)
    return hi, (v - hi.astype(f32)).astype(bf16)


def lanes():
    return (lax.broadcasted_iota(jnp.int32, (128, 128), 0), lax.broadcasted_iota(jnp.int32, (128, 128), 1))


def ones_where(cond):
    return jnp.where(cond, 1.0, 0.0).astype(bf16)


def halves(parts):
    return jnp.concatenate(split(jnp.concatenate(parts, axis=0)), axis=1)


def dot(a, b):
    return jnp.dot(a, b, preferred_element_type=f32)


def faces():
    slab = lax.axis_index("slab")
    one = jnp.float32(1.0)
    zero = jnp.float32(0.0)
    return jnp.where(slab > 0, one, zero), jnp.where(slab < lax.axis_size("slab") - 1, one, zero)


def even_slab():
    return lax.rem(lax.axis_index("slab"), 2) == 0


def row_inside(d):
    row = lax.broadcasted_iota(jnp.int32, (8, 128), 0)
    return (row + d >= 0) & (row + d < 8)


def describe(planes, xs, box3, tb, desc, low, high):
    nd = planes + 16
    ng = nd // 8

    def squares(g, carry, scale=None):
        c1, c2 = carry
        for i in range(8):
            s = g * 8 + i
            ld = lambda n, p: xs[n, pl.ds(pl.multiple_of(p * 8, 8), 8), :]
            near = [ld(0, s + 2), ld(0, s)] + [ld(j, s + 1) for j in (1, 2, 3, 4)]
            n1, n2 = [], []
            done = []
            for k, (a, b) in enumerate(PAIRS):
                d = near[a] - near[b]
                q = d * d
                if scale is not None:
                    q = q * scale
                done.append(c2[k] + q)
                n2.append(c1[k] + q)
                n1.append(q)
            put(s, done)
            c1, c2 = n1, n2
        return c1, c2

    def put(s, done):
        at = pl.ds(s * PITCH, 8)
        for k in range(12):
            tb[k, at, :] = done[k]
        while len(done) > 1:
            done = [done[n] + done[n + 1] for n in range(0, len(done) - 1, 2)] + done[len(done) // 2 * 2:]
        tb[12, at, :] = done[0]

    zero = [jnp.zeros((8, 128), f32)] * 12
    carry = squares(0, (zero, zero), low)
    carry = lax.fori_loop(1, ng - 1, squares, carry)
    c1, c2 = squares(ng - 1, carry, high)
    put(nd, c2)

    for g in range(ng):
        parts = []
        for k in (12,) + tuple(range(12)):
            t = [tb[k, pl.ds((g * 8 + 1) * PITCH + r, 8, stride=PITCH), :] for r in range(8)]
            p = [t[r] + t[r + 1] for r in range(7)]
            parts += [p[0]] + [p[r - 1] + t[r + 1] for r in range(1, 7)] + [p[6]]
        box = dot(halves(parts), box3[...])
        inv = [(-LOG2E / 27.0) / (box[r * 8:r * 8 + 8] * (1.0 / 324.0) + 0.1) for r in range(8)]
        for k in range(12):
            for r in range(8):
                n = (k + 1) * 64 + r * 8
                e = jnp.exp2(box[n:n + 8] * inv[r])
                if g == 0:
                    e = e * low
                if g == ng - 1:
                    e = e * high
                desc[k, pl.ds(g * 8 * PITCH + r, 8, stride=PITCH), :] = e


def depth_sums(planes, value, ys, q):
    nd, nf = planes + 16, planes + 8
    d = [value(t) for t in range(nd)]
    for f in range(nf):
        if f % 16 == 0:
            s2 = [d[f + t] + d[f + t + 1] for t in (0, 2, 4, 6)]
            total = ((s2[0] + s2[1]) + (s2[2] + s2[3])) + d[f + 8]
        else:
            total = (total - d[f - 1]) + d[f + 8]
        ys[q, pl.ds(f * PITCH, 8), :] = total


def row_sums(ys, q, g):
    t = [ys[q, pl.ds(g * 8 * PITCH + r, 8, stride=PITCH), :] for r in range(8)]
    lo = (t[0] + t[1]) + (t[2] + t[3])
    hi = (t[4] + t[5]) + (t[6] + t[7])
    w0 = lo + t[4]
    w1 = w0 + t[5]
    w7 = hi + t[3]
    w6 = w7 + t[2]
    return [w0, w1, w1 + t[6], lo + hi, lo + hi, w6 + t[1], w6, w7]


def own_kernel(planes, own, desc, mean, slope, grads, box3, box9, grad, xs, tb, ys):
    nx, nd, nf = planes + 18, planes + 16, planes + 8
    low, high = faces()
    i, j = lanes()
    for h in (0, 128):
        box3[h:h + 128] = ones_where(jnp.abs(i - j) <= 1)
        box9[h:h + 128] = ones_where(jnp.abs(i - j) <= 4)
        grad[h:h + 128] = jnp.where(i == j + 1, 1.0, jnp.where(i == j - 1, -1.0, 0.0)).astype(bf16)
    x = own[...]
    xs[0] = x.astype(f32)
    xs[3] = dot(x, ones_where(i == j + 1))
    xs[4] = dot(x, ones_where(i == j - 1))

    def prep(p, _):
        at = pl.ds(pl.multiple_of(p * 8, 8), 8)
        v = xs[0, at, :]
        xs[1, at, :] = jnp.where(row_inside(1), pltpu.roll(v, 7, 0), 0.0)
        xs[2, at, :] = jnp.where(row_inside(-1), pltpu.roll(v, 1, 0), 0.0)
        return 0
    lax.fori_loop(0, nx, prep, 0, unroll=6)
    describe(planes, xs, box3, tb, desc, low, high)

    def channels(k, _):
        for h in range(UNROLL):
            one_channel(UNROLL * k + h, h)
        return 0

    def one_channel(k, h):
        ld = lambda t: desc[k, pl.ds(t * PITCH, 8), :]
        depth_sums(planes, ld, ys, 2 * h)
        depth_sums(planes, lambda t: ld(t) * ld(t), ys, 2 * h + 1)
        parts, centre = [], []
        for g in range(nf // 8):
            for q in range(2):
                parts += row_sums(ys, 2 * h + q, g)
            centre += [desc[k, pl.ds((g * 8 + 4) * PITCH + r, 8, stride=PITCH), :] for r in range(8)]
        sums = dot(halves(parts), box9[...])
        across = dot(halves(centre), grad[...])
        for g in range(nf // 8):
            a = centre[g * 8:g * 8 + 8]
            for r in range(8):
                at = pl.ds(g * 64 + r * 8, 8)
                mo, so = [sums[(g * 16 + q * 8 + r) * 8:(g * 16 + q * 8 + r) * 8 + 8] for q in range(2)]
                gc = across[(g * 8 + r) * 8:(g * 8 + r) * 8 + 8]
                inv = lax.rsqrt(VOLUME * so - mo * mo + FLOOR)
                gz = desc[k, pl.ds((g * 8 + 5) * PITCH + r, 8, stride=PITCH), :] - desc[k, pl.ds((g * 8 + 3) * PITCH + r, 8, stride=PITCH), :]
                gr = a[1] if r == 0 else -a[6] if r == 7 else a[r + 1] - a[r - 1]
                mean[k, at, :] = mo
                slope[k, at, :] = (inv * inv) * (VOLUME * a[r] - mo)
                for c, gg in enumerate((gz, gr, gc)):
                    grads[c, k, at, :] = gg * inv
    lax.fori_loop(0, 12 // UNROLL, channels, 0)


def mate_kernel(planes, count, *refs):
    inner, outer = refs[:count], refs[count:2 * count]
    meta, adesc, mean, slope, grads, vel, out, box3, box9, smooth, xs, raw, tb, desc, ys, frc = refs[2 * count:]
    nx, nd, nf = planes + 18, planes + 16, planes + 8
    low, high = faces()
    which, dc = meta[0:1, :], meta[16:17, :]
    dr = jnp.max(meta[8:16, :])
    i, j = lanes()
    weights = jnp.zeros((128, 128), f32)
    for d in range(4):
        weights = jnp.where(jnp.abs(i - j) == d, TAPS[3 + d], weights)
    whi, wlo = split(weights)
    for h in (0, 128):
        box3[h:h + 128] = ones_where(jnp.abs(i - j) <= 1)
        box9[h:h + 128] = ones_where(jnp.abs(i - j) <= 4)
        smooth[h:h + 128] = whi
    smooth[256:384] = wlo
    row = lax.broadcasted_iota(jnp.int32, (8, 128), 0)

    x, y = inner[0][...], outer[0][...]
    for n in range(1, count):
        x = jnp.where(which == n + 1, inner[n][...], x)
        y = jnp.where(which == n + 1, outer[n][...], y)
    middle = (planes - 2) * 8
    even = even_slab()
    x, side = x[0:middle], x[middle:middle + 80]
    x = jnp.concatenate([jnp.where(even, y, side), x, jnp.where(even, side, y)], axis=0)
    for n, d in ((0, 0), (1, 1), (2, -1)):
        take = ones_where((i == j + d + dc) & (j + d >= 0) & (j + d < 128))
        raw[n, pl.ds(8, nx * 8), :] = dot(x, take)

    def prep(p, _):
        at = pl.multiple_of(p * 8, 8)
        for n, b, d in ((0, 0, 0), (1, 0, 1), (2, 0, -1), (3, 1, 0), (4, 2, 0)):
            v = raw[b, pl.ds(at + 8 + dr + d, 8), :]
            xs[n, pl.ds(at, 8), :] = jnp.where(row_inside(d) & row_inside(d + dr), v, 0.0)
        return 0
    lax.fori_loop(0, nx, prep, 0, unroll=6)
    describe(planes, xs, box3, tb, desc, low, high)

    def channels(step, _):
        ks = [UNROLL * step + h for h in range(UNROLL)]
        sums = []
        for h, k in enumerate(ks):
            lda = lambda t: adesc[k, pl.ds(t * PITCH, 8), :]
            ldb = lambda t: desc[k, pl.ds(t * PITCH, 8), :]
            depth_sums(planes, ldb, ys, 3 * h)
            depth_sums(planes, lambda t: ldb(t) * ldb(t), ys, 3 * h + 1)
            depth_sums(planes, lambda t: lda(t) * ldb(t), ys, 3 * h + 2)
            parts = []
            for g in range(nf // 8):
                for q in range(3):
                    parts += row_sums(ys, 3 * h + q, g)
            sums.append(dot(halves(parts), box9[...]))
        for g in range(nf // 8):
            for r in range(8):
                at = pl.ds(g * 64 + r * 8, 8)
                acc = [frc[c, at, :] for c in range(3)]
                for h, k in enumerate(ks):
                    mm, sm, sc = [sums[h][(g * 24 + q * 8 + r) * 8:(g * 24 + q * 8 + r) * 8 + 8] for q in range(3)]
                    b = desc[k, pl.ds((g * 8 + 4) * PITCH + r, 8, stride=PITCH), :]
                    inv = lax.rsqrt(VOLUME * sm - mm * mm + FLOOR)
                    cov = VOLUME * sc - mean[k, at, :] * mm
                    coef = (VOLUME * b - mm - cov * slope[k, at, :]) * inv
                    acc = [acc[c] + coef * grads[c, k, at, :] for c in range(3)]
                for c in range(3):
                    frc[c, at, :] = acc[c]
        return 0
    frc[...] = jnp.zeros_like(frc)
    lax.fori_loop(0, 12 // UNROLL, channels, 0)

    parts = []
    for c in range(3):
        for g in range(nf // 8):
            for r in range(8):
                v = frc[c, pl.ds(g * 64 + r * 8, 8), :]
                if g == 0:
                    v = jnp.where(row >= 4, v, v * low)
                if g == nf // 8 - 1:
                    v = jnp.where(row < 4, v, v * high)
                ys[0, pl.ds(g * 8 * PITCH + r, 8, stride=PITCH), :] = v
        for o in range(planes):
            p = [ys[0, pl.ds((o + 1 + n) * PITCH, 8), :] for n in range(7)]
            v = TAPS[3] * p[3]
            for n in range(3):
                v = v + TAPS[n] * (p[n] + p[6 - n])
            ys[1, pl.ds(o * PITCH, 8), :] = v
        for g in range(planes // 8):
            t = [ys[1, pl.ds(g * 8 * PITCH + r, 8, stride=PITCH), :] for r in range(8)]
            for r in range(8):
                v = TAPS[3] * t[r]
                for n in range(1, 4):
                    s = [t[q] for q in (r - n, r + n) if 0 <= q < 8]
                    v = v + TAPS[3 + n] * (s[0] + s[1] if len(s) == 2 else s[0])
                parts.append(v)
    both = halves(parts)
    res = dot(both, smooth[0:256]) + dot(both[:, 0:128], smooth[256:384])
    for c in range(3):
        for g in range(planes // 8):
            for r in range(8):
                n = ((c * planes + g * 8) + r) * 8
                ys[0, pl.ds(g * 8 * PITCH + r, 8, stride=PITCH), :] = res[n:n + 8]
        for o in range(planes):
            out[c, o] = vel[c, o] + (8.0 * VOLUME / 24.0) * ys[0, pl.ds(o * PITCH, 8), :]


VM = pl.BlockSpec(memory_space=pltpu.VMEM)
HBM = pl.BlockSpec(memory_space=pltpu.HBM)


def own_part(planes, own):
    nx, nd, nf = planes + 18, planes + 16, planes + 8
    shape = jax.ShapeDtypeStruct
    return pl.pallas_call(
        functools.partial(own_kernel, planes),
        out_shape=(
            shape((12, nd * PITCH + SPARE, 128), f32),
            shape((12, nf * 8, 128), f32),
            shape((12, nf * 8, 128), f32),
            shape((3, 12, nf * 8, 128), f32),
        ),
        in_specs=[VM],
        out_specs=(VM,) * 4,
        scratch_shapes=[
            pltpu.VMEM((256, 128), bf16),
            pltpu.VMEM((256, 128), bf16),
            pltpu.VMEM((256, 128), bf16),
            pltpu.VMEM((5, nx * 8, 128), f32),
            pltpu.VMEM((13, (nd + 1) * PITCH + SPARE, 128), f32),
            pltpu.VMEM((2 * UNROLL, nf * PITCH + SPARE, 128), f32),
        ],
        compiler_params=pltpu.CompilerParams(vmem_limit_bytes=16 * 2**20),
        cost_estimate=pl.CostEstimate(flops=10**6, bytes_accessed=2**16, transcendentals=0),
        name="own",
    )(own.reshape(-1, 128))


def mate_part(planes, inner, outer, meta, owned, vel):
    nx, nd, nf = planes + 18, planes + 16, planes + 8
    count = len(inner)
    return pl.pallas_call(
        functools.partial(mate_kernel, planes, count),
        out_shape=jax.ShapeDtypeStruct(vel.shape, f32),
        in_specs=[VM] * (2 * count + 6),
        out_specs=VM,
        scratch_shapes=[
            pltpu.VMEM((256, 128), bf16),
            pltpu.VMEM((256, 128), bf16),
            pltpu.VMEM((384, 128), bf16),
            pltpu.VMEM((5, nx * 8, 128), f32),
            pltpu.VMEM((3, nx * 8 + 16, 128), f32),
            pltpu.VMEM((13, (nd + 1) * PITCH + SPARE, 128), f32),
            pltpu.VMEM((12, nd * PITCH + SPARE, 128), f32),
            pltpu.VMEM((3 * UNROLL, nf * PITCH + SPARE, 128), f32),
            pltpu.VMEM((3, nf * 8, 128), f32),
        ],
        compiler_params=pltpu.CompilerParams(vmem_limit_bytes=16 * 2**20),
        name="mate",
    )(*[m.reshape(-1, 128) for m in inner + outer], meta, *owned, vel)


def advect_kernel(planes, image_hbm, vel_hbm, partner_hbm, offsets_hbm, warp, first, second, meta, image, vel, down, up, partner, offsets, sems):
    copies = [
        pltpu.make_async_copy(vel_hbm, vel, sems.at[0]),
        pltpu.make_async_copy(image_hbm, image, sems.at[1]),
        pltpu.make_async_copy(partner_hbm, partner, sems.at[2]),
        pltpu.make_async_copy(offsets_hbm, offsets, sems.at[3]),
    ]
    for copy in copies:
        copy.start()
    for copy in copies:
        copy.wait()
    lane = lax.broadcasted_iota(jnp.int32, (8, 128), 1)

    for z in range(planes):
        x = image[0, z].astype(f32)
        before = image[0, z - 1].astype(f32) if z > 0 else x
        after = image[0, z + 1].astype(f32) if z < planes - 1 else x
        sides = (
            (before, after),
            (jnp.where(row_inside(-1), pltpu.roll(x, 1, 0), 0.0), jnp.where(row_inside(1), pltpu.roll(x, 7, 0), 0.0)),
            (jnp.where(lane >= 1, pltpu.roll(x, 1, 1), 0.0), jnp.where(lane < 127, pltpu.roll(x, 127, 1), 0.0)),
        )
        moved = 0.0
        for c, (lo, hi) in enumerate(sides):
            v = vel[0, c, z]
            moved = moved + (jnp.maximum(v, 0.0) * (x - lo) + jnp.minimum(v, 0.0) * (hi - x))
        y = x - moved
        warp[z] = y
        if z == 0 or z == planes - 1:
            v = jnp.maximum(vel[0, 0, z], 0.0) if z == 0 else jnp.minimum(vel[0, 0, z], 0.0)
            edge = split(y) + split(v) + (image[0, z],)
            for n, part in enumerate(edge):
                (down if z == 0 else up)[8 + n] = part
        if 1 <= z <= 8:
            down[z - 1] = y.astype(bf16)
        if planes - 9 <= z < planes - 1:
            up[z - (planes - 9)] = y.astype(bf16)
    me = lax.axis_index("brain")
    mate = partner[me]
    for n, value in enumerate((me ^ mate, offsets[0, mate] - offsets[0, me], offsets[1, mate] - offsets[1, me])):
        meta[n * 8:n * 8 + 8, :] = jnp.full((8, 128), value, jnp.int32)
    even = even_slab()
    for n in range(EDGE):
        first[n] = jnp.where(even, up[n], down[n])
        second[n] = jnp.where(even, down[n], up[n])


def face_planes(planes, warp, mine, got, put, bottom):
    ld = lambda ref, n: ref[n].astype(f32)
    v, x0, x1 = ld(mine, 10) + ld(mine, 11), ld(mine, 12), ld(got, 12)
    w = ld(got, 10) + ld(got, 11)
    here = jnp.where(bottom, warp[0], warp[planes - 1])
    step = jnp.where(bottom, x0 - x1, x1 - x0)
    near = here - v * step
    far = (ld(got, 8) + ld(got, 9)) - w * step
    low, high = faces()
    scale = jnp.where(bottom, low, high)
    planes_got = [ld(got, n) * scale for n in range(8)]
    up = [near, far * scale] + planes_got
    down = planes_got + [far * scale, near]
    for n in range(10):
        put(n, jnp.where(bottom, down[n], up[n]).astype(bf16))


def widen_even_kernel(planes, warp, mine, got, out):
    for z in range(1, planes - 1):
        out[z - 1] = warp[z].astype(bf16)

    def put(n, value):
        out[planes - 2 + n] = value
    face_planes(planes, warp, mine, got, put, jnp.logical_not(even_slab()))


def widen_odd_kernel(planes, warp, mine, got, most, own, outer):
    even = even_slab()

    def put(n, value):
        outer[n] = value
    face_planes(planes, warp, mine, got, put, even)
    for z in range(planes - 2):
        own[10 + z] = most[z]
    for n in range(10):
        a, b = outer[n], most[planes - 2 + n]
        own[n] = jnp.where(even, a, b)
        own[planes + 8 + n] = jnp.where(even, b, a)


def from_brains(x, partner, order=(1, 2, 3)):
    if lax.axis_size("brain") == 4:
        got = {k: lax.ppermute(x, "brain", [(n, n ^ k) for n in range(4)]) for k in order}
        return [got[k] for k in (1, 2, 3)]
    gathered = lax.all_gather(x, "brain")
    return [lax.dynamic_index_in_dim(gathered, partner[lax.axis_index("brain")], 0, keepdims=False)]


def shards(intensity, velocity, partner, offsets):
    planes = intensity.shape[1]
    slabs, brains = lax.axis_size("slab"), lax.axis_size("brain")
    edge = jax.ShapeDtypeStruct((EDGE, 8, 128), bf16)
    warp, first, second, meta = pl.pallas_call(
        functools.partial(advect_kernel, planes),
        out_shape=(jax.ShapeDtypeStruct((planes, 8, 128), f32), edge, edge, jax.ShapeDtypeStruct((24, 128), jnp.int32)),
        in_specs=[HBM] * 4,
        out_specs=(VM,) * 4,
        scratch_shapes=[
            pltpu.VMEM(intensity.shape, bf16),
            pltpu.VMEM(velocity.shape, f32),
            pltpu.VMEM(edge.shape, bf16),
            pltpu.VMEM(edge.shape, bf16),
            pltpu.SMEM(partner.shape, jnp.int32),
            pltpu.SMEM(offsets.shape[::-1], jnp.int32),
            pltpu.SemaphoreType.DMA((4,)),
        ],
        compiler_params=pltpu.CompilerParams(vmem_limit_bytes=8 * 2**20),
        name="advect",
    )(*[pltpu.with_memory_space_constraint(v, pltpu.HBM) for v in (intensity, velocity, partner, offsets.T)])
    odd_pairs = [(n, n + 1) for n in range(1, slabs - 1, 2)]
    even_pairs = [(n, n + 1) for n in range(0, slabs - 1, 2)]
    both_ways = lambda pairs: pairs + [(b, a) for a, b in pairs]
    from_odd = lax.ppermute(second, "slab", both_ways(odd_pairs))
    from_even = lax.ppermute(first, "slab", both_ways(even_pairs))
    small = pltpu.CompilerParams(vmem_limit_bytes=8 * 2**20)
    most = pl.pallas_call(
        functools.partial(widen_even_kernel, planes),
        out_shape=jax.ShapeDtypeStruct((planes + 8, 8, 128), bf16),
        in_specs=[VM] * 3,
        out_specs=VM,
        compiler_params=small,
        name="widen_even",
    )(warp, first, from_even)
    inners = from_brains(most, partner)
    own, outer = pl.pallas_call(
        functools.partial(widen_odd_kernel, planes),
        out_shape=(jax.ShapeDtypeStruct((planes + 18, 8, 128), bf16), jax.ShapeDtypeStruct((10, 8, 128), bf16)),
        in_specs=[VM] * 4,
        out_specs=(VM,) * 2,
        compiler_params=small,
        name="widen_odd",
    )(warp, second, from_odd, most)
    outers = from_brains(outer, partner, (3, 2, 1))
    return mate_part(planes, inners, outers, meta, own_part(planes, own), velocity[0])[None]


def solution(mesh):
    return jax.shard_map(
        shards,
        mesh=mesh,
        in_specs=(
            P(("groups", "brain"), "slab", None, None),
            P(("groups", "brain"), None, "slab", None, None),
            P("groups"),
            P("groups", None),
        ),
        out_specs=P(("groups", "brain"), None, "slab", None, None),
        check_vma=False,
    )
```

```python
import functools
import jax, jax.numpy as jnp, numpy as np
from jax import lax
from jax.experimental import pallas as pl
from jax.experimental.pallas import tpu as pltpu
from jax.sharding import PartitionSpec as P

PAIRS = tuple((i, j) for i in range(6) for j in range(i + 1, 6) if i // 2 != j // 2)
TAPS = tuple(float(v) for v in np.exp(-np.arange(-3, 4) ** 2 / 4.5) / np.exp(-np.arange(-3, 4) ** 2 / 4.5).sum())
f32, bf16 = jnp.float32, jnp.bfloat16
LOG2E = 1.4426950408889634
EDGE = 13
VOLUME = 729.0
UNROLL = 2
PITCH = 9
SPARE = 16
FLOOR = 1e-5 * VOLUME * VOLUME


def split(v):
    hi = v.astype(bf16)
    return hi, (v - hi.astype(f32)).astype(bf16)


def lanes():
    return (lax.broadcasted_iota(jnp.int32, (128, 128), 0), lax.broadcasted_iota(jnp.int32, (128, 128), 1))


def ones_where(cond):
    return jnp.where(cond, 1.0, 0.0).astype(bf16)


def halves(parts):
    return jnp.concatenate(split(jnp.concatenate(parts, axis=0)), axis=1)


def dot(a, b):
    return jnp.dot(a, b, preferred_element_type=f32)


def faces():
    slab = lax.axis_index("slab")
    one = jnp.float32(1.0)
    zero = jnp.float32(0.0)
    return jnp.where(slab > 0, one, zero), jnp.where(slab < lax.axis_size("slab") - 1, one, zero)


def even_slab():
    return lax.rem(lax.axis_index("slab"), 2) == 0


def row_inside(d):
    row = lax.broadcasted_iota(jnp.int32, (8, 128), 0)
    return (row + d >= 0) & (row + d < 8)


def describe(planes, xs, box3, tb, desc, low, high):
    nd = planes + 16
    ng = nd // 8

    def squares(g, carry, scale=None):
        c1, c2 = carry
        for i in range(8):
            s = g * 8 + i
            ld = lambda n, p: xs[n, pl.ds(pl.multiple_of(p * 8, 8), 8), :]
            near = [ld(0, s + 2), ld(0, s)] + [ld(j, s + 1) for j in (1, 2, 3, 4)]
            n1, n2 = [], []
            done = []
            for k, (a, b) in enumerate(PAIRS):
                d = near[a] - near[b]
                q = d * d
                if scale is not None:
                    q = q * scale
                done.append(c2[k] + q)
                n2.append(c1[k] + q)
                n1.append(q)
            put(s, done)
            c1, c2 = n1, n2
        return c1, c2

    def put(s, done):
        at = pl.ds(s * PITCH, 8)
        for k in range(12):
            tb[k, at, :] = done[k]
        while len(done) > 1:
            done = [done[n] + done[n + 1] for n in range(0, len(done) - 1, 2)] + done[len(done) // 2 * 2:]
        tb[12, at, :] = done[0]

    zero = [jnp.zeros((8, 128), f32)] * 12
    carry = squares(0, (zero, zero), low)
    carry = lax.fori_loop(1, ng - 1, squares, carry)
    c1, c2 = squares(ng - 1, carry, high)
    put(nd, c2)

    for g in range(ng):
        parts = []
        for k in (12,) + tuple(range(12)):
            t = [tb[k, pl.ds((g * 8 + 1) * PITCH + r, 8, stride=PITCH), :] for r in range(8)]
            p = [t[r] + t[r + 1] for r in range(7)]
            parts += [p[0]] + [p[r - 1] + t[r + 1] for r in range(1, 7)] + [p[6]]
        box = dot(halves(parts), box3[...])
        inv = [(-LOG2E / 27.0) / (box[r * 8:r * 8 + 8] * (1.0 / 324.0) + 0.1) for r in range(8)]
        for k in range(12):
            for r in range(8):
                n = (k + 1) * 64 + r * 8
                e = jnp.exp2(box[n:n + 8] * inv[r])
                if g == 0:
                    e = e * low
                if g == ng - 1:
                    e = e * high
                desc[k, pl.ds(g * 8 * PITCH + r, 8, stride=PITCH), :] = e


def depth_sums(planes, value, ys, q):
    nd, nf = planes + 16, planes + 8
    d = [value(t) for t in range(nd)]
    for f in range(nf):
        if f % 16 == 0:
            s2 = [d[f + t] + d[f + t + 1] for t in (0, 2, 4, 6)]
            total = ((s2[0] + s2[1]) + (s2[2] + s2[3])) + d[f + 8]
        else:
            total = (total - d[f - 1]) + d[f + 8]
        ys[q, pl.ds(f * PITCH, 8), :] = total


def row_sums(ys, q, g):
    t = [ys[q, pl.ds(g * 8 * PITCH + r, 8, stride=PITCH), :] for r in range(8)]
    lo = (t[0] + t[1]) + (t[2] + t[3])
    hi = (t[4] + t[5]) + (t[6] + t[7])
    w0 = lo + t[4]
    w1 = w0 + t[5]
    w7 = hi + t[3]
    w6 = w7 + t[2]
    return [w0, w1, w1 + t[6], lo + hi, lo + hi, w6 + t[1], w6, w7]


def own_kernel(planes, own, desc, mean, slope, grads, box3, box9, grad, xs, tb, ys):
    nx, nd, nf = planes + 18, planes + 16, planes + 8
    low, high = faces()
    i, j = lanes()
    for h in (0, 128):
        box3[h:h + 128] = ones_where(jnp.abs(i - j) <= 1)
        box9[h:h + 128] = ones_where(jnp.abs(i - j) <= 4)
        grad[h:h + 128] = jnp.where(i == j + 1, 1.0, jnp.where(i == j - 1, -1.0, 0.0)).astype(bf16)
    x = own[...]
    xs[0] = x.astype(f32)
    xs[3] = dot(x, ones_where(i == j + 1))
    xs[4] = dot(x, ones_where(i == j - 1))

    def prep(p, _):
        at = pl.ds(pl.multiple_of(p * 8, 8), 8)
        v = xs[0, at, :]
        xs[1, at, :] = jnp.where(row_inside(1), pltpu.roll(v, 7, 0), 0.0)
        xs[2, at, :] = jnp.where(row_inside(-1), pltpu.roll(v, 1, 0), 0.0)
        return 0
    lax.fori_loop(0, nx, prep, 0, unroll=6)
    describe(planes, xs, box3, tb, desc, low, high)

    def channels(k, _):
        for h in range(UNROLL):
            one_channel(UNROLL * k + h, h)
        return 0

    def one_channel(k, h):
        ld = lambda t: desc[k, pl.ds(t * PITCH, 8), :]
        depth_sums(planes, ld, ys, 2 * h)
        depth_sums(planes, lambda t: ld(t) * ld(t), ys, 2 * h + 1)
        parts, centre = [], []
        for g in range(nf // 8):
            for q in range(2):
                parts += row_sums(ys, 2 * h + q, g)
            centre += [desc[k, pl.ds((g * 8 + 4) * PITCH + r, 8, stride=PITCH), :] for r in range(8)]
        sums = dot(halves(parts), box9[...])
        across = dot(halves(centre), grad[...])
        for g in range(nf // 8):
            a = centre[g * 8:g * 8 + 8]
            for r in range(8):
                at = pl.ds(g * 64 + r * 8, 8)
                mo, so = [sums[(g * 16 + q * 8 + r) * 8:(g * 16 + q * 8 + r) * 8 + 8] for q in range(2)]
                gc = across[(g * 8 + r) * 8:(g * 8 + r) * 8 + 8]
                inv = lax.rsqrt(VOLUME * so - mo * mo + FLOOR)
                gz = desc[k, pl.ds((g * 8 + 5) * PITCH + r, 8, stride=PITCH), :] - desc[k, pl.ds((g * 8 + 3) * PITCH + r, 8, stride=PITCH), :]
                gr = a[1] if r == 0 else -a[6] if r == 7 else a[r + 1] - a[r - 1]
                mean[k, at, :] = mo
                slope[k, at, :] = (inv * inv) * (VOLUME * a[r] - mo)
                for c, gg in enumerate((gz, gr, gc)):
                    grads[c, k, at, :] = gg * inv
    lax.fori_loop(0, 12 // UNROLL, channels, 0)


def mate_kernel(planes, count, *refs):
    inner, outer = refs[:count], refs[count:2 * count][::-1]
    meta, adesc, mean, slope, grads, vel_hbm, out, box3, box9, smooth, xs, raw, tb, desc, ys, frc, vel, sem = refs[2 * count:]
    fetch = pltpu.make_async_copy(vel_hbm, vel, sem)
    fetch.start()
    nx, nd, nf = planes + 18, planes + 16, planes + 8
    low, high = faces()
    which, dc = meta[0:1, :], meta[16:17, :]
    dr = jnp.max(meta[8:16, :])
    i, j = lanes()
    weights = jnp.zeros((128, 128), f32)
    for d in range(4):
        weights = jnp.where(jnp.abs(i - j) == d, TAPS[3 + d], weights)
    whi, wlo = split(weights)
    for h in (0, 128):
        box3[h:h + 128] = ones_where(jnp.abs(i - j) <= 1)
        box9[h:h + 128] = ones_where(jnp.abs(i - j) <= 4)
        smooth[h:h + 128] = whi
    smooth[256:384] = wlo
    row = lax.broadcasted_iota(jnp.int32, (8, 128), 0)

    x, y = inner[0][...], outer[0][...]
    for n in range(1, count):
        x = jnp.where(which == n + 1, inner[n][...], x)
        y = jnp.where(which == n + 1, outer[n][...], y)
    middle = (planes - 2) * 8
    even = even_slab()
    x, side = x[0:middle], x[middle:middle + 80]
    x = jnp.concatenate([jnp.where(even, y, side), x, jnp.where(even, side, y)], axis=0)
    for n, d in ((0, 0), (1, 1), (2, -1)):
        take = ones_where((i == j + d + dc) & (j + d >= 0) & (j + d < 128))
        raw[n, pl.ds(8, nx * 8), :] = dot(x, take)

    def prep(p, _):
        at = pl.multiple_of(p * 8, 8)
        for n, b, d in ((0, 0, 0), (1, 0, 1), (2, 0, -1), (3, 1, 0), (4, 2, 0)):
            v = raw[b, pl.ds(at + 8 + dr + d, 8), :]
            xs[n, pl.ds(at, 8), :] = jnp.where(row_inside(d) & row_inside(d + dr), v, 0.0)
        return 0
    lax.fori_loop(0, nx, prep, 0, unroll=6)
    describe(planes, xs, box3, tb, desc, low, high)

    def channels(step, _):
        ks = [UNROLL * step + h for h in range(UNROLL)]
        sums = []
        for h, k in enumerate(ks):
            lda = lambda t: adesc[k, pl.ds(t * PITCH, 8), :]
            ldb = lambda t: desc[k, pl.ds(t * PITCH, 8), :]
            depth_sums(planes, ldb, ys, 3 * h)
            depth_sums(planes, lambda t: ldb(t) * ldb(t), ys, 3 * h + 1)
            depth_sums(planes, lambda t: lda(t) * ldb(t), ys, 3 * h + 2)
            parts = []
            for g in range(nf // 8):
                for q in range(3):
                    parts += row_sums(ys, 3 * h + q, g)
            sums.append(dot(halves(parts), box9[...]))
        for g in range(nf // 8):
            for r in range(8):
                at = pl.ds(g * 64 + r * 8, 8)
                acc = [frc[c, at, :] for c in range(3)]
                for h, k in enumerate(ks):
                    mm, sm, sc = [sums[h][(g * 24 + q * 8 + r) * 8:(g * 24 + q * 8 + r) * 8 + 8] for q in range(3)]
                    b = desc[k, pl.ds((g * 8 + 4) * PITCH + r, 8, stride=PITCH), :]
                    inv = lax.rsqrt(VOLUME * sm - mm * mm + FLOOR)
                    cov = VOLUME * sc - mean[k, at, :] * mm
                    coef = (VOLUME * b - mm - cov * slope[k, at, :]) * inv
                    acc = [acc[c] + coef * grads[c, k, at, :] for c in range(3)]
                for c in range(3):
                    frc[c, at, :] = acc[c]
        return 0
    frc[...] = jnp.zeros_like(frc)
    lax.fori_loop(0, 12 // UNROLL, channels, 0)

    parts = []
    for c in range(3):
        for g in range(nf // 8):
            for r in range(8):
                v = frc[c, pl.ds(g * 64 + r * 8, 8), :]
                if g == 0:
                    v = jnp.where(row >= 4, v, v * low)
                if g == nf // 8 - 1:
                    v = jnp.where(row < 4, v, v * high)
                ys[0, pl.ds(g * 8 * PITCH + r, 8, stride=PITCH), :] = v
        for o in range(planes):
            p = [ys[0, pl.ds((o + 1 + n) * PITCH, 8), :] for n in range(7)]
            v = TAPS[3] * p[3]
            for n in range(3):
                v = v + TAPS[n] * (p[n] + p[6 - n])
            ys[1, pl.ds(o * PITCH, 8), :] = v
        for g in range(planes // 8):
            t = [ys[1, pl.ds(g * 8 * PITCH + r, 8, stride=PITCH), :] for r in range(8)]
            for r in range(8):
                v = TAPS[3] * t[r]
                for n in range(1, 4):
                    s = [t[q] for q in (r - n, r + n) if 0 <= q < 8]
                    v = v + TAPS[3 + n] * (s[0] + s[1] if len(s) == 2 else s[0])
                parts.append(v)
    fetch.wait()
    both = halves(parts)
    res = dot(both, smooth[0:256]) + dot(both[:, 0:128], smooth[256:384])
    for c in range(3):
        for g in range(planes // 8):
            for r in range(8):
                n = ((c * planes + g * 8) + r) * 8
                ys[0, pl.ds(g * 8 * PITCH + r, 8, stride=PITCH), :] = res[n:n + 8]
        for o in range(planes):
            out[c, o] = vel[c, o] + (8.0 * VOLUME / 24.0) * ys[0, pl.ds(o * PITCH, 8), :]


VM = pl.BlockSpec(memory_space=pltpu.VMEM)
HBM = pl.BlockSpec(memory_space=pltpu.HBM)


def own_part(planes, own):
    nx, nd, nf = planes + 18, planes + 16, planes + 8
    shape = jax.ShapeDtypeStruct
    return pl.pallas_call(
        functools.partial(own_kernel, planes),
        out_shape=(
            shape((12, nd * PITCH + SPARE, 128), f32),
            shape((12, nf * 8, 128), f32),
            shape((12, nf * 8, 128), f32),
            shape((3, 12, nf * 8, 128), f32),
        ),
        in_specs=[VM],
        out_specs=(VM,) * 4,
        scratch_shapes=[
            pltpu.VMEM((256, 128), bf16),
            pltpu.VMEM((256, 128), bf16),
            pltpu.VMEM((256, 128), bf16),
            pltpu.VMEM((5, nx * 8, 128), f32),
            pltpu.VMEM((13, (nd + 1) * PITCH + SPARE, 128), f32),
            pltpu.VMEM((2 * UNROLL, nf * PITCH + SPARE, 128), f32),
        ],
        compiler_params=pltpu.CompilerParams(vmem_limit_bytes=16 * 2**20),
        cost_estimate=pl.CostEstimate(flops=10**6, bytes_accessed=2**16, transcendentals=0),
        name="own",
    )(own.reshape(-1, 128))


def mate_part(planes, inner, outer, meta, owned, vel):
    nx, nd, nf = planes + 18, planes + 16, planes + 8
    count = len(inner)
    return pl.pallas_call(
        functools.partial(mate_kernel, planes, count),
        out_shape=jax.ShapeDtypeStruct(vel.shape, f32),
        in_specs=[VM] * (2 * count + 5) + [HBM],
        out_specs=VM,
        scratch_shapes=[
            pltpu.VMEM((256, 128), bf16),
            pltpu.VMEM((256, 128), bf16),
            pltpu.VMEM((384, 128), bf16),
            pltpu.VMEM((5, nx * 8, 128), f32),
            pltpu.VMEM((3, nx * 8 + 16, 128), f32),
            pltpu.VMEM((13, (nd + 1) * PITCH + SPARE, 128), f32),
            pltpu.VMEM((12, nd * PITCH + SPARE, 128), f32),
            pltpu.VMEM((3 * UNROLL, nf * PITCH + SPARE, 128), f32),
            pltpu.VMEM((3, nf * 8, 128), f32),
            pltpu.VMEM(vel.shape, f32),
            pltpu.SemaphoreType.DMA,
        ],
        compiler_params=pltpu.CompilerParams(vmem_limit_bytes=16 * 2**20),
        name="mate",
    )(*[m.reshape(-1, 128) for m in inner + outer[::-1]], meta, *owned, pltpu.with_memory_space_constraint(vel, pltpu.HBM))


def advect_kernel(planes, image_hbm, vel_hbm, partner_hbm, offsets_hbm, warp, first, second, meta, image, vel, down, up, partner, offsets, sems):
    copies = [
        pltpu.make_async_copy(vel_hbm, vel, sems.at[0]),
        pltpu.make_async_copy(image_hbm, image, sems.at[1]),
        pltpu.make_async_copy(partner_hbm, partner, sems.at[2]),
        pltpu.make_async_copy(offsets_hbm, offsets, sems.at[3]),
    ]
    for copy in copies:
        copy.start()
    for copy in copies:
        copy.wait()
    lane = lax.broadcasted_iota(jnp.int32, (8, 128), 1)

    for z in range(planes):
        x = image[0, z].astype(f32)
        before = image[0, z - 1].astype(f32) if z > 0 else x
        after = image[0, z + 1].astype(f32) if z < planes - 1 else x
        sides = (
            (before, after),
            (jnp.where(row_inside(-1), pltpu.roll(x, 1, 0), 0.0), jnp.where(row_inside(1), pltpu.roll(x, 7, 0), 0.0)),
            (jnp.where(lane >= 1, pltpu.roll(x, 1, 1), 0.0), jnp.where(lane < 127, pltpu.roll(x, 127, 1), 0.0)),
        )
        moved = 0.0
        for c, (lo, hi) in enumerate(sides):
            v = vel[0, c, z]
            moved = moved + (jnp.maximum(v, 0.0) * (x - lo) + jnp.minimum(v, 0.0) * (hi - x))
        y = x - moved
        warp[z] = y
        if z == 0 or z == planes - 1:
            v = jnp.maximum(vel[0, 0, z], 0.0) if z == 0 else jnp.minimum(vel[0, 0, z], 0.0)
            edge = split(y) + split(v) + (image[0, z],)
            for n, part in enumerate(edge):
                (down if z == 0 else up)[8 + n] = part
        if 1 <= z <= 8:
            down[z - 1] = y.astype(bf16)
        if planes - 9 <= z < planes - 1:
            up[z - (planes - 9)] = y.astype(bf16)
    me = lax.axis_index("brain")
    mate = partner[me]
    for n, value in enumerate((me ^ mate, offsets[0, mate] - offsets[0, me], offsets[1, mate] - offsets[1, me])):
        meta[n * 8:n * 8 + 8, :] = jnp.full((8, 128), value, jnp.int32)
    even = even_slab()
    for n in range(EDGE):
        first[n] = jnp.where(even, up[n], down[n])
        second[n] = jnp.where(even, down[n], up[n])


def face_planes(planes, warp, mine, got, put, bottom):
    ld = lambda ref, n: ref[n].astype(f32)
    v, x0, x1 = ld(mine, 10) + ld(mine, 11), ld(mine, 12), ld(got, 12)
    w = ld(got, 10) + ld(got, 11)
    here = jnp.where(bottom, warp[0], warp[planes - 1])
    step = jnp.where(bottom, x0 - x1, x1 - x0)
    near = here - v * step
    far = (ld(got, 8) + ld(got, 9)) - w * step
    low, high = faces()
    scale = jnp.where(bottom, low, high)
    planes_got = [ld(got, n) * scale for n in range(8)]
    up = [near, far * scale] + planes_got
    down = planes_got + [far * scale, near]
    for n in range(10):
        put(n, jnp.where(bottom, down[n], up[n]).astype(bf16))


def widen_even_kernel(planes, warp, mine, got, out):
    for z in range(1, planes - 1):
        out[z - 1] = warp[z].astype(bf16)

    def put(n, value):
        out[planes - 2 + n] = value
    face_planes(planes, warp, mine, got, put, jnp.logical_not(even_slab()))


def widen_odd_kernel(planes, warp, mine, got, most, own, outer):
    even = even_slab()

    def put(n, value):
        outer[n] = value
    face_planes(planes, warp, mine, got, put, even)
    for z in range(planes - 2):
        own[10 + z] = most[z]
    for n in range(10):
        a, b = outer[n], most[planes - 2 + n]
        own[n] = jnp.where(even, a, b)
        own[planes + 8 + n] = jnp.where(even, b, a)


def from_brains(x, partner, order=(1, 2, 3)):
    if lax.axis_size("brain") == 4:
        got = {k: lax.ppermute(x, "brain", [(n, n ^ k) for n in range(4)]) for k in order}
        return [got[k] for k in (1, 2, 3)]
    gathered = lax.all_gather(x, "brain")
    return [lax.dynamic_index_in_dim(gathered, partner[lax.axis_index("brain")], 0, keepdims=False)]


def shards(intensity, velocity, partner, offsets):
    planes = intensity.shape[1]
    slabs, brains = lax.axis_size("slab"), lax.axis_size("brain")
    edge = jax.ShapeDtypeStruct((EDGE, 8, 128), bf16)
    warp, first, second, meta = pl.pallas_call(
        functools.partial(advect_kernel, planes),
        out_shape=(jax.ShapeDtypeStruct((planes, 8, 128), f32), edge, edge, jax.ShapeDtypeStruct((24, 128), jnp.int32)),
        in_specs=[HBM] * 4,
        out_specs=(VM,) * 4,
        scratch_shapes=[
            pltpu.VMEM(intensity.shape, bf16),
            pltpu.VMEM(velocity.shape, f32),
            pltpu.VMEM(edge.shape, bf16),
            pltpu.VMEM(edge.shape, bf16),
            pltpu.SMEM(partner.shape, jnp.int32),
            pltpu.SMEM(offsets.shape[::-1], jnp.int32),
            pltpu.SemaphoreType.DMA((4,)),
        ],
        compiler_params=pltpu.CompilerParams(vmem_limit_bytes=8 * 2**20),
        name="advect",
    )(*[pltpu.with_memory_space_constraint(v, pltpu.HBM) for v in (intensity, velocity, partner, offsets.T)])
    odd_pairs = [(n, n + 1) for n in range(1, slabs - 1, 2)]
    even_pairs = [(n, n + 1) for n in range(0, slabs - 1, 2)]
    both_ways = lambda pairs: pairs + [(b, a) for a, b in pairs]
    from_odd = lax.ppermute(second, "slab", both_ways(odd_pairs))
    from_even = lax.ppermute(first, "slab", both_ways(even_pairs))
    small = pltpu.CompilerParams(vmem_limit_bytes=8 * 2**20)
    most = pl.pallas_call(
        functools.partial(widen_even_kernel, planes),
        out_shape=jax.ShapeDtypeStruct((planes + 8, 8, 128), bf16),
        in_specs=[VM] * 3,
        out_specs=VM,
        compiler_params=small,
        name="widen_even",
    )(warp, first, from_even)
    inners = from_brains(most, partner)
    own, outer = pl.pallas_call(
        functools.partial(widen_odd_kernel, planes),
        out_shape=(jax.ShapeDtypeStruct((planes + 18, 8, 128), bf16), jax.ShapeDtypeStruct((10, 8, 128), bf16)),
        in_specs=[VM] * 4,
        out_specs=(VM,) * 2,
        compiler_params=small,
        name="widen_odd",
    )(warp, second, from_odd, most)
    outers = from_brains(outer, partner, (3, 2, 1))
    return mate_part(planes, inners, outers, meta, own_part(planes, own), velocity[0])[None]


def solution(mesh):
    return jax.shard_map(
        shards,
        mesh=mesh,
        in_specs=(
            P(("groups", "brain"), "slab", None, None),
            P(("groups", "brain"), None, "slab", None, None),
            P("groups"),
            P("groups", None),
        ),
        out_specs=P(("groups", "brain"), None, "slab", None, None),
        check_vma=False,
    )
```

```python
import functools
import jax, jax.numpy as jnp, numpy as np
from jax import lax
from jax.experimental import pallas as pl
from jax.experimental.pallas import tpu as pltpu
from jax.sharding import PartitionSpec as P

PAIRS = tuple((i, j) for i in range(6) for j in range(i + 1, 6) if i // 2 != j // 2)
TAPS = tuple(float(v) for v in np.exp(-np.arange(-3, 4) ** 2 / 4.5) / np.exp(-np.arange(-3, 4) ** 2 / 4.5).sum())
f32, bf16 = jnp.float32, jnp.bfloat16
LOG2E = 1.4426950408889634
EDGE = 13
VOLUME = 729.0
UNROLL = 2
PITCH = 9
SPARE = 16
FLOOR = 1e-5 * VOLUME * VOLUME


def split(v):
    hi = v.astype(bf16)
    return hi, (v - hi.astype(f32)).astype(bf16)


def lanes():
    return (lax.broadcasted_iota(jnp.int32, (128, 128), 0), lax.broadcasted_iota(jnp.int32, (128, 128), 1))


def ones_where(cond):
    return jnp.where(cond, 1.0, 0.0).astype(bf16)


def halves(parts):
    return jnp.concatenate(split(jnp.concatenate(parts, axis=0)), axis=1)


def dot(a, b):
    return jnp.dot(a, b, preferred_element_type=f32)


def faces():
    slab = lax.axis_index("slab")
    one = jnp.float32(1.0)
    zero = jnp.float32(0.0)
    return jnp.where(slab > 0, one, zero), jnp.where(slab < lax.axis_size("slab") - 1, one, zero)


def row_inside(d):
    row = lax.broadcasted_iota(jnp.int32, (8, 128), 0)
    return (row + d >= 0) & (row + d < 8)


def describe(planes, xs, box3, tb, desc, low, high):
    nd = planes + 16
    ng = nd // 8

    def squares(g, carry, scale=None):
        c1, c2 = carry
        for i in range(8):
            s = g * 8 + i
            ld = lambda n, p: xs[n, pl.ds(pl.multiple_of(p * 8, 8), 8), :]
            near = [ld(0, s + 2), ld(0, s)] + [ld(j, s + 1) for j in (1, 2, 3, 4)]
            n1, n2 = [], []
            done = []
            for k, (a, b) in enumerate(PAIRS):
                d = near[a] - near[b]
                q = d * d
                if scale is not None:
                    q = q * scale
                done.append(c2[k] + q)
                n2.append(c1[k] + q)
                n1.append(q)
            put(s, done)
            c1, c2 = n1, n2
        return c1, c2

    def put(s, done):
        at = pl.ds(s * PITCH, 8)
        for k in range(12):
            tb[k, at, :] = done[k]
        while len(done) > 1:
            done = [done[n] + done[n + 1] for n in range(0, len(done) - 1, 2)] + done[len(done) // 2 * 2:]
        tb[12, at, :] = done[0]

    zero = [jnp.zeros((8, 128), f32)] * 12
    carry = squares(0, (zero, zero), low)
    carry = lax.fori_loop(1, ng - 1, squares, carry)
    c1, c2 = squares(ng - 1, carry, high)
    put(nd, c2)

    for g in range(ng):
        parts = []
        for k in (12,) + tuple(range(12)):
            t = [tb[k, pl.ds((g * 8 + 1) * PITCH + r, 8, stride=PITCH), :] for r in range(8)]
            p = [t[r] + t[r + 1] for r in range(7)]
            parts += [p[0]] + [p[r - 1] + t[r + 1] for r in range(1, 7)] + [p[6]]
        box = dot(halves(parts), box3[...])
        inv = [(-LOG2E / 27.0) / (box[r * 8:r * 8 + 8] * (1.0 / 324.0) + 0.1) for r in range(8)]
        for k in range(12):
            for r in range(8):
                n = (k + 1) * 64 + r * 8
                e = jnp.exp2(box[n:n + 8] * inv[r])
                if g == 0:
                    e = e * low
                if g == ng - 1:
                    e = e * high
                desc[k, pl.ds(g * 8 * PITCH + r, 8, stride=PITCH), :] = e


def depth_sums(planes, value, ys, q):
    nd, nf = planes + 16, planes + 8
    d = [value(t) for t in range(nd)]
    for f in range(nf):
        if f % 16 == 0:
            s2 = [d[f + t] + d[f + t + 1] for t in (0, 2, 4, 6)]
            total = ((s2[0] + s2[1]) + (s2[2] + s2[3])) + d[f + 8]
        else:
            total = (total - d[f - 1]) + d[f + 8]
        ys[q, pl.ds(f * PITCH, 8), :] = total


def row_sums(ys, q, g):
    t = [ys[q, pl.ds(g * 8 * PITCH + r, 8, stride=PITCH), :] for r in range(8)]
    lo = (t[0] + t[1]) + (t[2] + t[3])
    hi = (t[4] + t[5]) + (t[6] + t[7])
    w0 = lo + t[4]
    w1 = w0 + t[5]
    w7 = hi + t[3]
    w6 = w7 + t[2]
    return [w0, w1, w1 + t[6], lo + hi, lo + hi, w6 + t[1], w6, w7]


def own_kernel(planes, own, desc, mean, slope, grads, box3, box9, grad, xs, tb, ys):
    nx, nd, nf = planes + 18, planes + 16, planes + 8
    low, high = faces()
    i, j = lanes()
    for h in (0, 128):
        box3[h:h + 128] = ones_where(jnp.abs(i - j) <= 1)
        box9[h:h + 128] = ones_where(jnp.abs(i - j) <= 4)
        grad[h:h + 128] = jnp.where(i == j + 1, 1.0, jnp.where(i == j - 1, -1.0, 0.0)).astype(bf16)
    x = own[...]
    xs[0] = x.astype(f32)
    xs[3] = dot(x, ones_where(i == j + 1))
    xs[4] = dot(x, ones_where(i == j - 1))

    def prep(p, _):
        at = pl.ds(pl.multiple_of(p * 8, 8), 8)
        v = xs[0, at, :]
        xs[1, at, :] = jnp.where(row_inside(1), pltpu.roll(v, 7, 0), 0.0)
        xs[2, at, :] = jnp.where(row_inside(-1), pltpu.roll(v, 1, 0), 0.0)
        return 0
    lax.fori_loop(0, nx, prep, 0, unroll=6)
    describe(planes, xs, box3, tb, desc, low, high)

    def channels(k, _):
        for h in range(UNROLL):
            one_channel(UNROLL * k + h, h)
        return 0

    def one_channel(k, h):
        ld = lambda t: desc[k, pl.ds(t * PITCH, 8), :]
        depth_sums(planes, ld, ys, 2 * h)
        depth_sums(planes, lambda t: ld(t) * ld(t), ys, 2 * h + 1)
        parts, centre = [], []
        for g in range(nf // 8):
            for q in range(2):
                parts += row_sums(ys, 2 * h + q, g)
            centre += [desc[k, pl.ds((g * 8 + 4) * PITCH + r, 8, stride=PITCH), :] for r in range(8)]
        sums = dot(halves(parts), box9[...])
        across = dot(halves(centre), grad[...])
        for g in range(nf // 8):
            a = centre[g * 8:g * 8 + 8]
            for r in range(8):
                at = pl.ds(g * 64 + r * 8, 8)
                mo, so = [sums[(g * 16 + q * 8 + r) * 8:(g * 16 + q * 8 + r) * 8 + 8] for q in range(2)]
                gc = across[(g * 8 + r) * 8:(g * 8 + r) * 8 + 8]
                inv = lax.rsqrt(VOLUME * so - mo * mo + FLOOR)
                gz = desc[k, pl.ds((g * 8 + 5) * PITCH + r, 8, stride=PITCH), :] - desc[k, pl.ds((g * 8 + 3) * PITCH + r, 8, stride=PITCH), :]
                gr = a[1] if r == 0 else -a[6] if r == 7 else a[r + 1] - a[r - 1]
                mean[k, at, :] = mo
                slope[k, at, :] = (inv * inv) * (VOLUME * a[r] - mo)
                for c, gg in enumerate((gz, gr, gc)):
                    grads[c, k, at, :] = gg * inv
    lax.fori_loop(0, 12 // UNROLL, channels, 0)


def mate_kernel(planes, count, *refs):
    inner, outer = refs[:count][::-1], refs[count:2 * count]
    meta, adesc, mean, slope, grads, vel, out, box3, box9, smooth, xs, raw, tb, desc, ys, frc = refs[2 * count:]
    nx, nd, nf = planes + 18, planes + 16, planes + 8
    low, high = faces()
    which, dc = meta[0:1, :], meta[16:17, :]
    dr = jnp.max(meta[8:16, :])
    i, j = lanes()
    weights = jnp.zeros((128, 128), f32)
    for d in range(4):
        weights = jnp.where(jnp.abs(i - j) == d, TAPS[3 + d], weights)
    whi, wlo = split(weights)
    for h in (0, 128):
        box3[h:h + 128] = ones_where(jnp.abs(i - j) <= 1)
        box9[h:h + 128] = ones_where(jnp.abs(i - j) <= 4)
        smooth[h:h + 128] = whi
    smooth[256:384] = wlo
    row = lax.broadcasted_iota(jnp.int32, (8, 128), 0)

    x, y = inner[0][...], outer[0][...]
    for n in range(1, count):
        x = jnp.where(which == n + 1, inner[n][...], x)
        y = jnp.where(which == n + 1, outer[n][...], y)
    x = jnp.concatenate([y[0:80], x, y[80:160]], axis=0)
    for n, d in ((0, 0), (1, 1), (2, -1)):
        take = ones_where((i == j + d + dc) & (j + d >= 0) & (j + d < 128))
        raw[n, pl.ds(8, nx * 8), :] = dot(x, take)

    def prep(p, _):
        at = pl.multiple_of(p * 8, 8)
        for n, b, d in ((0, 0, 0), (1, 0, 1), (2, 0, -1), (3, 1, 0), (4, 2, 0)):
            v = raw[b, pl.ds(at + 8 + dr + d, 8), :]
            xs[n, pl.ds(at, 8), :] = jnp.where(row_inside(d) & row_inside(d + dr), v, 0.0)
        return 0
    lax.fori_loop(0, nx, prep, 0, unroll=6)
    describe(planes, xs, box3, tb, desc, low, high)

    def channels(step, _):
        ks = [UNROLL * step + h for h in range(UNROLL)]
        sums = []
        for h, k in enumerate(ks):
            lda = lambda t: adesc[k, pl.ds(t * PITCH, 8), :]
            ldb = lambda t: desc[k, pl.ds(t * PITCH, 8), :]
            depth_sums(planes, ldb, ys, 3 * h)
            depth_sums(planes, lambda t: ldb(t) * ldb(t), ys, 3 * h + 1)
            depth_sums(planes, lambda t: lda(t) * ldb(t), ys, 3 * h + 2)
            parts = []
            for g in range(nf // 8):
                for q in range(3):
                    parts += row_sums(ys, 3 * h + q, g)
            sums.append(dot(halves(parts), box9[...]))
        for g in range(nf // 8):
            for r in range(8):
                at = pl.ds(g * 64 + r * 8, 8)
                acc = [frc[c, at, :] for c in range(3)]
                for h, k in enumerate(ks):
                    mm, sm, sc = [sums[h][(g * 24 + q * 8 + r) * 8:(g * 24 + q * 8 + r) * 8 + 8] for q in range(3)]
                    b = desc[k, pl.ds((g * 8 + 4) * PITCH + r, 8, stride=PITCH), :]
                    inv = lax.rsqrt(VOLUME * sm - mm * mm + FLOOR)
                    cov = VOLUME * sc - mean[k, at, :] * mm
                    coef = (VOLUME * b - mm - cov * slope[k, at, :]) * inv
                    acc = [acc[c] + coef * grads[c, k, at, :] for c in range(3)]
                for c in range(3):
                    frc[c, at, :] = acc[c]
        return 0
    frc[...] = jnp.zeros_like(frc)
    lax.fori_loop(0, 12 // UNROLL, channels, 0)

    parts = []
    for c in range(3):
        for g in range(nf // 8):
            for r in range(8):
                v = frc[c, pl.ds(g * 64 + r * 8, 8), :]
                if g == 0:
                    v = jnp.where(row >= 4, v, v * low)
                if g == nf // 8 - 1:
                    v = jnp.where(row < 4, v, v * high)
                ys[0, pl.ds(g * 8 * PITCH + r, 8, stride=PITCH), :] = v
        for o in range(planes):
            p = [ys[0, pl.ds((o + 1 + n) * PITCH, 8), :] for n in range(7)]
            v = TAPS[3] * p[3]
            for n in range(3):
                v = v + TAPS[n] * (p[n] + p[6 - n])
            ys[1, pl.ds(o * PITCH, 8), :] = v
        for g in range(planes // 8):
            t = [ys[1, pl.ds(g * 8 * PITCH + r, 8, stride=PITCH), :] for r in range(8)]
            for r in range(8):
                v = TAPS[3] * t[r]
                for n in range(1, 4):
                    s = [t[q] for q in (r - n, r + n) if 0 <= q < 8]
                    v = v + TAPS[3 + n] * (s[0] + s[1] if len(s) == 2 else s[0])
                parts.append(v)
    both = halves(parts)
    res = dot(both, smooth[0:256]) + dot(both[:, 0:128], smooth[256:384])
    for c in range(3):
        for g in range(planes // 8):
            for r in range(8):
                n = ((c * planes + g * 8) + r) * 8
                ys[0, pl.ds(g * 8 * PITCH + r, 8, stride=PITCH), :] = res[n:n + 8]
        for o in range(planes):
            out[c, o] = vel[c, o] + (8.0 * VOLUME / 24.0) * ys[0, pl.ds(o * PITCH, 8), :]


VM = pl.BlockSpec(memory_space=pltpu.VMEM)
HBM = pl.BlockSpec(memory_space=pltpu.HBM)


def own_part(planes, own):
    nx, nd, nf = planes + 18, planes + 16, planes + 8
    shape = jax.ShapeDtypeStruct
    return pl.pallas_call(
        functools.partial(own_kernel, planes),
        out_shape=(
            shape((12, nd * PITCH + SPARE, 128), f32),
            shape((12, nf * 8, 128), f32),
            shape((12, nf * 8, 128), f32),
            shape((3, 12, nf * 8, 128), f32),
        ),
        in_specs=[VM],
        out_specs=(VM,) * 4,
        scratch_shapes=[
            pltpu.VMEM((256, 128), bf16),
            pltpu.VMEM((256, 128), bf16),
            pltpu.VMEM((256, 128), bf16),
            pltpu.VMEM((5, nx * 8, 128), f32),
            pltpu.VMEM((13, (nd + 1) * PITCH + SPARE, 128), f32),
            pltpu.VMEM((2 * UNROLL, nf * PITCH + SPARE, 128), f32),
        ],
        compiler_params=pltpu.CompilerParams(vmem_limit_bytes=16 * 2**20),
        cost_estimate=pl.CostEstimate(flops=6 * 10**8, bytes_accessed=16 * 2**20, transcendentals=10**6),
        name="own",
    )(own.reshape(-1, 128))


def mate_part(planes, inner, outer, meta, owned, vel):
    nx, nd, nf = planes + 18, planes + 16, planes + 8
    count = len(inner)
    return pl.pallas_call(
        functools.partial(mate_kernel, planes, count),
        out_shape=jax.ShapeDtypeStruct(vel.shape, f32),
        in_specs=[VM] * (2 * count + 6),
        out_specs=VM,
        scratch_shapes=[
            pltpu.VMEM((256, 128), bf16),
            pltpu.VMEM((256, 128), bf16),
            pltpu.VMEM((384, 128), bf16),
            pltpu.VMEM((5, nx * 8, 128), f32),
            pltpu.VMEM((3, nx * 8 + 16, 128), f32),
            pltpu.VMEM((13, (nd + 1) * PITCH + SPARE, 128), f32),
            pltpu.VMEM((12, nd * PITCH + SPARE, 128), f32),
            pltpu.VMEM((3 * UNROLL, nf * PITCH + SPARE, 128), f32),
            pltpu.VMEM((3, nf * 8, 128), f32),
        ],
        compiler_params=pltpu.CompilerParams(vmem_limit_bytes=16 * 2**20),
        name="mate",
    )(*[m.reshape(-1, 128) for m in inner[::-1] + outer], meta, *owned, vel)


def advect_kernel(planes, image_hbm, vel_hbm, partner_hbm, offsets_hbm, warp, inner, first, second, meta, image, vel, down, up, partner, offsets, sems):
    copies = [
        pltpu.make_async_copy(vel_hbm, vel, sems.at[0]),
        pltpu.make_async_copy(image_hbm, image, sems.at[1]),
        pltpu.make_async_copy(partner_hbm, partner, sems.at[2]),
        pltpu.make_async_copy(offsets_hbm, offsets, sems.at[3]),
    ]
    for copy in copies:
        copy.start()
    for copy in copies:
        copy.wait()
    lane = lax.broadcasted_iota(jnp.int32, (8, 128), 1)

    for z in range(planes):
        x = image[0, z].astype(f32)
        before = image[0, z - 1].astype(f32) if z > 0 else x
        after = image[0, z + 1].astype(f32) if z < planes - 1 else x
        sides = (
            (before, after),
            (jnp.where(row_inside(-1), pltpu.roll(x, 1, 0), 0.0), jnp.where(row_inside(1), pltpu.roll(x, 7, 0), 0.0)),
            (jnp.where(lane >= 1, pltpu.roll(x, 1, 1), 0.0), jnp.where(lane < 127, pltpu.roll(x, 127, 1), 0.0)),
        )
        moved = 0.0
        for c, (lo, hi) in enumerate(sides):
            v = vel[0, c, z]
            moved = moved + (jnp.maximum(v, 0.0) * (x - lo) + jnp.minimum(v, 0.0) * (hi - x))
        y = x - moved
        warp[z] = y
        if z == 0 or z == planes - 1:
            v = jnp.maximum(vel[0, 0, z], 0.0) if z == 0 else jnp.minimum(vel[0, 0, z], 0.0)
            edge = split(y) + split(v) + (image[0, z],)
            for n, part in enumerate(edge):
                (down if z == 0 else up)[8 + n] = part
        else:
            inner[z - 1] = y.astype(bf16)
        if 1 <= z <= 8:
            down[z - 1] = y.astype(bf16)
        if planes - 9 <= z < planes - 1:
            up[z - (planes - 9)] = y.astype(bf16)
    me = lax.axis_index("brain")
    mate = partner[me]
    for n, value in enumerate((me ^ mate, offsets[0, mate] - offsets[0, me], offsets[1, mate] - offsets[1, me])):
        meta[n * 8:n * 8 + 8, :] = jnp.full((8, 128), value, jnp.int32)
    even = lax.rem(lax.axis_index("slab"), 2) == 0
    for n in range(EDGE):
        first[n] = jnp.where(even, up[n], down[n])
        second[n] = jnp.where(even, down[n], up[n])


def widen_kernel(planes, warp, sent1, sent2, got1, got2, out, outer):
    low, high = faces()
    even = lax.rem(lax.axis_index("slab"), 2) == 0
    down, up, below, above = (sent2, sent1), (sent1, sent2), (got2, got1), (got1, got2)
    ld = lambda pair, n: jnp.where(even, pair[0][n], pair[1][n]).astype(f32)
    top = planes - 1
    first, last = ld(down, 12), ld(up, 12)
    for n in range(8):
        out[n] = (ld(below, n) * low).astype(bf16)
        out[planes + 10 + n] = (ld(above, n) * high).astype(bf16)
    out[8] = (low * ((ld(below, 8) + ld(below, 9)) - (ld(below, 10) + ld(below, 11)) * (first - ld(below, 12)))).astype(bf16)
    out[planes + 9] = (high * ((ld(above, 8) + ld(above, 9)) - (ld(above, 10) + ld(above, 11)) * (ld(above, 12) - last))).astype(bf16)
    for z in range(1, top):
        out[9 + z] = warp[z].astype(bf16)
    out[9] = (warp[0] - (ld(down, 10) + ld(down, 11)) * (first - ld(below, 12))).astype(bf16)
    out[9 + top] = (warp[top] - (ld(up, 10) + ld(up, 11)) * (ld(above, 12) - last)).astype(bf16)

    for n in range(10):
        outer[n] = out[n]
        outer[10 + n] = out[planes + 8 + n]


def from_brains(x, partner):
    if lax.axis_size("brain") == 4:
        return [lax.ppermute(x, "brain", [(n, n ^ k) for n in range(4)]) for k in (1, 2, 3)]
    gathered = lax.all_gather(x, "brain")
    return [lax.dynamic_index_in_dim(gathered, partner[lax.axis_index("brain")], 0, keepdims=False)]


def shards(intensity, velocity, partner, offsets):
    planes = intensity.shape[1]
    slabs, brains = lax.axis_size("slab"), lax.axis_size("brain")
    edge = jax.ShapeDtypeStruct((EDGE, 8, 128), bf16)
    warp, inner, first, second, meta = pl.pallas_call(
        functools.partial(advect_kernel, planes),
        out_shape=(jax.ShapeDtypeStruct((planes, 8, 128), f32), jax.ShapeDtypeStruct((planes - 2, 8, 128), bf16), edge, edge, jax.ShapeDtypeStruct((24, 128), jnp.int32)),
        in_specs=[HBM] * 4,
        out_specs=(VM,) * 5,
        scratch_shapes=[
            pltpu.VMEM(intensity.shape, bf16),
            pltpu.VMEM(velocity.shape, f32),
            pltpu.VMEM(edge.shape, bf16),
            pltpu.VMEM(edge.shape, bf16),
            pltpu.SMEM(partner.shape, jnp.int32),
            pltpu.SMEM(offsets.shape[::-1], jnp.int32),
            pltpu.SemaphoreType.DMA((4,)),
        ],
        compiler_params=pltpu.CompilerParams(vmem_limit_bytes=8 * 2**20),
        name="advect",
    )(*[pltpu.with_memory_space_constraint(v, pltpu.HBM) for v in (intensity, velocity, partner, offsets.T)])
    odd_pairs = [(n, n + 1) for n in range(1, slabs - 1, 2)]
    even_pairs = [(n, n + 1) for n in range(0, slabs - 1, 2)]
    both_ways = lambda pairs: pairs + [(b, a) for a, b in pairs]
    from_odd = lax.ppermute(second, "slab", both_ways(odd_pairs))
    from_even = lax.ppermute(first, "slab", both_ways(even_pairs))
    inners = from_brains(inner, partner)
    own, outer = pl.pallas_call(
        functools.partial(widen_kernel, planes),
        out_shape=(jax.ShapeDtypeStruct((planes + 18, 8, 128), bf16), jax.ShapeDtypeStruct((20, 8, 128), bf16)),
        in_specs=[VM] * 5,
        out_specs=(VM,) * 2,
        compiler_params=pltpu.CompilerParams(vmem_limit_bytes=8 * 2**20),
        name="widen",
    )(warp, first, second, from_even, from_odd)
    outers = from_brains(outer, partner)
    return mate_part(planes, inners, outers, meta, own_part(planes, own), velocity[0])[None]


def solution(mesh):
    return jax.shard_map(
        shards,
        mesh=mesh,
        in_specs=(
            P(("groups", "brain"), "slab", None, None),
            P(("groups", "brain"), None, "slab", None, None),
            P("groups"),
            P("groups", None),
        ),
        out_specs=P(("groups", "brain"), None, "slab", None, None),
        check_vma=False,
    )
```

```python
import functools
import jax, jax.numpy as jnp, numpy as np
from jax import lax
from jax.experimental import pallas as pl
from jax.experimental.pallas import tpu as pltpu
from jax.sharding import PartitionSpec as P

PAIRS = tuple((i, j) for i in range(6) for j in range(i + 1, 6) if i // 2 != j // 2)
TAPS = tuple(float(v) for v in np.exp(-np.arange(-3, 4) ** 2 / 4.5) / np.exp(-np.arange(-3, 4) ** 2 / 4.5).sum())
f32, bf16 = jnp.float32, jnp.bfloat16
LOG2E = 1.4426950408889634
EDGE = 13
VOLUME = 729.0
UNROLL = 2
PITCH = 9
SPARE = 16
FLOOR = 1e-5 * VOLUME * VOLUME


def split(v):
    hi = v.astype(bf16)
    return hi, (v - hi.astype(f32)).astype(bf16)


def lanes():
    return (lax.broadcasted_iota(jnp.int32, (128, 128), 0), lax.broadcasted_iota(jnp.int32, (128, 128), 1))


def ones_where(cond):
    return jnp.where(cond, 1.0, 0.0).astype(bf16)


def halves(parts):
    return jnp.concatenate(split(jnp.concatenate(parts, axis=0)), axis=1)


def dot(a, b):
    return jnp.dot(a, b, preferred_element_type=f32)


def faces():
    slab = lax.axis_index("slab")
    one = jnp.float32(1.0)
    zero = jnp.float32(0.0)
    return jnp.where(slab > 0, one, zero), jnp.where(slab < lax.axis_size("slab") - 1, one, zero)


def row_inside(d):
    row = lax.broadcasted_iota(jnp.int32, (8, 128), 0)
    return (row + d >= 0) & (row + d < 8)


def describe(planes, xs, box3, tb, desc, low, high):
    nd = planes + 16
    ng = nd // 8

    def squares(g, carry, scale=None):
        c1, c2 = carry
        for i in range(8):
            s = g * 8 + i
            ld = lambda n, p: xs[n, pl.ds(pl.multiple_of(p * 8, 8), 8), :]
            near = [ld(0, s + 2), ld(0, s)] + [ld(j, s + 1) for j in (1, 2, 3, 4)]
            n1, n2 = [], []
            done = []
            for k, (a, b) in enumerate(PAIRS):
                d = near[a] - near[b]
                q = d * d
                if scale is not None:
                    q = q * scale
                done.append(c2[k] + q)
                n2.append(c1[k] + q)
                n1.append(q)
            put(s, done)
            c1, c2 = n1, n2
        return c1, c2

    def put(s, done):
        at = pl.ds(s * PITCH, 8)
        for k in range(12):
            tb[k, at, :] = done[k]
        while len(done) > 1:
            done = [done[n] + done[n + 1] for n in range(0, len(done) - 1, 2)] + done[len(done) // 2 * 2:]
        tb[12, at, :] = done[0]

    zero = [jnp.zeros((8, 128), f32)] * 12
    carry = squares(0, (zero, zero), low)
    carry = lax.fori_loop(1, ng - 1, squares, carry)
    c1, c2 = squares(ng - 1, carry, high)
    put(nd, c2)

    for g in range(ng):
        parts = []
        for k in (12,) + tuple(range(12)):
            t = [tb[k, pl.ds((g * 8 + 1) * PITCH + r, 8, stride=PITCH), :] for r in range(8)]
            p = [t[r] + t[r + 1] for r in range(7)]
            parts += [p[0]] + [p[r - 1] + t[r + 1] for r in range(1, 7)] + [p[6]]
        box = dot(halves(parts), box3[...])
        inv = [(-LOG2E / 27.0) / (box[r * 8:r * 8 + 8] * (1.0 / 324.0) + 0.1) for r in range(8)]
        for k in range(12):
            for r in range(8):
                n = (k + 1) * 64 + r * 8
                e = jnp.exp2(box[n:n + 8] * inv[r])
                if g == 0:
                    e = e * low
                if g == ng - 1:
                    e = e * high
                desc[k, pl.ds(g * 8 * PITCH + r, 8, stride=PITCH), :] = e


def depth_sums(planes, value, ys, q):
    nd, nf = planes + 16, planes + 8
    d = [value(t) for t in range(nd)]
    for f in range(nf):
        if f % 16 == 0:
            s2 = [d[f + t] + d[f + t + 1] for t in (0, 2, 4, 6)]
            total = ((s2[0] + s2[1]) + (s2[2] + s2[3])) + d[f + 8]
        else:
            total = (total - d[f - 1]) + d[f + 8]
        ys[q, pl.ds(f * PITCH, 8), :] = total


def row_sums(ys, q, g):
    t = [ys[q, pl.ds(g * 8 * PITCH + r, 8, stride=PITCH), :] for r in range(8)]
    lo = (t[0] + t[1]) + (t[2] + t[3])
    hi = (t[4] + t[5]) + (t[6] + t[7])
    w0 = lo + t[4]
    w1 = w0 + t[5]
    w7 = hi + t[3]
    w6 = w7 + t[2]
    return [w0, w1, w1 + t[6], lo + hi, lo + hi, w6 + t[1], w6, w7]


def own_kernel(planes, own, box3, box9, grad, step, desc, mean, slope, grads, xs, tb, ys):
    nx, nd, nf = planes + 18, planes + 16, planes + 8
    low, high = faces()
    x = own[...]
    xs[0] = x.astype(f32)
    xs[3] = dot(x, step[0])
    xs[4] = dot(x, step[1])

    def prep(p, _):
        at = pl.ds(pl.multiple_of(p * 8, 8), 8)
        v = xs[0, at, :]
        xs[1, at, :] = jnp.where(row_inside(1), pltpu.roll(v, 7, 0), 0.0)
        xs[2, at, :] = jnp.where(row_inside(-1), pltpu.roll(v, 1, 0), 0.0)
        return 0
    lax.fori_loop(0, nx, prep, 0, unroll=6)
    describe(planes, xs, box3, tb, desc, low, high)

    def channels(k, _):
        for h in range(UNROLL):
            one_channel(UNROLL * k + h, h)
        return 0

    def one_channel(k, h):
        ld = lambda t: desc[k, pl.ds(t * PITCH, 8), :]
        depth_sums(planes, ld, ys, 2 * h)
        depth_sums(planes, lambda t: ld(t) * ld(t), ys, 2 * h + 1)
        parts, centre = [], []
        for g in range(nf // 8):
            for q in range(2):
                parts += row_sums(ys, 2 * h + q, g)
            centre += [desc[k, pl.ds((g * 8 + 4) * PITCH + r, 8, stride=PITCH), :] for r in range(8)]
        sums = dot(halves(parts), box9[...])
        across = dot(halves(centre), grad[...])
        for g in range(nf // 8):
            a = centre[g * 8:g * 8 + 8]
            for r in range(8):
                at = pl.ds(g * 64 + r * 8, 8)
                mo, so = [sums[(g * 16 + q * 8 + r) * 8:(g * 16 + q * 8 + r) * 8 + 8] for q in range(2)]
                gc = across[(g * 8 + r) * 8:(g * 8 + r) * 8 + 8]
                inv = lax.rsqrt(VOLUME * so - mo * mo + FLOOR)
                gz = desc[k, pl.ds((g * 8 + 5) * PITCH + r, 8, stride=PITCH), :] - desc[k, pl.ds((g * 8 + 3) * PITCH + r, 8, stride=PITCH), :]
                gr = a[1] if r == 0 else -a[6] if r == 7 else a[r + 1] - a[r - 1]
                mean[k, at, :] = mo
                slope[k, at, :] = (inv * inv) * (VOLUME * a[r] - mo)
                for c, gg in enumerate((gz, gr, gc)):
                    grads[c, k, at, :] = gg * inv
    lax.fori_loop(0, 12 // UNROLL, channels, 0)


def tables_kernel(meta, box3, box9, grad, step, smooth, take):
    i, j = lanes()
    weights = jnp.zeros((128, 128), f32)
    for d in range(4):
        weights = jnp.where(jnp.abs(i - j) == d, TAPS[3 + d], weights)
    whi, wlo = split(weights)
    for h in (0, 128):
        grad[h:h + 128] = jnp.where(i == j + 1, 1.0, jnp.where(i == j - 1, -1.0, 0.0)).astype(bf16)
        box3[h:h + 128] = ones_where(jnp.abs(i - j) <= 1)
        box9[h:h + 128] = ones_where(jnp.abs(i - j) <= 4)
        smooth[h:h + 128] = whi
    smooth[256:384] = wlo
    step[0] = ones_where(i == j + 1)
    step[1] = ones_where(i == j - 1)
    dc = meta[16:17, :]
    for n, d in ((0, 0), (1, 1), (2, -1)):
        take[n] = ones_where((i == j + d + dc) & (j + d >= 0) & (j + d < 128))


def mate_kernel(planes, count, *refs):
    inner, outer = refs[:count][::-1], refs[count:2 * count]
    meta, box3, box9, smooth, take, adesc, mean, slope, grads, vel, out, xs, raw, tb, desc, ys, frc, result, sems = refs[2 * count:]
    nx, nd, nf = planes + 18, planes + 16, planes + 8
    low, high = faces()
    which = meta[0:1, :]
    dr = jnp.max(meta[8:16, :])
    row = lax.broadcasted_iota(jnp.int32, (8, 128), 0)

    x, y = inner[0][...], outer[0][...]
    for n in range(1, count):
        x = jnp.where(which == n + 1, inner[n][...], x)
        y = jnp.where(which == n + 1, outer[n][...], y)
    x = jnp.concatenate([y[0:80], x, y[80:160]], axis=0)
    for n in range(3):
        raw[n, pl.ds(8, nx * 8), :] = dot(x, take[n])

    def prep(p, _):
        at = pl.multiple_of(p * 8, 8)
        for n, b, d in ((0, 0, 0), (1, 0, 1), (2, 0, -1), (3, 1, 0), (4, 2, 0)):
            v = raw[b, pl.ds(at + 8 + dr + d, 8), :]
            xs[n, pl.ds(at, 8), :] = jnp.where(row_inside(d) & row_inside(d + dr), v, 0.0)
        return 0
    lax.fori_loop(0, nx, prep, 0, unroll=6)
    describe(planes, xs, box3, tb, desc, low, high)

    def channels(step, _):
        ks = [UNROLL * step + h for h in range(UNROLL)]
        sums = []
        for h, k in enumerate(ks):
            lda = lambda t: adesc[k, pl.ds(t * PITCH, 8), :]
            ldb = lambda t: desc[k, pl.ds(t * PITCH, 8), :]
            depth_sums(planes, ldb, ys, 3 * h)
            depth_sums(planes, lambda t: ldb(t) * ldb(t), ys, 3 * h + 1)
            depth_sums(planes, lambda t: lda(t) * ldb(t), ys, 3 * h + 2)
            parts = []
            for g in range(nf // 8):
                for q in range(3):
                    parts += row_sums(ys, 3 * h + q, g)
            sums.append(dot(halves(parts), box9[...]))
        for g in range(nf // 8):
            for r in range(8):
                at = pl.ds(g * 64 + r * 8, 8)
                acc = [frc[c, at, :] for c in range(3)]
                for h, k in enumerate(ks):
                    mm, sm, sc = [sums[h][(g * 24 + q * 8 + r) * 8:(g * 24 + q * 8 + r) * 8 + 8] for q in range(3)]
                    b = desc[k, pl.ds((g * 8 + 4) * PITCH + r, 8, stride=PITCH), :]
                    inv = lax.rsqrt(VOLUME * sm - mm * mm + FLOOR)
                    cov = VOLUME * sc - mean[k, at, :] * mm
                    coef = (VOLUME * b - mm - cov * slope[k, at, :]) * inv
                    acc = [acc[c] + coef * grads[c, k, at, :] for c in range(3)]
                for c in range(3):
                    frc[c, at, :] = acc[c]
        return 0
    frc[...] = jnp.zeros_like(frc)
    lax.fori_loop(0, 12 // UNROLL, channels, 0)

    parts = []
    for c in range(3):
        for g in range(nf // 8):
            for r in range(8):
                v = frc[c, pl.ds(g * 64 + r * 8, 8), :]
                if g == 0:
                    v = jnp.where(row >= 4, v, v * low)
                if g == nf // 8 - 1:
                    v = jnp.where(row < 4, v, v * high)
                ys[0, pl.ds(g * 8 * PITCH + r, 8, stride=PITCH), :] = v
        for o in range(planes):
            p = [ys[0, pl.ds((o + 1 + n) * PITCH, 8), :] for n in range(7)]
            v = TAPS[3] * p[3]
            for n in range(3):
                v = v + TAPS[n] * (p[n] + p[6 - n])
            ys[1, pl.ds(o * PITCH, 8), :] = v
        for g in range(planes // 8):
            t = [ys[1, pl.ds(g * 8 * PITCH + r, 8, stride=PITCH), :] for r in range(8)]
            for r in range(8):
                v = TAPS[3] * t[r]
                for n in range(1, 4):
                    s = [t[q] for q in (r - n, r + n) if 0 <= q < 8]
                    v = v + TAPS[3 + n] * (s[0] + s[1] if len(s) == 2 else s[0])
                parts.append(v)
    both = halves(parts)
    res = dot(both, smooth[0:256]) + dot(both[:, 0:128], smooth[256:384])
    copies = []
    for c in range(3):
        for g in range(planes // 8):
            for r in range(8):
                n = ((c * planes + g * 8) + r) * 8
                ys[0, pl.ds(g * 8 * PITCH + r, 8, stride=PITCH), :] = res[n:n + 8]
        for o in range(planes):
            result[c, o] = vel[0, c, o] + (8.0 * VOLUME / 24.0) * ys[0, pl.ds(o * PITCH, 8), :]
        copies.append(pltpu.make_async_copy(result.at[c], out.at[c], sems.at[c]))
        copies[c].start()
    for copy in copies:
        copy.wait()


VM = pl.BlockSpec(memory_space=pltpu.VMEM)
HBM = pl.BlockSpec(memory_space=pltpu.HBM)


def own_part(planes, own, tables):
    nx, nd, nf = planes + 18, planes + 16, planes + 8
    shape = jax.ShapeDtypeStruct
    return pl.pallas_call(
        functools.partial(own_kernel, planes),
        out_shape=(
            shape((12, nd * PITCH + SPARE, 128), f32),
            shape((12, nf * 8, 128), f32),
            shape((12, nf * 8, 128), f32),
            shape((3, 12, nf * 8, 128), f32),
        ),
        in_specs=[VM] * 5,
        out_specs=(VM,) * 4,
        scratch_shapes=[
            pltpu.VMEM((5, nx * 8, 128), f32),
            pltpu.VMEM((13, (nd + 1) * PITCH + SPARE, 128), f32),
            pltpu.VMEM((2 * UNROLL, nf * PITCH + SPARE, 128), f32),
        ],
        compiler_params=pltpu.CompilerParams(vmem_limit_bytes=16 * 2**20),
        cost_estimate=pl.CostEstimate(flops=6 * 10**8, bytes_accessed=16 * 2**20, transcendentals=10**6),
        name="own",
    )(own.reshape(-1, 128), *tables[:4])


def mate_part(planes, inner, outer, meta, tables, owned, vel):
    nx, nd, nf = planes + 18, planes + 16, planes + 8
    count = len(inner)
    return pl.pallas_call(
        functools.partial(mate_kernel, planes, count),
        out_shape=jax.ShapeDtypeStruct(vel.shape[1:], f32),
        in_specs=[VM] * (2 * count + 10),
        out_specs=HBM,
        scratch_shapes=[
            pltpu.VMEM((5, nx * 8, 128), f32),
            pltpu.VMEM((3, nx * 8 + 16, 128), f32),
            pltpu.VMEM((13, (nd + 1) * PITCH + SPARE, 128), f32),
            pltpu.VMEM((12, nd * PITCH + SPARE, 128), f32),
            pltpu.VMEM((3 * UNROLL, nf * PITCH + SPARE, 128), f32),
            pltpu.VMEM((3, nf * 8, 128), f32),
            pltpu.VMEM(vel.shape[1:], f32),
            pltpu.SemaphoreType.DMA((3,)),
        ],
        compiler_params=pltpu.CompilerParams(vmem_limit_bytes=16 * 2**20),
        name="mate",
    )(*[m.reshape(-1, 128) for m in inner[::-1] + outer], meta, tables[0], tables[1], *tables[4:], *owned, vel)


def advect_kernel(planes, image_hbm, vel_hbm, partner_hbm, offsets_hbm, warp, inner, first, second, meta, vel, image, down, up, partner, offsets, sems):
    copies = [
        pltpu.make_async_copy(vel_hbm, vel, sems.at[0]),
        pltpu.make_async_copy(image_hbm, image, sems.at[1]),
        pltpu.make_async_copy(partner_hbm, partner, sems.at[2]),
        pltpu.make_async_copy(offsets_hbm, offsets, sems.at[3]),
    ]
    for copy in copies:
        copy.start()
    for copy in copies:
        copy.wait()
    lane = lax.broadcasted_iota(jnp.int32, (8, 128), 1)

    for z in range(planes):
        x = image[0, z].astype(f32)
        before = image[0, z - 1].astype(f32) if z > 0 else x
        after = image[0, z + 1].astype(f32) if z < planes - 1 else x
        sides = (
            (before, after),
            (jnp.where(row_inside(-1), pltpu.roll(x, 1, 0), 0.0), jnp.where(row_inside(1), pltpu.roll(x, 7, 0), 0.0)),
            (jnp.where(lane >= 1, pltpu.roll(x, 1, 1), 0.0), jnp.where(lane < 127, pltpu.roll(x, 127, 1), 0.0)),
        )
        moved = 0.0
        for c, (lo, hi) in enumerate(sides):
            v = vel[0, c, z]
            moved = moved + (jnp.maximum(v, 0.0) * (x - lo) + jnp.minimum(v, 0.0) * (hi - x))
        y = x - moved
        warp[z] = y
        if z == 0 or z == planes - 1:
            v = jnp.maximum(vel[0, 0, z], 0.0) if z == 0 else jnp.minimum(vel[0, 0, z], 0.0)
            edge = split(y) + split(v) + (image[0, z],)
            for n, part in enumerate(edge):
                (down if z == 0 else up)[8 + n] = part
        else:
            inner[z - 1] = y.astype(bf16)
        if 1 <= z <= 8:
            down[z - 1] = y.astype(bf16)
        if planes - 9 <= z < planes - 1:
            up[z - (planes - 9)] = y.astype(bf16)
    me = lax.axis_index("brain")
    mate = partner[me]
    for n, value in enumerate((me ^ mate, offsets[0, mate] - offsets[0, me], offsets[1, mate] - offsets[1, me])):
        meta[n * 8:n * 8 + 8, :] = jnp.full((8, 128), value, jnp.int32)
    even = lax.rem(lax.axis_index("slab"), 2) == 0
    for n in range(EDGE):
        first[n] = jnp.where(even, up[n], down[n])
        second[n] = jnp.where(even, down[n], up[n])


def widen_kernel(planes, warp, sent1, sent2, got1, got2, out, outer):
    low, high = faces()
    even = lax.rem(lax.axis_index("slab"), 2) == 0
    down, up, below, above = (sent2, sent1), (sent1, sent2), (got2, got1), (got1, got2)
    ld = lambda pair, n: jnp.where(even, pair[0][n], pair[1][n]).astype(f32)
    top = planes - 1
    first, last = ld(down, 12), ld(up, 12)
    for n in range(8):
        out[n] = (ld(below, n) * low).astype(bf16)
        out[planes + 10 + n] = (ld(above, n) * high).astype(bf16)
    out[8] = (low * ((ld(below, 8) + ld(below, 9)) - (ld(below, 10) + ld(below, 11)) * (first - ld(below, 12)))).astype(bf16)
    out[planes + 9] = (high * ((ld(above, 8) + ld(above, 9)) - (ld(above, 10) + ld(above, 11)) * (ld(above, 12) - last))).astype(bf16)
    for z in range(1, top):
        out[9 + z] = warp[z].astype(bf16)
    out[9] = (warp[0] - (ld(down, 10) + ld(down, 11)) * (first - ld(below, 12))).astype(bf16)
    out[9 + top] = (warp[top] - (ld(up, 10) + ld(up, 11)) * (ld(above, 12) - last)).astype(bf16)

    for n in range(10):
        outer[n] = out[n]
        outer[10 + n] = out[planes + 8 + n]


def from_brains(x, partner):
    if lax.axis_size("brain") == 4:
        return [lax.ppermute(x, "brain", [(n, n ^ k) for n in range(4)]) for k in (1, 2, 3)]
    gathered = lax.all_gather(x, "brain")
    return [lax.dynamic_index_in_dim(gathered, partner[lax.axis_index("brain")], 0, keepdims=False)]


def shards(intensity, velocity, partner, offsets):
    planes = intensity.shape[1]
    slabs, brains = lax.axis_size("slab"), lax.axis_size("brain")
    edge = jax.ShapeDtypeStruct((EDGE, 8, 128), bf16)
    warp, inner, first, second, meta, vel = pl.pallas_call(
        functools.partial(advect_kernel, planes),
        out_shape=(jax.ShapeDtypeStruct((planes, 8, 128), f32), jax.ShapeDtypeStruct((planes - 2, 8, 128), bf16), edge, edge, jax.ShapeDtypeStruct((24, 128), jnp.int32), jax.ShapeDtypeStruct(velocity.shape, f32)),
        in_specs=[HBM] * 4,
        out_specs=(VM,) * 6,
        scratch_shapes=[
            pltpu.VMEM(intensity.shape, bf16),
            pltpu.VMEM(edge.shape, bf16),
            pltpu.VMEM(edge.shape, bf16),
            pltpu.SMEM(partner.shape, jnp.int32),
            pltpu.SMEM(offsets.shape[::-1], jnp.int32),
            pltpu.SemaphoreType.DMA((4,)),
        ],
        compiler_params=pltpu.CompilerParams(vmem_limit_bytes=8 * 2**20),
        name="advect",
    )(*[pltpu.with_memory_space_constraint(v, pltpu.HBM) for v in (intensity, velocity, partner, offsets.T)])
    odd_pairs = [(n, n + 1) for n in range(1, slabs - 1, 2)]
    even_pairs = [(n, n + 1) for n in range(0, slabs - 1, 2)]
    both_ways = lambda pairs: pairs + [(b, a) for a, b in pairs]
    from_odd = lax.ppermute(second, "slab", both_ways(odd_pairs))
    from_even = lax.ppermute(first, "slab", both_ways(even_pairs))
    inners = from_brains(inner, partner)
    matrix = lambda *shape: jax.ShapeDtypeStruct(shape, bf16)
    tables = pl.pallas_call(
        tables_kernel,
        out_shape=(matrix(256, 128),) * 3 + (matrix(2, 128, 128), matrix(384, 128), matrix(3, 128, 128)),
        in_specs=[VM],
        out_specs=(VM,) * 6,
        compiler_params=pltpu.CompilerParams(vmem_limit_bytes=8 * 2**20),
        cost_estimate=pl.CostEstimate(flops=10**7, bytes_accessed=2**19, transcendentals=0),
        name="tables",
    )(meta)
    own, outer = pl.pallas_call(
        functools.partial(widen_kernel, planes),
        out_shape=(jax.ShapeDtypeStruct((planes + 18, 8, 128), bf16), jax.ShapeDtypeStruct((20, 8, 128), bf16)),
        in_specs=[VM] * 5,
        out_specs=(VM,) * 2,
        compiler_params=pltpu.CompilerParams(vmem_limit_bytes=8 * 2**20),
        name="widen",
    )(warp, first, second, from_even, from_odd)
    outers = from_brains(outer, partner)
    return mate_part(planes, inners, outers, meta, tables, own_part(planes, own, tables), vel)[None]


def solution(mesh):
    return jax.shard_map(
        shards,
        mesh=mesh,
        in_specs=(
            P(("groups", "brain"), "slab", None, None),
            P(("groups", "brain"), None, "slab", None, None),
            P("groups"),
            P("groups", None),
        ),
        out_specs=P(("groups", "brain"), None, "slab", None, None),
        check_vma=False,
    )
```

```python
import functools
import jax, jax.numpy as jnp, numpy as np
from jax import lax
from jax.experimental import pallas as pl
from jax.experimental.pallas import tpu as pltpu
from jax.sharding import PartitionSpec as P

PAIRS = tuple((i, j) for i in range(6) for j in range(i + 1, 6) if i // 2 != j // 2)
TAPS = tuple(float(v) for v in np.exp(-np.arange(-3, 4) ** 2 / 4.5) / np.exp(-np.arange(-3, 4) ** 2 / 4.5).sum())
f32, bf16 = jnp.float32, jnp.bfloat16
LOG2E = 1.4426950408889634
EDGE = 13
VOLUME = 729.0
UNROLL = 2
PITCH = 9
SPARE = 16
FLOOR = 1e-5 * VOLUME
ROOT = 1.0 / 27.0


def split(v):
    hi = v.astype(bf16)
    return hi, (v - hi.astype(f32)).astype(bf16)


def lanes():
    return (lax.broadcasted_iota(jnp.int32, (128, 128), 0), lax.broadcasted_iota(jnp.int32, (128, 128), 1))


def ones_where(cond):
    return jnp.where(cond, 1.0, 0.0).astype(bf16)


def halves(parts):
    return jnp.concatenate(split(jnp.concatenate(parts, axis=0)), axis=1)


def dot(a, b):
    return jnp.dot(a, b, preferred_element_type=f32)


def faces():
    slab = lax.axis_index("slab")
    one = jnp.float32(1.0)
    zero = jnp.float32(0.0)
    return jnp.where(slab > 0, one, zero), jnp.where(slab < lax.axis_size("slab") - 1, one, zero)


def row_inside(d):
    row = lax.broadcasted_iota(jnp.int32, (8, 128), 0)
    return (row + d >= 0) & (row + d < 8)


def describe(planes, xs, box3, tb, desc, low, high):
    nd = planes + 16
    ng = nd // 8

    def squares(g, carry, scale=None):
        c1, c2 = carry
        for i in range(8):
            s = g * 8 + i
            ld = lambda n, p: xs[n, pl.ds(pl.multiple_of(p * 8, 8), 8), :]
            near = [ld(0, s + 2), ld(0, s)] + [ld(j, s + 1) for j in (1, 2, 3, 4)]
            n1, n2 = [], []
            done = []
            for k, (a, b) in enumerate(PAIRS):
                d = near[a] - near[b]
                q = d * d
                if scale is not None:
                    q = q * scale
                done.append(c2[k] + q)
                n2.append(c1[k] + q)
                n1.append(q)
            put(s, done)
            c1, c2 = n1, n2
        return c1, c2

    def put(s, done):
        at = pl.ds(s * PITCH, 8)
        for k in range(12):
            tb[k, at, :] = done[k]
        while len(done) > 1:
            done = [done[n] + done[n + 1] for n in range(0, len(done) - 1, 2)] + done[len(done) // 2 * 2:]
        tb[12, at, :] = done[0]

    zero = [jnp.zeros((8, 128), f32)] * 12
    carry = squares(0, (zero, zero), low)
    carry = lax.fori_loop(1, ng - 1, squares, carry)
    c1, c2 = squares(ng - 1, carry, high)
    put(nd, c2)

    for g in range(ng):
        parts = []
        for k in (12,) + tuple(range(12)):
            t = [tb[k, pl.ds((g * 8 + 1) * PITCH + r, 8, stride=PITCH), :] for r in range(8)]
            p = [t[r] + t[r + 1] for r in range(7)]
            parts += [p[0]] + [p[r - 1] + t[r + 1] for r in range(1, 7)] + [p[6]]
        box = dot(halves(parts), box3[...])
        inv = [(-LOG2E / 27.0) / (box[r * 8:r * 8 + 8] * (1.0 / 324.0) + 0.1) for r in range(8)]
        for k in range(12):
            for r in range(8):
                n = (k + 1) * 64 + r * 8
                e = jnp.exp2(box[n:n + 8] * inv[r])
                if g == 0:
                    e = e * low
                if g == ng - 1:
                    e = e * high
                desc[k, pl.ds(g * 8 * PITCH + r, 8, stride=PITCH), :] = e


def depth_sums(planes, value, ys, q):
    nd, nf = planes + 16, planes + 8
    d = [value(t) for t in range(nd)]
    for f in range(nf):
        if f % 16 == 0:
            s2 = [d[f + t] + d[f + t + 1] for t in (0, 2, 4, 6)]
            total = ((s2[0] + s2[1]) + (s2[2] + s2[3])) + d[f + 8]
        else:
            total = (total - d[f - 1]) + d[f + 8]
        ys[q, pl.ds(f * PITCH, 8), :] = total


def row_sums(ys, q, g):
    t = [ys[q, pl.ds(g * 8 * PITCH + r, 8, stride=PITCH), :] for r in range(8)]
    lo = (t[0] + t[1]) + (t[2] + t[3])
    hi = (t[4] + t[5]) + (t[6] + t[7])
    w0 = lo + t[4]
    w1 = w0 + t[5]
    w7 = hi + t[3]
    w6 = w7 + t[2]
    return [w0, w1, w1 + t[6], lo + hi, lo + hi, w6 + t[1], w6, w7]


def own_kernel(planes, own, box3, box9, grad, step, desc, mean, slope, grads, xs, tb, ys):
    nx, nd, nf = planes + 18, planes + 16, planes + 8
    low, high = faces()
    x = own[...]
    xs[0] = x.astype(f32)
    xs[3] = dot(x, step[0])
    xs[4] = dot(x, step[1])

    def prep(p, _):
        at = pl.ds(pl.multiple_of(p * 8, 8), 8)
        v = xs[0, at, :]
        xs[1, at, :] = jnp.where(row_inside(1), pltpu.roll(v, 7, 0), 0.0)
        xs[2, at, :] = jnp.where(row_inside(-1), pltpu.roll(v, 1, 0), 0.0)
        return 0
    lax.fori_loop(0, nx, prep, 0, unroll=6)
    describe(planes, xs, box3, tb, desc, low, high)

    def channels(k, _):
        for h in range(UNROLL):
            one_channel(UNROLL * k + h, h)
        return 0

    def one_channel(k, h):
        ld = lambda t: desc[k, pl.ds(t * PITCH, 8), :]
        depth_sums(planes, ld, ys, 2 * h)
        depth_sums(planes, lambda t: ld(t) * ld(t), ys, 2 * h + 1)
        parts, centre = [], []
        for g in range(nf // 8):
            for q in range(2):
                parts += row_sums(ys, 2 * h + q, g)
            centre += [desc[k, pl.ds((g * 8 + 4) * PITCH + r, 8, stride=PITCH), :] for r in range(8)]
        sums = dot(halves(parts), box9[...])
        across = dot(halves(centre), grad[...])
        for g in range(nf // 8):
            a = centre[g * 8:g * 8 + 8]
            for r in range(8):
                at = pl.ds(g * 64 + r * 8, 8)
                mo, so = [sums[(g * 16 + q * 8 + r) * 8:(g * 16 + q * 8 + r) * 8 + 8] for q in range(2)]
                gc = across[(g * 8 + r) * 8:(g * 8 + r) * 8 + 8]
                mo = mo * ROOT
                inv = lax.rsqrt(so - mo * mo + FLOOR)
                gz = desc[k, pl.ds((g * 8 + 5) * PITCH + r, 8, stride=PITCH), :] - desc[k, pl.ds((g * 8 + 3) * PITCH + r, 8, stride=PITCH), :]
                gr = a[1] if r == 0 else -a[6] if r == 7 else a[r + 1] - a[r - 1]
                mean[k, at, :] = mo
                slope[k, at, :] = (inv * inv) * (a[r] - mo * ROOT)
                for c, gg in enumerate((gz, gr, gc)):
                    grads[c, k, at, :] = gg * inv
    lax.fori_loop(0, 12 // UNROLL, channels, 0)


def tables_kernel(meta, box3, box9, grad, step, smooth, take):
    i, j = lanes()
    weights = jnp.zeros((128, 128), f32)
    for d in range(4):
        weights = jnp.where(jnp.abs(i - j) == d, TAPS[3 + d], weights)
    whi, wlo = split(weights)
    for h in (0, 128):
        grad[h:h + 128] = jnp.where(i == j + 1, 1.0, jnp.where(i == j - 1, -1.0, 0.0)).astype(bf16)
        box3[h:h + 128] = ones_where(jnp.abs(i - j) <= 1)
        box9[h:h + 128] = ones_where(jnp.abs(i - j) <= 4)
        smooth[h:h + 128] = whi
    smooth[256:384] = wlo
    step[0] = ones_where(i == j + 1)
    step[1] = ones_where(i == j - 1)
    dc = meta[16:17, :]
    for n, d in ((0, 0), (1, 1), (2, -1)):
        take[n] = ones_where((i == j + d + dc) & (j + d >= 0) & (j + d < 128))


def mate_kernel(planes, count, *refs):
    inner, outer = refs[:count][::-1], refs[count:2 * count]
    meta, box3, box9, smooth, take, adesc, mean, slope, grads, vel, out, xs, raw, tb, desc, ys, frc = refs[2 * count:]
    nx, nd, nf = planes + 18, planes + 16, planes + 8
    low, high = faces()
    which = meta[0:1, :]
    dr = jnp.max(meta[8:16, :])
    row = lax.broadcasted_iota(jnp.int32, (8, 128), 0)

    x, y = inner[0][...], outer[0][...]
    for n in range(1, count):
        x = jnp.where(which == n + 1, inner[n][...], x)
        y = jnp.where(which == n + 1, outer[n][...], y)
    x = jnp.concatenate([y[0:80], x, y[80:160]], axis=0)
    for n in range(3):
        raw[n, pl.ds(8, nx * 8), :] = dot(x, take[n])

    def prep(p, _):
        at = pl.multiple_of(p * 8, 8)
        for n, b, d in ((0, 0, 0), (1, 0, 1), (2, 0, -1), (3, 1, 0), (4, 2, 0)):
            v = raw[b, pl.ds(at + 8 + dr + d, 8), :]
            xs[n, pl.ds(at, 8), :] = jnp.where(row_inside(d) & row_inside(d + dr), v, 0.0)
        return 0
    lax.fori_loop(0, nx, prep, 0, unroll=6)
    describe(planes, xs, box3, tb, desc, low, high)

    def channels(step, _):
        ks = [UNROLL * step + h for h in range(UNROLL)]
        sums = []
        for h, k in enumerate(ks):
            lda = lambda t: adesc[k, pl.ds(t * PITCH, 8), :]
            ldb = lambda t: desc[k, pl.ds(t * PITCH, 8), :]
            depth_sums(planes, ldb, ys, 3 * h)
            depth_sums(planes, lambda t: ldb(t) * ldb(t), ys, 3 * h + 1)
            depth_sums(planes, lambda t: lda(t) * ldb(t), ys, 3 * h + 2)
            parts = []
            for g in range(nf // 8):
                for q in range(3):
                    parts += row_sums(ys, 3 * h + q, g)
            sums.append(dot(halves(parts), box9[...]))
        for g in range(nf // 8):
            for r in range(8):
                at = pl.ds(g * 64 + r * 8, 8)
                acc = [frc[c, at, :] for c in range(3)]
                for h, k in enumerate(ks):
                    mm, sm, sc = [sums[h][(g * 24 + q * 8 + r) * 8:(g * 24 + q * 8 + r) * 8 + 8] for q in range(3)]
                    b = desc[k, pl.ds((g * 8 + 4) * PITCH + r, 8, stride=PITCH), :]
                    mm = mm * ROOT
                    inv = lax.rsqrt(sm - mm * mm + FLOOR)
                    cov = sc - mean[k, at, :] * mm
                    coef = (b - mm * ROOT - cov * slope[k, at, :]) * inv
                    acc = [acc[c] + coef * grads[c, k, at, :] for c in range(3)]
                for c in range(3):
                    frc[c, at, :] = acc[c]
        return 0
    frc[...] = jnp.zeros_like(frc)
    lax.fori_loop(0, 12 // UNROLL, channels, 0)

    parts = []
    for c in range(3):
        for g in range(nf // 8):
            for r in range(8):
                v = frc[c, pl.ds(g * 64 + r * 8, 8), :]
                if g == 0:
                    v = jnp.where(row >= 4, v, v * low)
                if g == nf // 8 - 1:
                    v = jnp.where(row < 4, v, v * high)
                ys[0, pl.ds(g * 8 * PITCH + r, 8, stride=PITCH), :] = v
        for o in range(planes):
            p = [ys[0, pl.ds((o + 1 + n) * PITCH, 8), :] for n in range(7)]
            v = TAPS[3] * p[3]
            for n in range(3):
                v = v + TAPS[n] * (p[n] + p[6 - n])
            ys[1, pl.ds(o * PITCH, 8), :] = v
        for g in range(planes // 8):
            t = [ys[1, pl.ds(g * 8 * PITCH + r, 8, stride=PITCH), :] for r in range(8)]
            for r in range(8):
                v = TAPS[3] * t[r]
                for n in range(1, 4):
                    s = [t[q] for q in (r - n, r + n) if 0 <= q < 8]
                    v = v + TAPS[3 + n] * (s[0] + s[1] if len(s) == 2 else s[0])
                parts.append(v)
    both = halves(parts)
    res = dot(both, smooth[0:256]) + dot(both[:, 0:128], smooth[256:384])
    for c in range(3):
        for g in range(planes // 8):
            for r in range(8):
                n = ((c * planes + g * 8) + r) * 8
                ys[0, pl.ds(g * 8 * PITCH + r, 8, stride=PITCH), :] = res[n:n + 8]
        for o in range(planes):
            out[c, o] = vel[0, c, o] + (8.0 * VOLUME / 24.0) * ys[0, pl.ds(o * PITCH, 8), :]


VM = pl.BlockSpec(memory_space=pltpu.VMEM)
HBM = pl.BlockSpec(memory_space=pltpu.HBM)


def own_part(planes, own, tables):
    nx, nd, nf = planes + 18, planes + 16, planes + 8
    shape = jax.ShapeDtypeStruct
    return pl.pallas_call(
        functools.partial(own_kernel, planes),
        out_shape=(
            shape((12, nd * PITCH + SPARE, 128), f32),
            shape((12, nf * 8, 128), f32),
            shape((12, nf * 8, 128), f32),
            shape((3, 12, nf * 8, 128), f32),
        ),
        in_specs=[VM] * 5,
        out_specs=(VM,) * 4,
        scratch_shapes=[
            pltpu.VMEM((5, nx * 8, 128), f32),
            pltpu.VMEM((13, (nd + 1) * PITCH + SPARE, 128), f32),
            pltpu.VMEM((2 * UNROLL, nf * PITCH + SPARE, 128), f32),
        ],
        compiler_params=pltpu.CompilerParams(vmem_limit_bytes=16 * 2**20),
        cost_estimate=pl.CostEstimate(flops=6 * 10**8, bytes_accessed=16 * 2**20, transcendentals=10**6),
        name="own",
    )(own.reshape(-1, 128), *tables[:4])


def mate_part(planes, inner, outer, meta, tables, owned, vel):
    nx, nd, nf = planes + 18, planes + 16, planes + 8
    count = len(inner)
    return pl.pallas_call(
        functools.partial(mate_kernel, planes, count),
        out_shape=jax.ShapeDtypeStruct(vel.shape[1:], f32),
        in_specs=[VM] * (2 * count + 10),
        out_specs=VM,
        scratch_shapes=[
            pltpu.VMEM((5, nx * 8, 128), f32),
            pltpu.VMEM((3, nx * 8 + 16, 128), f32),
            pltpu.VMEM((13, (nd + 1) * PITCH + SPARE, 128), f32),
            pltpu.VMEM((12, nd * PITCH + SPARE, 128), f32),
            pltpu.VMEM((3 * UNROLL, nf * PITCH + SPARE, 128), f32),
            pltpu.VMEM((3, nf * 8, 128), f32),
        ],
        compiler_params=pltpu.CompilerParams(vmem_limit_bytes=16 * 2**20),
        name="mate",
    )(*[m.reshape(-1, 128) for m in inner[::-1] + outer], meta, tables[0], tables[1], *tables[4:], *owned, vel)


def advect_kernel(planes, image_hbm, vel_hbm, partner_hbm, offsets_hbm, warp, inner, first, second, meta, vel, image, down, up, partner, offsets, sems):
    copies = [
        pltpu.make_async_copy(vel_hbm, vel, sems.at[0]),
        pltpu.make_async_copy(image_hbm, image, sems.at[1]),
        pltpu.make_async_copy(partner_hbm, partner, sems.at[2]),
        pltpu.make_async_copy(offsets_hbm, offsets, sems.at[3]),
    ]
    for copy in copies:
        copy.start()
    for copy in copies:
        copy.wait()
    lane = lax.broadcasted_iota(jnp.int32, (8, 128), 1)

    for z in range(planes):
        x = image[0, z].astype(f32)
        before = image[0, z - 1].astype(f32) if z > 0 else x
        after = image[0, z + 1].astype(f32) if z < planes - 1 else x
        sides = (
            (before, after),
            (jnp.where(row_inside(-1), pltpu.roll(x, 1, 0), 0.0), jnp.where(row_inside(1), pltpu.roll(x, 7, 0), 0.0)),
            (jnp.where(lane >= 1, pltpu.roll(x, 1, 1), 0.0), jnp.where(lane < 127, pltpu.roll(x, 127, 1), 0.0)),
        )
        moved = 0.0
        for c, (lo, hi) in enumerate(sides):
            v = vel[0, c, z]
            moved = moved + (jnp.maximum(v, 0.0) * (x - lo) + jnp.minimum(v, 0.0) * (hi - x))
        y = x - moved
        warp[z] = y
        if z == 0 or z == planes - 1:
            v = jnp.maximum(vel[0, 0, z], 0.0) if z == 0 else jnp.minimum(vel[0, 0, z], 0.0)
            edge = split(y) + split(v) + (image[0, z],)
            for n, part in enumerate(edge):
                (down if z == 0 else up)[8 + n] = part
        else:
            inner[z - 1] = y.astype(bf16)
        if 1 <= z <= 8:
            down[z - 1] = y.astype(bf16)
        if planes - 9 <= z < planes - 1:
            up[z - (planes - 9)] = y.astype(bf16)
    me = lax.axis_index("brain")
    mate = partner[me]
    for n, value in enumerate((me ^ mate, offsets[0, mate] - offsets[0, me], offsets[1, mate] - offsets[1, me])):
        meta[n * 8:n * 8 + 8, :] = jnp.full((8, 128), value, jnp.int32)
    even = lax.rem(lax.axis_index("slab"), 2) == 0
    for n in range(EDGE):
        first[n] = jnp.where(even, up[n], down[n])
        second[n] = jnp.where(even, down[n], up[n])


def widen_kernel(planes, warp, sent1, sent2, got1, got2, out, outer):
    low, high = faces()
    even = lax.rem(lax.axis_index("slab"), 2) == 0
    down, up, below, above = (sent2, sent1), (sent1, sent2), (got2, got1), (got1, got2)
    ld = lambda pair, n: jnp.where(even, pair[0][n], pair[1][n]).astype(f32)
    top = planes - 1
    first, last = ld(down, 12), ld(up, 12)
    for n in range(8):
        out[n] = (ld(below, n) * low).astype(bf16)
        out[planes + 10 + n] = (ld(above, n) * high).astype(bf16)
    out[8] = (low * ((ld(below, 8) + ld(below, 9)) - (ld(below, 10) + ld(below, 11)) * (first - ld(below, 12)))).astype(bf16)
    out[planes + 9] = (high * ((ld(above, 8) + ld(above, 9)) - (ld(above, 10) + ld(above, 11)) * (ld(above, 12) - last))).astype(bf16)
    for z in range(1, top):
        out[9 + z] = warp[z].astype(bf16)
    out[9] = (warp[0] - (ld(down, 10) + ld(down, 11)) * (first - ld(below, 12))).astype(bf16)
    out[9 + top] = (warp[top] - (ld(up, 10) + ld(up, 11)) * (ld(above, 12) - last)).astype(bf16)

    for n in range(10):
        outer[n] = out[n]
        outer[10 + n] = out[planes + 8 + n]


def from_brains(x, partner):
    if lax.axis_size("brain") == 4:
        return [lax.ppermute(x, "brain", [(n, n ^ k) for n in range(4)]) for k in (1, 2, 3)]
    gathered = lax.all_gather(x, "brain")
    return [lax.dynamic_index_in_dim(gathered, partner[lax.axis_index("brain")], 0, keepdims=False)]


def shards(intensity, velocity, partner, offsets):
    planes = intensity.shape[1]
    slabs, brains = lax.axis_size("slab"), lax.axis_size("brain")
    edge = jax.ShapeDtypeStruct((EDGE, 8, 128), bf16)
    warp, inner, first, second, meta, vel = pl.pallas_call(
        functools.partial(advect_kernel, planes),
        out_shape=(jax.ShapeDtypeStruct((planes, 8, 128), f32), jax.ShapeDtypeStruct((planes - 2, 8, 128), bf16), edge, edge, jax.ShapeDtypeStruct((24, 128), jnp.int32), jax.ShapeDtypeStruct(velocity.shape, f32)),
        in_specs=[HBM] * 4,
        out_specs=(VM,) * 6,
        scratch_shapes=[
            pltpu.VMEM(intensity.shape, bf16),
            pltpu.VMEM(edge.shape, bf16),
            pltpu.VMEM(edge.shape, bf16),
            pltpu.SMEM(partner.shape, jnp.int32),
            pltpu.SMEM(offsets.shape[::-1], jnp.int32),
            pltpu.SemaphoreType.DMA((4,)),
        ],
        compiler_params=pltpu.CompilerParams(vmem_limit_bytes=8 * 2**20),
        name="advect",
    )(*[pltpu.with_memory_space_constraint(v, pltpu.HBM) for v in (intensity, velocity, partner, offsets.T)])
    odd_pairs = [(n, n + 1) for n in range(1, slabs - 1, 2)]
    even_pairs = [(n, n + 1) for n in range(0, slabs - 1, 2)]
    both_ways = lambda pairs: pairs + [(b, a) for a, b in pairs]
    from_odd = lax.ppermute(second, "slab", both_ways(odd_pairs))
    from_even = lax.ppermute(first, "slab", both_ways(even_pairs))
    inners = from_brains(inner, partner)
    matrix = lambda *shape: jax.ShapeDtypeStruct(shape, bf16)
    tables = pl.pallas_call(
        tables_kernel,
        out_shape=(matrix(256, 128),) * 3 + (matrix(2, 128, 128), matrix(384, 128), matrix(3, 128, 128)),
        in_specs=[VM],
        out_specs=(VM,) * 6,
        compiler_params=pltpu.CompilerParams(vmem_limit_bytes=8 * 2**20),
        cost_estimate=pl.CostEstimate(flops=10**7, bytes_accessed=2**19, transcendentals=0),
        name="tables",
    )(meta)
    own, outer = pl.pallas_call(
        functools.partial(widen_kernel, planes),
        out_shape=(jax.ShapeDtypeStruct((planes + 18, 8, 128), bf16), jax.ShapeDtypeStruct((20, 8, 128), bf16)),
        in_specs=[VM] * 5,
        out_specs=(VM,) * 2,
        compiler_params=pltpu.CompilerParams(vmem_limit_bytes=8 * 2**20),
        name="widen",
    )(warp, first, second, from_even, from_odd)
    outers = from_brains(outer, partner)
    return mate_part(planes, inners, outers, meta, tables, own_part(planes, own, tables), vel)[None]


def solution(mesh):
    return jax.shard_map(
        shards,
        mesh=mesh,
        in_specs=(
            P(("groups", "brain"), "slab", None, None),
            P(("groups", "brain"), None, "slab", None, None),
            P("groups"),
            P("groups", None),
        ),
        out_specs=P(("groups", "brain"), None, "slab", None, None),
        check_vma=False,
    )
```

```python
import functools
import jax, jax.numpy as jnp, numpy as np
from jax import lax
from jax.experimental import pallas as pl
from jax.experimental.pallas import tpu as pltpu
from jax.sharding import PartitionSpec as P

PAIRS = tuple((i, j) for i in range(6) for j in range(i + 1, 6) if i // 2 != j // 2)
TAPS = tuple(float(v) for v in np.exp(-np.arange(-3, 4) ** 2 / 4.5) / np.exp(-np.arange(-3, 4) ** 2 / 4.5).sum())
f32, bf16 = jnp.float32, jnp.bfloat16
LOG2E = 1.4426950408889634
EDGE = 13
VOLUME = 729.0
UNROLL = 2
PITCH = 9
SPARE = 16
FLOOR = 1e-5 * VOLUME * VOLUME


def split(v):
    hi = v.astype(bf16)
    return hi, (v - hi.astype(f32)).astype(bf16)


def lanes():
    return (lax.broadcasted_iota(jnp.int32, (128, 128), 0), lax.broadcasted_iota(jnp.int32, (128, 128), 1))


def ones_where(cond):
    return jnp.where(cond, 1.0, 0.0).astype(bf16)


def halves(parts):
    return jnp.concatenate(split(jnp.concatenate(parts, axis=0)), axis=1)


def dot(a, b):
    return jnp.dot(a, b, preferred_element_type=f32)


def faces():
    slab = lax.axis_index("slab")
    one = jnp.float32(1.0)
    zero = jnp.float32(0.0)
    return jnp.where(slab > 0, one, zero), jnp.where(slab < lax.axis_size("slab") - 1, one, zero)


def row_inside(d):
    row = lax.broadcasted_iota(jnp.int32, (8, 128), 0)
    return (row + d >= 0) & (row + d < 8)


def describe(planes, xs, box3, tb, desc, low, high):
    nd = planes + 16
    ng = nd // 8

    def squares(g, carry, scale=None):
        c1, c2 = carry
        for i in range(8):
            s = g * 8 + i
            ld = lambda n, p: xs[n, pl.ds(pl.multiple_of(p * 8, 8), 8), :]
            near = [ld(0, s + 2), ld(0, s)] + [ld(j, s + 1) for j in (1, 2, 3, 4)]
            n1, n2 = [], []
            done = []
            for k, (a, b) in enumerate(PAIRS):
                d = near[a] - near[b]
                q = d * d
                if scale is not None:
                    q = q * scale
                done.append(c2[k] + q)
                n2.append(c1[k] + q)
                n1.append(q)
            put(s, done)
            c1, c2 = n1, n2
        return c1, c2

    def put(s, done):
        at = pl.ds(s * PITCH, 8)
        for k in range(12):
            tb[k, at, :] = done[k]
        while len(done) > 1:
            done = [done[n] + done[n + 1] for n in range(0, len(done) - 1, 2)] + done[len(done) // 2 * 2:]
        tb[12, at, :] = done[0]

    zero = [jnp.zeros((8, 128), f32)] * 12
    carry = squares(0, (zero, zero), low)
    carry = lax.fori_loop(1, ng - 1, squares, carry)
    c1, c2 = squares(ng - 1, carry, high)
    put(nd, c2)

    for g in range(ng):
        parts = []
        for k in (12,) + tuple(range(12)):
            t = [tb[k, pl.ds((g * 8 + 1) * PITCH + r, 8, stride=PITCH), :] for r in range(8)]
            p = [t[r] + t[r + 1] for r in range(7)]
            parts += [p[0]] + [p[r - 1] + t[r + 1] for r in range(1, 7)] + [p[6]]
        box = dot(halves(parts), box3[...])
        inv = [(-LOG2E / 27.0) / (box[r * 8:r * 8 + 8] * (1.0 / 324.0) + 0.1) for r in range(8)]
        for k in range(12):
            for r in range(8):
                n = (k + 1) * 64 + r * 8
                e = jnp.exp2(box[n:n + 8] * inv[r])
                if g == 0:
                    e = e * low
                if g == ng - 1:
                    e = e * high
                desc[k, pl.ds(g * 8 * PITCH + r, 8, stride=PITCH), :] = e


def depth_sums(planes, value, ys, q):
    nd, nf = planes + 16, planes + 8
    d = [value(t) for t in range(nd)]
    for f in range(nf):
        if f % 16 == 0:
            s2 = [d[f + t] + d[f + t + 1] for t in (0, 2, 4, 6)]
            total = ((s2[0] + s2[1]) + (s2[2] + s2[3])) + d[f + 8]
        else:
            total = (total - d[f - 1]) + d[f + 8]
        ys[q, pl.ds(f * PITCH, 8), :] = total


def row_sums(ys, q, g):
    t = [ys[q, pl.ds(g * 8 * PITCH + r, 8, stride=PITCH), :] for r in range(8)]
    lo = (t[0] + t[1]) + (t[2] + t[3])
    hi = (t[4] + t[5]) + (t[6] + t[7])
    w0 = lo + t[4]
    w1 = w0 + t[5]
    w7 = hi + t[3]
    w6 = w7 + t[2]
    return [w0, w1, w1 + t[6], lo + hi, lo + hi, w6 + t[1], w6, w7]


def own_kernel(planes, own, box3, box9, grad, step, desc, mean, slope, grads, xs, tb, ys):
    nx, nd, nf = planes + 18, planes + 16, planes + 8
    low, high = faces()
    x = own[...]
    xs[0] = x.astype(f32)
    xs[3] = dot(x, step[0])
    xs[4] = dot(x, step[1])

    def prep(p, _):
        at = pl.ds(pl.multiple_of(p * 8, 8), 8)
        v = xs[0, at, :]
        xs[1, at, :] = jnp.where(row_inside(1), pltpu.roll(v, 7, 0), 0.0)
        xs[2, at, :] = jnp.where(row_inside(-1), pltpu.roll(v, 1, 0), 0.0)
        return 0
    lax.fori_loop(0, nx, prep, 0, unroll=6)
    describe(planes, xs, box3, tb, desc, low, high)

    def channels(k, _):
        for h in range(UNROLL):
            one_channel(UNROLL * k + h, h)
        return 0

    def one_channel(k, h):
        ld = lambda t: desc[k, pl.ds(t * PITCH, 8), :]
        depth_sums(planes, ld, ys, 2 * h)
        depth_sums(planes, lambda t: ld(t) * ld(t), ys, 2 * h + 1)
        parts, centre = [], []
        for g in range(nf // 8):
            for q in range(2):
                parts += row_sums(ys, 2 * h + q, g)
            centre += [desc[k, pl.ds((g * 8 + 4) * PITCH + r, 8, stride=PITCH), :] for r in range(8)]
        sums = dot(halves(parts), box9[...])
        across = dot(halves(centre), grad[...])
        for g in range(nf // 8):
            a = centre[g * 8:g * 8 + 8]
            for r in range(8):
                at = pl.ds(g * 64 + r * 8, 8)
                mo, so = [sums[(g * 16 + q * 8 + r) * 8:(g * 16 + q * 8 + r) * 8 + 8] for q in range(2)]
                gc = across[(g * 8 + r) * 8:(g * 8 + r) * 8 + 8]
                inv = lax.rsqrt(VOLUME * so - mo * mo + FLOOR)
                gz = desc[k, pl.ds((g * 8 + 5) * PITCH + r, 8, stride=PITCH), :] - desc[k, pl.ds((g * 8 + 3) * PITCH + r, 8, stride=PITCH), :]
                gr = a[1] if r == 0 else -a[6] if r == 7 else a[r + 1] - a[r - 1]
                mean[k, at, :] = mo
                slope[k, at, :] = (inv * inv) * (VOLUME * a[r] - mo)
                for c, gg in enumerate((gz, gr, gc)):
                    grads[c, k, at, :] = gg * inv
    lax.fori_loop(0, 12 // UNROLL, channels, 0)


def tables_kernel(meta, box3, box9, grad, step, smooth, take):
    i, j = lanes()
    weights = jnp.zeros((128, 128), f32)
    for d in range(4):
        weights = jnp.where(jnp.abs(i - j) == d, TAPS[3 + d], weights)
    whi, wlo = split(weights)
    for h in (0, 128):
        grad[h:h + 128] = jnp.where(i == j + 1, 1.0, jnp.where(i == j - 1, -1.0, 0.0)).astype(bf16)
        box3[h:h + 128] = ones_where(jnp.abs(i - j) <= 1)
        box9[h:h + 128] = ones_where(jnp.abs(i - j) <= 4)
        smooth[h:h + 128] = whi
    smooth[256:384] = wlo
    step[0] = ones_where(i == j + 1)
    step[1] = ones_where(i == j - 1)
    dc = meta[16:17, :]
    for n, d in ((0, 0), (1, 1), (2, -1)):
        take[n] = ones_where((i == j + d + dc) & (j + d >= 0) & (j + d < 128))


def mate_kernel(planes, count, *refs):
    inner, outer = refs[:count][::-1], refs[count:2 * count]
    meta, box3, box9, smooth, take, adesc, mean, slope, grads, vel, out, xs, raw, tb, desc, ys, frc = refs[2 * count:]
    nx, nd, nf = planes + 18, planes + 16, planes + 8
    low, high = faces()
    which = meta[0:1, :]
    dr = jnp.max(meta[8:16, :])
    row = lax.broadcasted_iota(jnp.int32, (8, 128), 0)

    x, y = inner[0][...], outer[0][...]
    for n in range(1, count):
        x = jnp.where(which == n + 1, inner[n][...], x)
        y = jnp.where(which == n + 1, outer[n][...], y)
    x = jnp.concatenate([y[0:80], x, y[80:160]], axis=0)
    for n in range(3):
        raw[n, pl.ds(8, nx * 8), :] = dot(x, take[n])

    def prep(p, _):
        at = pl.multiple_of(p * 8, 8)
        for n, b, d in ((0, 0, 0), (1, 0, 1), (2, 0, -1), (3, 1, 0), (4, 2, 0)):
            v = raw[b, pl.ds(at + 8 + dr + d, 8), :]
            xs[n, pl.ds(at, 8), :] = jnp.where(row_inside(d) & row_inside(d + dr), v, 0.0)
        return 0
    lax.fori_loop(0, nx, prep, 0, unroll=6)
    describe(planes, xs, box3, tb, desc, low, high)

    def channels(step, _):
        ks = [UNROLL * step + h for h in range(UNROLL)]
        sums = []
        for h, k in enumerate(ks):
            lda = lambda t: adesc[k, pl.ds(t * PITCH, 8), :]
            ldb = lambda t: desc[k, pl.ds(t * PITCH, 8), :]
            depth_sums(planes, ldb, ys, 3 * h)
            depth_sums(planes, lambda t: ldb(t) * ldb(t), ys, 3 * h + 1)
            depth_sums(planes, lambda t: lda(t) * ldb(t), ys, 3 * h + 2)
            parts = []
            for g in range(nf // 8):
                for q in range(3):
                    parts += row_sums(ys, 3 * h + q, g)
            sums.append(dot(halves(parts), box9[...]))
        for g in range(nf // 8):
            for r in range(8):
                at = pl.ds(g * 64 + r * 8, 8)
                acc = [frc[c, at, :] for c in range(3)]
                for h, k in enumerate(ks):
                    mm, sm, sc = [sums[h][(g * 24 + q * 8 + r) * 8:(g * 24 + q * 8 + r) * 8 + 8] for q in range(3)]
                    b = desc[k, pl.ds((g * 8 + 4) * PITCH + r, 8, stride=PITCH), :]
                    inv = lax.rsqrt(VOLUME * sm - mm * mm + FLOOR)
                    cov = VOLUME * sc - mean[k, at, :] * mm
                    coef = (VOLUME * b - mm - cov * slope[k, at, :]) * inv
                    acc = [acc[c] + coef * grads[c, k, at, :] for c in range(3)]
                for c in range(3):
                    frc[c, at, :] = acc[c]
        return 0
    frc[...] = jnp.zeros_like(frc)
    lax.fori_loop(0, 12 // UNROLL, channels, 0)

    parts = []
    for c in range(3):
        for g in range(nf // 8):
            for r in range(8):
                v = frc[c, pl.ds(g * 64 + r * 8, 8), :]
                if g == 0:
                    v = jnp.where(row >= 4, v, v * low)
                if g == nf // 8 - 1:
                    v = jnp.where(row < 4, v, v * high)
                ys[0, pl.ds(g * 8 * PITCH + r, 8, stride=PITCH), :] = v
        for o in range(planes):
            p = [ys[0, pl.ds((o + 1 + n) * PITCH, 8), :] for n in range(7)]
            v = TAPS[3] * p[3]
            for n in range(3):
                v = v + TAPS[n] * (p[n] + p[6 - n])
            ys[1, pl.ds(o * PITCH, 8), :] = v
        for g in range(planes // 8):
            t = [ys[1, pl.ds(g * 8 * PITCH + r, 8, stride=PITCH), :] for r in range(8)]
            for r in range(8):
                v = TAPS[3] * t[r]
                for n in range(1, 4):
                    s = [t[q] for q in (r - n, r + n) if 0 <= q < 8]
                    v = v + TAPS[3 + n] * (s[0] + s[1] if len(s) == 2 else s[0])
                parts.append(v)
    both = halves(parts)
    res = dot(both, smooth[0:256]) + dot(both[:, 0:128], smooth[256:384])
    for c in range(3):
        for g in range(planes // 8):
            for r in range(8):
                n = ((c * planes + g * 8) + r) * 8
                ys[0, pl.ds(g * 8 * PITCH + r, 8, stride=PITCH), :] = res[n:n + 8]
        for o in range(planes):
            out[c, o] = vel[0, c, o] + (8.0 * VOLUME / 24.0) * ys[0, pl.ds(o * PITCH, 8), :]


VM = pl.BlockSpec(memory_space=pltpu.VMEM)
HBM = pl.BlockSpec(memory_space=pltpu.HBM)


def own_part(planes, own, tables):
    nx, nd, nf = planes + 18, planes + 16, planes + 8
    shape = jax.ShapeDtypeStruct
    return pl.pallas_call(
        functools.partial(own_kernel, planes),
        out_shape=(
            shape((12, nd * PITCH + SPARE, 128), f32),
            shape((12, nf * 8, 128), f32),
            shape((12, nf * 8, 128), f32),
            shape((3, 12, nf * 8, 128), f32),
        ),
        in_specs=[VM] * 5,
        out_specs=(VM,) * 4,
        scratch_shapes=[
            pltpu.VMEM((5, nx * 8, 128), f32),
            pltpu.VMEM((13, (nd + 1) * PITCH + SPARE, 128), f32),
            pltpu.VMEM((2 * UNROLL, nf * PITCH + SPARE, 128), f32),
        ],
        compiler_params=pltpu.CompilerParams(vmem_limit_bytes=16 * 2**20),
        cost_estimate=pl.CostEstimate(flops=6 * 10**8, bytes_accessed=16 * 2**20, transcendentals=10**6),
        name="own",
    )(own.reshape(-1, 128), *tables[:4])


def mate_part(planes, inner, outer, meta, tables, owned, vel):
    nx, nd, nf = planes + 18, planes + 16, planes + 8
    count = len(inner)
    return pl.pallas_call(
        functools.partial(mate_kernel, planes, count),
        out_shape=jax.ShapeDtypeStruct(vel.shape[1:], f32),
        in_specs=[VM] * (2 * count + 10),
        out_specs=VM,
        scratch_shapes=[
            pltpu.VMEM((5, nx * 8, 128), f32),
            pltpu.VMEM((3, nx * 8 + 16, 128), f32),
            pltpu.VMEM((13, (nd + 1) * PITCH + SPARE, 128), f32),
            pltpu.VMEM((12, nd * PITCH + SPARE, 128), f32),
            pltpu.VMEM((3 * UNROLL, nf * PITCH + SPARE, 128), f32),
            pltpu.VMEM((3, nf * 8, 128), f32),
        ],
        compiler_params=pltpu.CompilerParams(vmem_limit_bytes=16 * 2**20),
        name="mate",
    )(*[m.reshape(-1, 128) for m in inner[::-1] + outer], meta, tables[0], tables[1], *tables[4:], *owned, vel)


def advect_kernel(planes, image_hbm, vel_hbm, partner_hbm, offsets_hbm, warp, inner, first, second, meta, vel, image, down, up, partner, offsets, sems):
    copies = [
        pltpu.make_async_copy(vel_hbm, vel, sems.at[0]),
        pltpu.make_async_copy(image_hbm, image, sems.at[1]),
        pltpu.make_async_copy(partner_hbm, partner, sems.at[2]),
        pltpu.make_async_copy(offsets_hbm, offsets, sems.at[3]),
    ]
    for copy in copies:
        copy.start()
    for copy in copies:
        copy.wait()
    lane = lax.broadcasted_iota(jnp.int32, (8, 128), 1)

    for z in range(planes):
        x = image[0, z].astype(f32)
        before = image[0, z - 1].astype(f32) if z > 0 else x
        after = image[0, z + 1].astype(f32) if z < planes - 1 else x
        sides = (
            (before, after),
            (jnp.where(row_inside(-1), pltpu.roll(x, 1, 0), 0.0), jnp.where(row_inside(1), pltpu.roll(x, 7, 0), 0.0)),
            (jnp.where(lane >= 1, pltpu.roll(x, 1, 1), 0.0), jnp.where(lane < 127, pltpu.roll(x, 127, 1), 0.0)),
        )
        moved = 0.0
        for c, (lo, hi) in enumerate(sides):
            v = vel[0, c, z]
            moved = moved + (jnp.maximum(v, 0.0) * (x - lo) + jnp.minimum(v, 0.0) * (hi - x))
        y = x - moved
        warp[z] = y
        if z == 0 or z == planes - 1:
            v = jnp.maximum(vel[0, 0, z], 0.0) if z == 0 else jnp.minimum(vel[0, 0, z], 0.0)
            edge = split(y) + split(v) + (image[0, z],)
            for n, part in enumerate(edge):
                (down if z == 0 else up)[8 + n] = part
        else:
            inner[z - 1] = y.astype(bf16)
        if 1 <= z <= 8:
            down[z - 1] = y.astype(bf16)
        if planes - 9 <= z < planes - 1:
            up[z - (planes - 9)] = y.astype(bf16)
    me = lax.axis_index("brain")
    mate = partner[me]
    for n, value in enumerate((me ^ mate, offsets[0, mate] - offsets[0, me], offsets[1, mate] - offsets[1, me])):
        meta[n * 8:n * 8 + 8, :] = jnp.full((8, 128), value, jnp.int32)
    even = lax.rem(lax.axis_index("slab"), 2) == 0
    for n in range(EDGE):
        first[n] = jnp.where(even, up[n], down[n])
        second[n] = jnp.where(even, down[n], up[n])


def widen_kernel(planes, warp, sent1, sent2, got1, got2, out, outer):
    low, high = faces()
    even = lax.rem(lax.axis_index("slab"), 2) == 0
    down, up, below, above = (sent2, sent1), (sent1, sent2), (got2, got1), (got1, got2)
    ld = lambda pair, n: jnp.where(even, pair[0][n], pair[1][n]).astype(f32)
    top = planes - 1
    first, last = ld(down, 12), ld(up, 12)
    for n in range(8):
        out[n] = (ld(below, n) * low).astype(bf16)
        out[planes + 10 + n] = (ld(above, n) * high).astype(bf16)
    out[8] = (low * ((ld(below, 8) + ld(below, 9)) - (ld(below, 10) + ld(below, 11)) * (first - ld(below, 12)))).astype(bf16)
    out[planes + 9] = (high * ((ld(above, 8) + ld(above, 9)) - (ld(above, 10) + ld(above, 11)) * (ld(above, 12) - last))).astype(bf16)
    for z in range(1, top):
        out[9 + z] = warp[z].astype(bf16)
    out[9] = (warp[0] - (ld(down, 10) + ld(down, 11)) * (first - ld(below, 12))).astype(bf16)
    out[9 + top] = (warp[top] - (ld(up, 10) + ld(up, 11)) * (ld(above, 12) - last)).astype(bf16)

    for n in range(10):
        outer[n] = out[n]
        outer[10 + n] = out[planes + 8 + n]


def from_brains(x, partner):
    if lax.axis_size("brain") == 4:
        return [lax.ppermute(x, "brain", [(n, n ^ k) for n in range(4)]) for k in (1, 2, 3)]
    gathered = lax.all_gather(x, "brain")
    return [lax.dynamic_index_in_dim(gathered, partner[lax.axis_index("brain")], 0, keepdims=False)]


def shards(intensity, velocity, partner, offsets):
    planes = intensity.shape[1]
    slabs, brains = lax.axis_size("slab"), lax.axis_size("brain")
    edge = jax.ShapeDtypeStruct((EDGE, 8, 128), bf16)
    warp, inner, first, second, meta, vel = pl.pallas_call(
        functools.partial(advect_kernel, planes),
        out_shape=(jax.ShapeDtypeStruct((planes, 8, 128), f32), jax.ShapeDtypeStruct((planes - 2, 8, 128), bf16), edge, edge, jax.ShapeDtypeStruct((24, 128), jnp.int32), jax.ShapeDtypeStruct(velocity.shape, f32)),
        in_specs=[HBM] * 4,
        out_specs=(VM,) * 6,
        scratch_shapes=[
            pltpu.VMEM(intensity.shape, bf16),
            pltpu.VMEM(edge.shape, bf16),
            pltpu.VMEM(edge.shape, bf16),
            pltpu.SMEM(partner.shape, jnp.int32),
            pltpu.SMEM(offsets.shape[::-1], jnp.int32),
            pltpu.SemaphoreType.DMA((4,)),
        ],
        compiler_params=pltpu.CompilerParams(vmem_limit_bytes=8 * 2**20),
        name="advect",
    )(*[pltpu.with_memory_space_constraint(v, pltpu.HBM) for v in (intensity, velocity, partner, offsets.T)])
    odd_pairs = [(n, n + 1) for n in range(1, slabs - 1, 2)]
    even_pairs = [(n, n + 1) for n in range(0, slabs - 1, 2)]
    both_ways = lambda pairs: pairs + [(b, a) for a, b in pairs]
    from_odd = lax.ppermute(second, "slab", both_ways(odd_pairs))
    from_even = lax.ppermute(first, "slab", both_ways(even_pairs))
    inners = from_brains(inner, partner)
    matrix = lambda *shape: jax.ShapeDtypeStruct(shape, bf16)
    tables = pl.pallas_call(
        tables_kernel,
        out_shape=(matrix(256, 128),) * 3 + (matrix(2, 128, 128), matrix(384, 128), matrix(3, 128, 128)),
        in_specs=[VM],
        out_specs=(VM,) * 6,
        compiler_params=pltpu.CompilerParams(vmem_limit_bytes=8 * 2**20),
        cost_estimate=pl.CostEstimate(flops=10**7, bytes_accessed=2**19, transcendentals=0),
        name="tables",
    )(meta)
    own, outer = pl.pallas_call(
        functools.partial(widen_kernel, planes),
        out_shape=(jax.ShapeDtypeStruct((planes + 18, 8, 128), bf16), jax.ShapeDtypeStruct((20, 8, 128), bf16)),
        in_specs=[VM] * 5,
        out_specs=(VM,) * 2,
        compiler_params=pltpu.CompilerParams(vmem_limit_bytes=8 * 2**20),
        name="widen",
    )(warp, first, second, from_even, from_odd)
    outers = from_brains(outer, partner)
    return mate_part(planes, inners, outers, meta, tables, own_part(planes, own, tables), vel)[None]


def solution(mesh):
    return jax.shard_map(
        shards,
        mesh=mesh,
        in_specs=(
            P(("groups", "brain"), "slab", None, None),
            P(("groups", "brain"), None, "slab", None, None),
            P("groups"),
            P("groups", None),
        ),
        out_specs=P(("groups", "brain"), None, "slab", None, None),
        check_vma=False,
    )
```
